32 devices in a mesh: expert: 4 (over y, x), etp: 8 (over z, core).
Axes of the slice: x: 2, y: 2, z: 4, core: 2. Of those that a mesh axis runs over, the one named last changes fastest.
Arguments:
- tokens: bfloat16 [512, 3072], P('expert', 'etp'), may hold values from -6 to 6
- expert_ids: int32 [512, 2], P('expert'), may hold values from 0 to 3, all different within a row
- live_tokens: int32 [4], replicated, may hold values from 32 to 128, as said below
- replicated: int32 [4], replicated, may hold values from 0 to 1, as said below
- w_router: bfloat16 [3072, 4], P('etp'), may hold values from -0.109375 to 0.109375
- w_gate: bfloat16 [4, 3072, 8192], P('expert', None, 'etp'), may hold values from -0.109375 to 0.109375
- w_up: bfloat16 [4, 3072, 8192], P('expert', None, 'etp'), may hold values from -0.109375 to 0.109375
- w_down: bfloat16 [4, 8192, 3072], P('expert', 'etp'), may hold values from -0.0625 to 0.0625
- cotangent: bfloat16 [512, 3072], P('expert', 'etp'), may hold values from -6 to 6
Outputs:
- mixed: bfloat16 [512, 3072], P('expert', 'etp')
- grad_gate: bfloat16 [4, 3072, 8192], P('expert', None, 'etp')
- grad_up: bfloat16 [4, 3072, 8192], P('expert', None, 'etp')
- grad_down: bfloat16 [4, 8192, 3072], P('expert', 'etp')
- grad_router: bfloat16 [3072, 4], P('etp')
The draws below stay inside these ranges and needn't reach their ends.
Inputs may be any that keep to these rules, and one draw needn't show every extreme that they name: `replicated`: for every expert e below half of 4, exactly one of e and e plus half of 4 has the entry 1. `live_tokens`: some group has 128 live tokens and some other group has 32.
All inputs are finite; a program needn't handle non-finite values.
Results may differ from the reference program's by a relative error of at most 0.0065.
Values may be sent and summed in bfloat16 or wider, within the bound.
No kernel may reach another device: no remote copies, remote signals or barrier semaphores. Data moves between devices by JAX's collectives and lax.ppermute only.
A program may use at most 192 MiB of HBM per device.

```python
import jax
import jax.numpy as jnp
from jax import lax

D = 3072
FF = 8192
TOK_G = 128
CAPG = 32
RCAP = 8
EXPERTS = 4
TOKENS = 512


def draw_replicated(key, part):
    key = jax.random.fold_in(key, 7)
    halfway = EXPERTS // 2
    picked = jax.random.randint(key, (halfway,), 0, 2, dtype=jnp.int32)
    return jnp.concatenate([picked, 1 - picked]).astype(jnp.int32)


def draw_live_tokens(key, part):
    key = jax.random.fold_in(key, 11)
    key_len, key_perm = jax.random.split(key)
    lowest = TOK_G // 4
    spread = jax.random.randint(key_len, (EXPERTS,), lowest, TOK_G + 1, dtype=jnp.int32)
    ranks = jnp.arange(EXPERTS, dtype=jnp.int32)
    fixed = jnp.where(ranks == 0, TOK_G, jnp.where(ranks == 1, lowest, spread))
    order = jax.random.permutation(key_perm, EXPERTS)
    return fixed[order].astype(jnp.int32)


def shard_levels(stream_key, extent, cuts, low, largest):
    level, own = 1.0, jax.random.fold_in(stream_key, 6)
    for dim, parts in cuts:
        steps = jnp.exp(jax.random.uniform(jax.random.fold_in(own, dim), (parts,), jnp.float32, low / len(cuts), largest / len(cuts)))
        level = level * jnp.repeat(steps, extent[dim] // parts).reshape([-1 if axis == dim else 1 for axis in range(len(extent))])
    return level


def distinct(own_key, rows, number_of, top, lift):
    sequence = jax.random.permutation(jax.random.fold_in(own_key, 1), number_of)
    favour = sequence
    for power in range(3):
        favour = favour * favour // number_of
    favour = favour * lift // number_of
    chance = jax.random.randint(jax.random.fold_in(own_key, 2), (rows, number_of), 0, 4096) + favour
    fixed_rows = jax.random.permutation(jax.random.fold_in(own_key, 3), rows)[jnp.arange(number_of) % rows]
    chance = jnp.where(jnp.arange(rows)[:, None] == fixed_rows[None, :], 1 << 14, chance)
    merit = chance * number_of + jnp.arange(number_of)
    return lax.top_k(merit.astype(jnp.int32), top)[1].astype(jnp.int32)


def scatter_about(rng, extent, deviation, bound, cuts=(), kind=jnp.bfloat16):
    result = deviation * jax.random.normal(rng, extent, jnp.float32)
    if cuts:
        result = result * shard_levels(rng, extent, cuts, -0.22, 0.18)
    return jnp.clip(result, -bound, bound).astype(kind)


def setup_inputs(seed: int = 0) -> dict:
    seeds = jax.random.split(jax.random.key(seed), 10)
    tokens = scatter_about(seeds[0], (TOKENS, D), 1.0, 6.0, ((0, 4), (1, 8)))
    expert_ids = distinct(seeds[1], TOKENS, EXPERTS, 2, 4096)
    live_tokens = draw_live_tokens(jax.random.fold_in(seeds[9], 71), 0)
    replicated = draw_replicated(jax.random.fold_in(seeds[9], 71), 0)
    w_router = scatter_about(seeds[4], (D, EXPERTS), D ** -0.5, 0.109375, ((0, 8),))
    w_gate = scatter_about(seeds[5], (EXPERTS, D, FF), D ** -0.5, 0.109375, ((0, 4), (2, 8)))
    w_up = scatter_about(seeds[6], (EXPERTS, D, FF), D ** -0.5, 0.109375, ((0, 4), (2, 8)))
    w_down = scatter_about(seeds[7], (EXPERTS, FF, D), FF ** -0.5, 0.0625, ((0, 4), (1, 8)))
    cotangent = scatter_about(seeds[8], (TOKENS, D), 1.0, 6.0, ((0, 4), (1, 8)))
    return {"tokens": tokens, "expert_ids": expert_ids, "live_tokens": live_tokens, "replicated": replicated, "w_router": w_router, "w_gate": w_gate, "w_up": w_up, "w_down": w_down, "cotangent": cotangent}


def silu_parts(pre):
    sigma = jax.nn.sigmoid(pre)
    return pre * sigma, sigma * (1.0 + pre * (1.0 - sigma))


def expert_math(rows_x, rows_d, gate_w, up_w, down_w):
    gate_pre = jnp.dot(rows_x, gate_w, preferred_element_type=jnp.float32)
    up_pre = jnp.dot(rows_x, up_w, preferred_element_type=jnp.float32)
    active, slope = silu_parts(gate_pre)
    hidden = (active * up_pre).astype(jnp.bfloat16)
    output = jnp.dot(hidden, down_w, preferred_element_type=jnp.float32).astype(jnp.bfloat16)
    d_hidden = jnp.dot(rows_d, down_w.T, preferred_element_type=jnp.float32)
    d_gate = (d_hidden * up_pre * slope).astype(jnp.bfloat16)
    d_up = (d_hidden * active).astype(jnp.bfloat16)
    grad_g = jnp.dot(rows_x.T, d_gate, preferred_element_type=jnp.float32).astype(jnp.bfloat16)
    grad_u = jnp.dot(rows_x.T, d_up, preferred_element_type=jnp.float32).astype(jnp.bfloat16)
    grad_d = jnp.dot(hidden.T, rows_d, preferred_element_type=jnp.float32).astype(jnp.bfloat16)
    return output, grad_g, grad_u, grad_d


def reference(tokens, expert_ids, live_tokens, replicated, w_router, w_gate, w_up, w_down, cotangent):
    groups = live_tokens.shape[0]
    capacity = CAPG + RCAP
    slots_all = groups * capacity
    lanes = jnp.arange(EXPERTS, dtype=jnp.int32)
    logits = jnp.dot(tokens, w_router, preferred_element_type=jnp.float32)
    first_hot = expert_ids[:, 0][:, None] == lanes[None, :]
    second_hot = expert_ids[:, 1][:, None] == lanes[None, :]
    first_logit = jnp.sum(jnp.where(first_hot, logits, 0.0), axis=1)
    second_logit = jnp.sum(jnp.where(second_hot, logits, 0.0), axis=1)
    gate_one = jax.nn.sigmoid(first_logit - second_logit)
    gate_two = jax.nn.sigmoid(second_logit - first_logit)
    grouped = expert_ids.reshape(groups, TOK_G, 2)
    order = jnp.concatenate([grouped[:, :, 0], grouped[:, :, 1]], axis=1)
    live = jnp.arange(TOK_G, dtype=jnp.int32)[None, :] < live_tokens[:, None]
    alive = jnp.concatenate([live, live], axis=1)
    onehot = (order[:, :, None] == lanes[None, None, :]) & alive[:, :, None]
    ones = onehot.astype(jnp.int32)
    before = jnp.cumsum(ones, axis=1, dtype=jnp.int32) - ones
    slot = jnp.sum(jnp.where(onehot, before, 0), axis=2, dtype=jnp.int32)
    flagged = replicated[order]
    kept = alive & ((slot < CAPG) | ((flagged == 1) & (slot < capacity)))
    within = jnp.arange(TOK_G, dtype=jnp.int32)
    group_index = jnp.arange(groups, dtype=jnp.int32)[:, None]
    token_index = (group_index * TOK_G + jnp.concatenate([within, within])[None, :]).reshape(-1)
    position = (group_index * capacity + slot).reshape(-1)
    order = order.reshape(-1)
    kept = kept.reshape(-1)
    gates = jnp.concatenate([gate_one.reshape(groups, TOK_G), gate_two.reshape(groups, TOK_G)], axis=1).reshape(-1)
    dy_rows = cotangent[token_index].astype(jnp.float32)
    scaled = (gates[:, None] * dy_rows).astype(jnp.bfloat16)
    total = order.shape[0]

    def one_expert(items):
        expert, gate_w, up_w, down_w = items
        target = jnp.where(kept & (order == expert), position, slots_all)
        source = jnp.zeros((slots_all,), jnp.int32).at[target].set(jnp.arange(total, dtype=jnp.int32), mode="drop")
        valid = jnp.zeros((slots_all,), jnp.bool_).at[target].set(True, mode="drop")
        rows_x = jnp.where(valid[:, None], tokens[token_index[source]], jnp.zeros((), jnp.bfloat16))
        rows_d = jnp.where(valid[:, None], scaled[source], jnp.zeros((), jnp.bfloat16))
        return expert_math(rows_x, rows_d, gate_w, up_w, down_w)

    outputs, grad_gate, grad_up, grad_down = lax.map(one_expert, (lanes, w_gate, w_up, w_down))
    picked = outputs[order, jnp.minimum(position, slots_all - 1)].astype(jnp.float32)
    picked = jnp.where(kept[:, None], picked, jnp.zeros((), jnp.float32))
    per_group = picked.reshape(groups, 2, TOK_G, -1)
    first_out = per_group[:, 0].reshape(groups * TOK_G, -1)
    second_out = per_group[:, 1].reshape(groups * TOK_G, -1)
    mixed = (gate_one[:, None] * first_out + gate_two[:, None] * second_out).astype(jnp.bfloat16)
    dy = cotangent.astype(jnp.float32)
    dot_one = jnp.sum(first_out * dy, axis=1)
    dot_two = jnp.sum(second_out * dy, axis=1)
    d_logit = (dot_one - dot_two) * gate_one * gate_two
    d_logits = jnp.where(first_hot, d_logit[:, None], 0.0) - jnp.where(second_hot, d_logit[:, None], 0.0)
    grad_router = jnp.dot(tokens.astype(jnp.float32).T, d_logits, precision=lax.Precision.HIGHEST).astype(jnp.bfloat16)
    return mixed, grad_gate, grad_up, grad_down, grad_router
```

```python
import functools

import jax
import jax.numpy as jnp
from jax import lax
from jax.experimental import pallas as pl
from jax.experimental.pallas import tpu as pltpu
from jax.sharding import Mesh, PartitionSpec as P

CAPG = 32
RCAP = 8
CAP = CAPG + RCAP
META = 8
ROWS = CAP + META
MIB = 1024 * 1024
LANES = 128

F32 = jnp.float32
BF16 = jnp.bfloat16


def dot(a, b, dims):
    return lax.dot_general(a, b, (dims, ((), ())), preferred_element_type=F32)


def split3(value):
    hi = value.astype(BF16).astype(F32)
    rest = value - hi
    mid = rest.astype(BF16).astype(F32)
    return hi, mid, rest - mid


def pack_kernel(experts, *refs):
    sources, pos_ref, send_refs = refs[:6], refs[6], refs[7 : 7 + experts]
    held, sems = refs[7 + experts : 13 + experts], refs[13 + experts]
    copies = [pltpu.make_async_copy(a, b, sems.at[i]) for i, (a, b) in enumerate(zip(sources, held))]
    for copy in copies:
        copy.start()
    for copy in copies:
        copy.wait()
    live_ref, flags_ref, ids_ref, router_ref, tok_ref, cot_ref = held
    count, width = tok_ref.shape
    both = 2 * count
    lanes = max(experts, 8)
    group = lax.axis_index("expert")
    live = live_ref[group]
    ids = ids_ref[...]
    first, second = ids[0:1, :], ids[1:2, :]
    order = jnp.concatenate([first, second], axis=1)
    other = jnp.concatenate([second, first], axis=1)
    lane = lax.broadcasted_iota(jnp.int32, (1, both), 1)
    token = jnp.where(lane < count, lane, lane - count)
    alive = token < live
    expert_rows = lax.broadcasted_iota(jnp.int32, (lanes, both), 0)
    onehot = ((expert_rows == order) & alive).astype(F32)
    earlier = lax.broadcasted_iota(jnp.int32, (both, both), 0)
    later = lax.broadcasted_iota(jnp.int32, (both, both), 1)
    before = dot(onehot.astype(BF16), (earlier < later).astype(BF16), ((1,), (0,)))
    slot = jnp.sum(onehot * before, axis=0, keepdims=True).astype(jnp.int32)
    limit = jnp.full((1, both), CAPG, jnp.int32)
    for e in range(experts):
        limit = jnp.where(order == e, CAPG + RCAP * flags_ref[e], limit)
    kept = alive & (slot < limit)
    position = jnp.where(kept, (order ^ group) * ROWS + slot, -1)
    pos_ref[...] = position

    slots = lax.broadcasted_iota(jnp.int32, (experts * ROWS, both), 0)
    select = (slots == position).astype(F32)
    merged = (select[:, :count] + select[:, count:]).astype(BF16)
    rows_x = dot(merged, tok_ref[...], ((1,), (0,)))
    rows_d = dot(merged, cot_ref[...], ((1,), (0,)))

    logits = dot(router_ref[...], tok_ref[...], ((1,), (1,)))
    pick = lax.broadcasted_iota(jnp.int32, (experts, count), 0)
    gap = jnp.sum(
        jnp.where(pick == first, logits, 0.0) - jnp.where(pick == second, logits, 0.0),
        axis=0,
        keepdims=True,
    )
    hi, mid, low = split3(jnp.concatenate([gap, -gap], axis=1))
    meta_row = lax.broadcasted_iota(jnp.int32, (META, both), 0)
    meta = jnp.where(
        meta_row == 0,
        hi,
        jnp.where(
            meta_row == 1,
            mid,
            jnp.where(meta_row == 2, low, jnp.where(meta_row == 3, other.astype(F32), 0.0)),
        ),
    ).astype(BF16)
    span = min(width, LANES)
    near = lax.broadcasted_iota(jnp.int32, (span, both), 0)
    for e in range(experts):
        mine = ((near + e * ROWS == position) & (near < CAP)).astype(F32).astype(BF16)
        block = dot(meta, mine, ((1,), (1,)))
        if width > span:
            block = jnp.concatenate([block, jnp.zeros((META, width - span), F32)], axis=1)
        base = e * ROWS
        send_refs[e][:ROWS] = jnp.concatenate([rows_x[base : base + CAP], block], axis=0).astype(BF16)
        send_refs[e][ROWS:] = rows_d[base : base + CAP].astype(BF16)


def stack_kernel(count, lo, hi, *refs):
    for q in range(count):
        refs[-1][q] = refs[q][lo:hi]


def column(row):
    size = row.shape[1]
    down = lax.broadcasted_iota(jnp.int32, (size, size), 0)
    across = lax.broadcasted_iota(jnp.int32, (size, size), 1)
    return jnp.sum(jnp.where(down == across, row, 0.0), axis=1, keepdims=True)


def visit(groups, hops, width, relative, body):
    core = lax.axis_index("core")
    z = lax.axis_index("z")
    if width % LANES == 0:
        for side in range(2):
            for k in range(hops):
                at = ((z ^ k if relative else k) * 2 + (core ^ side)) * width
                body(side, k, pl.ds(pl.multiple_of(at, LANES), width))
        return
    for here in range(2):

        @pl.when(core == here)
        def _():
            for side in range(2):
                for k in range(hops):
                    at = (k * 2 + (here ^ side)) * width
                    body(side, k, pl.ds(at, width))


def load_kernel(source, out, mark, sem):
    mark[...] = jnp.zeros(mark.shape, F32)
    copy = pltpu.make_async_copy(source, out, sem)
    copy.start()
    copy.wait()


def reader(relative, hops, refs):
    if relative:
        return lambda side, q, k: refs[side * hops + k][q]
    return lambda side, q, k: refs[side][k, q]


def forward_kernel(relative, groups, hops, *refs):
    inputs = 2 * hops if relative else 2
    take = reader(relative, hops, refs[:inputs])
    gate_ref, up_ref, down_ref = refs[inputs : inputs + 3]
    x_ref, hid_ref, active_ref, slope_ref, gates_ref, rival_ref, other_ref, keep_ref, give_ref, total = refs[
        inputs + 3 :
    ]
    width = keep_ref.shape[-1]
    model = x_ref.shape[1]
    units = hid_ref.shape[1]
    tile = min(units, 256)

    def place(side, k, features):
        for q in range(groups):
            x_ref[q * ROWS : (q + 1) * ROWS, features] = take(side, q, k)[:ROWS]

    visit(groups, hops, width, relative, place)
    for q in range(groups):
        logit = jnp.zeros((META, ROWS), F32)
        for k in range(hops):
            for side in range(2):
                meta = take(side, q, k)[:ROWS].astype(F32)[CAP:, :ROWS]
                logit = logit + meta
        gap = column(logit[0:1] + logit[1:2] + logit[2:3])
        here = slice(q * ROWS, (q + 1) * ROWS)
        gates_ref[here, :] = jax.nn.sigmoid(gap)
        rival_ref[here, :] = jax.nn.sigmoid(-gap)
        other_ref[here, :] = column(meta[3:4])

    rows_x = x_ref[...]
    for f in range(0, units, tile):
        now = slice(f, f + tile)
        gate_pre = dot(rows_x, gate_ref[0, :, now], ((1,), (0,)))
        up_pre = dot(rows_x, up_ref[0, :, now], ((1,), (0,)))
        sigma = jax.nn.sigmoid(gate_pre)
        active = gate_pre * sigma
        active_ref[:, now] = active
        slope_ref[:, now] = sigma * (1.0 + gate_pre * (1.0 - sigma)) * up_pre
        hid_ref[:, now] = (active * up_pre).astype(BF16)
    hidden = hid_ref[...]
    for f in range(0, model, 512):
        now = slice(f, f + 512)
        total[:, now] = gates_ref[...] * dot(hidden, down_ref[0, :, now], ((1,), (0,)))

    def emit(side, k, features):
        for q in range(groups):
            rows = total[q * ROWS : (q + 1) * ROWS, features]
            if side == 0:
                keep_ref[k, q] = rows
            else:
                give_ref[k, q] = rows.astype(BF16)

    visit(groups, hops, width, relative, emit)


def backward_kernel(relative, groups, hops, *refs):
    inputs = 2 * hops if relative else 2
    take = reader(relative, hops, refs[:inputs])
    x_ref, active_ref, slope_ref, hid_ref, gates_ref, rival_ref, other_ref, down_ref = refs[inputs : inputs + 8]
    d_ref, dgate_ref, dup_ref, keep_ref, give_ref, scratch = refs[inputs + 8 :]
    experts, width = keep_ref.shape[1:]
    units = hid_ref.shape[1]
    tile = min(units, 256)

    def place(side, k, features):
        for q in range(groups):
            rows = gates_ref[q * ROWS : q * ROWS + CAP, :] * take(side, q, k)[ROWS:].astype(F32)
            rows = jnp.concatenate([rows, jnp.zeros((META, width), F32)], axis=0)
            d_ref[q * ROWS : (q + 1) * ROWS, features] = rows.astype(BF16)

    visit(groups, hops, width, relative, place)
    rows_d = d_ref[...]
    dots = jnp.zeros((rows_d.shape[0], 1), F32)
    for f in range(0, units, tile):
        now = slice(f, f + tile)
        d_hidden = dot(rows_d, down_ref[0, now, :], ((1,), (1,)))
        dgate_ref[:, now] = (d_hidden * slope_ref[:, now]).astype(BF16)
        dup_ref[:, now] = (d_hidden * active_ref[:, now]).astype(BF16)
        dots += jnp.sum(hid_ref[:, now].astype(F32) * d_hidden, axis=1, keepdims=True)
    weight = dots * rival_ref[...]
    lane = lax.broadcasted_iota(jnp.int32, (weight.shape[0], experts), 1)
    signed = jnp.where(lane == lax.axis_index("expert"), weight, 0.0) - jnp.where(
        lane == other_ref[...].astype(jnp.int32), weight, 0.0
    )
    router = jnp.zeros((experts, x_ref.shape[1]), F32)
    for piece in split3(signed):
        router = router + dot(piece.astype(BF16), x_ref[...], ((0,), (0,)))
    scratch[...] = router

    def emit(side, k, features):
        rows = scratch[:, features]
        if side == 0:
            keep_ref[k] = rows
        else:
            give_ref[k] = halves(rows).astype(BF16)

    visit(groups, hops, width, relative, emit)


def halves(rows):
    top = rows.astype(BF16).astype(F32)
    return jnp.concatenate([top, rows - top], axis=0)


def merge_kernel(keep_ref, got_ref, rkeep_ref, rgot_ref, *out_refs):
    experts = rkeep_ref.shape[1]
    hops = keep_ref.shape[0]
    for k in range(hops):
        got = rgot_ref[k].astype(F32)
        router = halves(rkeep_ref[k] + got[:experts] + got[experts:])
        put(out_refs[k], keep_ref[k] + got_ref[k].astype(F32), router)


def pass_kernel(block_ref, _, out_ref):
    out_ref[...] = block_ref[...]


def put(out_ref, blocks, router):
    groups, height, width = out_ref.shape
    spare = height - CAP - router.shape[0]
    for q in range(groups):
        rows = [blocks[q][:CAP], router]
        if spare:
            rows.append(jnp.zeros((spare, width), F32))
        out_ref[q] = jnp.concatenate(rows, axis=0).astype(BF16)


def grads_kernel(x_ref, d_ref, dgate_ref, dup_ref, hid_ref, _, gate_ref, up_ref, down_ref, mark_ref):
    rows_x = x_ref[...]
    first = ((0,), (0,))
    gate_ref[0] = dot(rows_x, dgate_ref[...], first).astype(BF16)
    up_ref[0] = dot(rows_x, dup_ref[...], first).astype(BF16)
    down_ref[0] = dot(hid_ref[...], d_ref[...], first).astype(BF16)
    mark_ref[...] = jnp.zeros(mark_ref.shape, F32)


def add_blocks(experts, parts, sends):
    router = None
    for q, send in enumerate(sends):
        block = parts[0][q].astype(F32)
        for ref in parts[1:]:
            block = block + ref[q].astype(F32)
        if router is None:
            router = halves(block[CAP : CAP + experts] + block[CAP + experts : CAP + 2 * experts])
        height, width = send.shape
        rows = [block[:CAP], router]
        if height > CAP + 2 * experts:
            rows.append(jnp.zeros((height - CAP - 2 * experts, width), F32))
        send[...] = jnp.concatenate(rows, axis=0).astype(BF16)


def sum_kernel(experts, groups, *refs):
    add_blocks(experts, refs[: len(refs) - groups - 1], refs[len(refs) - groups :])


def combine_kernel(groups, pos_ref, *refs):
    backs, mixed_ref, router_ref = refs[:groups], refs[groups], refs[groups + 1]
    experts, width = router_ref.shape
    count = mixed_ref.shape[0]
    blocks = []
    router = jnp.zeros((2 * experts, width), F32)
    for ref in backs:
        block = ref[...].astype(F32)
        router = router + block[CAP : CAP + 2 * experts]
        blocks.append(block[:CAP])
        blocks.append(jnp.zeros((ROWS - CAP, width), F32))
    rows = jnp.concatenate(blocks, axis=0).astype(BF16)
    slots = lax.broadcasted_iota(jnp.int32, (experts * ROWS, 2 * count), 0)
    select = (slots == pos_ref[...]).astype(F32)
    merged = (select[:, :count] + select[:, count:]).astype(BF16)
    mixed_ref[...] = dot(merged, rows, ((0,), (0,))).astype(BF16)
    router_ref[...] = (router[:experts] + router[experts:]).astype(BF16)


def swap(block, axis, bits):
    size = lax.axis_size(axis)
    return lax.ppermute(block, axis, [(i, i ^ bits) for i in range(size)])


def shards(tokens, expert_ids, live_tokens, replicated, w_router, w_gate, w_up, w_down, cotangent):
    groups = lax.axis_size("expert")
    hops = lax.axis_size("z")
    experts = w_router.shape[1]
    count, width = tokens.shape
    _, model, units = w_gate.shape
    rows = groups * ROWS
    height = -(-(CAP + 2 * experts) // 16) * 16
    relative = width % LANES == 0 and hops <= 4
    whole = pl.BlockSpec(memory_space=pltpu.VMEM)
    anywhere = pl.BlockSpec(memory_space=pl.ANY)
    fixed = pl.BlockSpec(memory_space=pltpu.HBM)
    shape = jax.ShapeDtypeStruct

    def call(kernel, args, outs, name, scratch=(), loose=(), cost=None, limit=4 * MIB):
        args = [pltpu.with_memory_space_constraint(a, pltpu.HBM) if i in loose else a for i, a in enumerate(args)]
        return pl.pallas_call(
            kernel,
            out_shape=tuple(outs),
            in_specs=[fixed if i in loose else whole for i in range(len(args))],
            out_specs=(whole,) * len(outs),
            scratch_shapes=list(scratch),
            compiler_params=pltpu.CompilerParams(vmem_limit_bytes=limit),
            cost_estimate=cost,
            name=name,
        )(*args)

    position, *sends = call(
        functools.partial(pack_kernel, experts),
        (live_tokens, replicated, expert_ids.T, w_router.T, tokens, cotangent),
        [shape((1, 2 * count), jnp.int32)] + [shape((ROWS + CAP, width), BF16)] * experts,
        "pack",
        scratch=[
            pltpu.SMEM(live_tokens.shape, jnp.int32),
            pltpu.SMEM(replicated.shape, jnp.int32),
            pltpu.VMEM((2, count), jnp.int32),
            pltpu.VMEM((experts, width), BF16),
            pltpu.VMEM((count, width), BF16),
            pltpu.VMEM((count, width), BF16),
            pltpu.SemaphoreType.DMA((6,)),
        ],
        loose=range(6),
    )
    arrived = [sends[0]] + [swap(sends[q], "expert", q) for q in range(1, groups)]
    def load(weight, name):
        return call(
            load_kernel,
            (weight,),
            [pltpu.VMEM(weight.shape, BF16), shape((8, LANES), F32)],
            name,
            scratch=[pltpu.SemaphoreType.DMA],
            loose=(0,),
            cost=pl.CostEstimate(flops=0, bytes_accessed=2 * 2 * model * units, transcendentals=0),
            limit=8 * MIB,
        )

    gate_w, gate_mark = load(w_gate, "load_gate")
    up_w, up_mark = load(w_up, "load_up")
    down_w, down_mark = load(w_down, "load_down")
    (stacked,) = call(
        functools.partial(stack_kernel, groups, 0, ROWS + CAP),
        (*arrived, gate_mark, up_mark),
        [shape((groups, ROWS + CAP, width), BF16)],
        "stack",
    )
    if relative:
        blocks = [stacked]
        if hops > 2:
            second = swap(stacked, "z", 2)
        if hops > 1:
            blocks.append(swap(stacked, "z", 1))
        if hops > 2:
            (relay,) = call(pass_kernel, (second, down_mark), [shape(second.shape, BF16)], "relay")
            blocks += [second, swap(relay, "z", 1)]
    else:
        blocks = [lax.all_gather(stacked, "z", axis=0, tiled=False)]
    blocks = blocks + [swap(block, "core", 1) for block in blocks]

    cost = 2 * rows * model * units
    rows_x, hidden, active, slope, gates, rival, others, keep, give = call(
        functools.partial(forward_kernel, relative, groups, hops),
        (*blocks, gate_w, up_w, down_w),
        [
            shape((rows, model), BF16),
            shape((rows, units), BF16),
            shape((rows, units), F32),
            shape((rows, units), F32),
            shape((rows, 1), F32),
            shape((rows, 1), F32),
            shape((rows, 1), F32),
            shape((hops, groups, ROWS, width), F32),
            shape((hops, groups, ROWS, width), BF16),
        ],
        "forward",
        scratch=[pltpu.VMEM((rows, model), F32)],
        cost=pl.CostEstimate(flops=3 * cost, bytes_accessed=6 * model * units, transcendentals=rows * units),
        limit=16 * MIB,
    )
    got = swap(give, "core", 1)
    rows_d, d_gate, d_up, router_keep, router_give = call(
        functools.partial(backward_kernel, relative, groups, hops),
        (*blocks, rows_x, active, slope, hidden, gates, rival, others, down_w),
        [
            shape((rows, model), BF16),
            shape((rows, units), BF16),
            shape((rows, units), BF16),
            shape((hops, experts, width), F32),
            shape((hops, 2 * experts, width), BF16),
        ],
        "backward",
        scratch=[pltpu.VMEM((experts, model), F32)],
        cost=pl.CostEstimate(flops=cost, bytes_accessed=2 * model * units, transcendentals=0),
        limit=14 * MIB,
    )
    router_got = swap(router_give, "core", 1)
    merged = call(
        merge_kernel,
        (keep, got, router_keep, router_got),
        [shape((groups, height, width), BF16)] * hops,
        "merge",
    )
    if relative:
        outs = [merged[0]] + [swap(merged[k], "z", k) for k in range(1, hops)]
    else:
        outs = lax.all_to_all(jnp.stack(merged), "z", split_axis=0, concat_axis=0, tiled=True)
        outs = [outs[k] for k in range(hops)]

    parts = 8
    once = lambda *shape: pl.BlockSpec(shape, lambda i: (0,) * len(shape))
    strip = max(units // parts, LANES)
    at = lambda i: i if units >= LANES * parts else 0
    grad_gate, grad_up, grad_down, mark = pl.pallas_call(
        grads_kernel,
        grid=(parts,),
        out_shape=(
            shape(w_gate.shape, BF16),
            shape(w_up.shape, BF16),
            shape(w_down.shape, BF16),
            shape((8, LANES), F32),
        ),
        in_specs=[
            pl.BlockSpec((rows, model // parts), lambda i: (0, i)),
            once(rows, model),
            once(rows, units),
            once(rows, units),
            pl.BlockSpec((rows, strip), lambda i: (0, at(i))),
            anywhere,
        ],
        out_specs=(
            pl.BlockSpec((1, model // parts, units), lambda i: (0, i, 0)),
            pl.BlockSpec((1, model // parts, units), lambda i: (0, i, 0)),
            pl.BlockSpec((1, strip, model), lambda i: (0, at(i), 0)),
            once(8, LANES),
        ),
        compiler_params=pltpu.CompilerParams(vmem_limit_bytes=24 * MIB),
        cost_estimate=pl.CostEstimate(flops=3 * cost, bytes_accessed=6 * model * units, transcendentals=0),
        name="grads",
    )(rows_x, rows_d, d_gate, d_up, hidden, merged[0])

    backs = call(
        functools.partial(sum_kernel, experts, groups),
        (*outs, mark),
        [shape((height, width), BF16)] * groups,
        "total",
    )
    backs = [backs[0]] + [swap(backs[q], "expert", q) for q in range(1, groups)]
    mixed, grad_router = call(
        functools.partial(combine_kernel, groups),
        (position, *backs),
        [shape((count, width), BF16), shape((experts, width), BF16)],
        "combine",
    )
    return (mixed, grad_gate, grad_up, grad_down, grad_router.T)


def solution(mesh):
    groups, etp = mesh.devices.shape
    inner = Mesh(mesh.devices.reshape(groups, etp // 2, 2), ("expert", "z", "core"))
    etp = ("z", "core")
    in_specs = (
        P("expert", etp),
        P("expert", None),
        P(),
        P(),
        P(etp, None),
        P("expert", None, etp),
        P("expert", None, etp),
        P("expert", etp, None),
        P("expert", etp),
    )
    out_specs = (
        P("expert", etp),
        P("expert", None, etp),
        P("expert", None, etp),
        P("expert", etp, None),
        P(etp, None),
    )
    return jax.shard_map(shards, mesh=inner, in_specs=in_specs, out_specs=out_specs, check_vma=False)
```

```python
import functools

import jax
import jax.numpy as jnp
from jax import lax
from jax.experimental import pallas as pl
from jax.experimental.pallas import tpu as pltpu
from jax.sharding import Mesh, PartitionSpec as P

CAPG = 32
RCAP = 8
CAP = CAPG + RCAP
META = 8
ROWS = CAP + META
MIB = 1024 * 1024
LANES = 128

F32 = jnp.float32
BF16 = jnp.bfloat16


def dot(a, b, dims):
    return lax.dot_general(a, b, (dims, ((), ())), preferred_element_type=F32)


def split3(value):
    hi = value.astype(BF16).astype(F32)
    rest = value - hi
    mid = rest.astype(BF16).astype(F32)
    return hi, mid, rest - mid


def chosen(position, experts):
    count = position.shape[1] // 2
    slots = lax.broadcasted_iota(jnp.int32, (experts * ROWS, 2 * count), 0)
    select = (slots == position).astype(F32)
    return (select[:, :count] + select[:, count:]).astype(BF16)


def pack_kernel(experts, *refs):
    sources, pos_ref, pass_ref, send_refs = refs[:6], refs[6], refs[7], refs[8 : 8 + experts]
    held, sems = [*refs[8 + experts : 13 + experts], pass_ref], refs[13 + experts]
    copies = [pltpu.make_async_copy(a, b, sems.at[i]) for i, (a, b) in enumerate(zip(sources, held))]
    for copy in copies:
        copy.start()
    for copy in copies:
        copy.wait()
    live_ref, flags_ref, ids_ref, router_ref, tok_ref, _ = held
    count, width = tok_ref.shape
    both = 2 * count
    lanes = max(experts, 8)
    group = lax.axis_index("expert")
    live = live_ref[group]
    ids = ids_ref[...]
    first, second = ids[0:1, :], ids[1:2, :]
    order = jnp.concatenate([first, second], axis=1)
    other = jnp.concatenate([second, first], axis=1)
    lane = lax.broadcasted_iota(jnp.int32, (1, both), 1)
    token = jnp.where(lane < count, lane, lane - count)
    alive = token < live
    expert_rows = lax.broadcasted_iota(jnp.int32, (lanes, both), 0)
    onehot = ((expert_rows == order) & alive).astype(F32)
    earlier = lax.broadcasted_iota(jnp.int32, (both, both), 0)
    later = lax.broadcasted_iota(jnp.int32, (both, both), 1)
    before = dot(onehot.astype(BF16), (earlier < later).astype(BF16), ((1,), (0,)))
    slot = jnp.sum(onehot * before, axis=0, keepdims=True).astype(jnp.int32)
    limit = jnp.full((1, both), CAPG, jnp.int32)
    for e in range(experts):
        limit = jnp.where(order == e, CAPG + RCAP * flags_ref[e], limit)
    kept = alive & (slot < limit)
    position = jnp.where(kept, (order ^ group) * ROWS + slot, -1)
    pos_ref[...] = position

    merged = chosen(position, experts)
    rows_x = dot(merged, tok_ref[...], ((1,), (0,)))

    logits = dot(router_ref[...], tok_ref[...], ((1,), (1,)))
    pick = lax.broadcasted_iota(jnp.int32, (experts, count), 0)
    gap = jnp.sum(
        jnp.where(pick == first, logits, 0.0) - jnp.where(pick == second, logits, 0.0),
        axis=0,
        keepdims=True,
    )
    hi, mid, low = split3(jnp.concatenate([gap, -gap], axis=1))
    meta_row = lax.broadcasted_iota(jnp.int32, (META, both), 0)
    meta = jnp.where(
        meta_row == 0,
        hi,
        jnp.where(
            meta_row == 1,
            mid,
            jnp.where(meta_row == 2, low, jnp.where(meta_row == 3, other.astype(F32), 0.0)),
        ),
    ).astype(BF16)
    span = min(width, LANES)
    near = lax.broadcasted_iota(jnp.int32, (span, both), 0)
    for e in range(experts):
        mine = ((near + e * ROWS == position) & (near < CAP)).astype(F32).astype(BF16)
        block = dot(meta, mine, ((1,), (1,)))
        if width > span:
            block = jnp.concatenate([block, jnp.zeros((META, width - span), F32)], axis=1)
        base = e * ROWS
        send_refs[e][...] = jnp.concatenate([rows_x[base : base + CAP], block], axis=0).astype(BF16)


def stack_kernel(count, *refs):
    for q in range(count):
        refs[-1][q] = refs[q][...]


def pick_kernel(relative, experts, hops, pos_ref, *refs):
    sources, sends = refs[: len(refs) - experts], refs[len(refs) - experts :]
    merged = chosen(pos_ref[...], experts)
    for k in range(hops):
        rows = dot(merged, sources[k][...] if relative else sources[0][k], ((1,), (0,)))
        for q in range(experts):
            sends[q][k] = rows[q * ROWS : q * ROWS + CAP].astype(BF16)


def column(row):
    size = row.shape[1]
    down = lax.broadcasted_iota(jnp.int32, (size, size), 0)
    across = lax.broadcasted_iota(jnp.int32, (size, size), 1)
    return jnp.sum(jnp.where(down == across, row, 0.0), axis=1, keepdims=True)


def visit(groups, hops, width, relative, body):
    core = lax.axis_index("core")
    z = lax.axis_index("z")
    if width % LANES == 0:
        for side in range(2):
            for k in range(hops):
                at = ((z ^ k if relative else k) * 2 + (core ^ side)) * width
                body(side, k, pl.ds(pl.multiple_of(at, LANES), width))
        return
    for here in range(2):

        @pl.when(core == here)
        def _():
            for side in range(2):
                for k in range(hops):
                    at = (k * 2 + (here ^ side)) * width
                    body(side, k, pl.ds(at, width))


def load_kernel(source, out, mark, sem):
    mark[...] = jnp.zeros(mark.shape, F32)
    copy = pltpu.make_async_copy(source, out, sem)
    copy.start()
    copy.wait()


def reader(relative, hops, refs):
    if relative:
        return lambda side, q, k: refs[side * hops + k][q]
    return lambda side, q, k: refs[side][k, q]


def forward_kernel(relative, groups, hops, *refs):
    inputs = 2 * hops if relative else 2
    take = reader(relative, hops, refs[:inputs])
    gate_ref, up_ref, _, down_hbm = refs[inputs : inputs + 4]
    x_ref, hid_ref, active_ref, slope_ref, gates_ref, rival_ref, other_ref, keep_ref, give_ref, down_ref = refs[
        inputs + 4 : inputs + 14
    ]
    total, sem = refs[inputs + 14 :]
    fetch = pltpu.make_async_copy(down_hbm, down_ref, sem)
    fetch.start()
    width = keep_ref.shape[-1]
    model = x_ref.shape[1]
    units = hid_ref.shape[1]
    tile = min(units, 256)

    def place(side, k, features):
        for q in range(groups):
            x_ref[q * ROWS : (q + 1) * ROWS, features] = take(side, q, k)

    visit(groups, hops, width, relative, place)
    for q in range(groups):
        logit = jnp.zeros((META, ROWS), F32)
        for k in range(hops):
            for side in range(2):
                meta = take(side, q, k).astype(F32)[CAP:, :ROWS]
                logit = logit + meta
        gap = column(logit[0:1] + logit[1:2] + logit[2:3])
        here = slice(q * ROWS, (q + 1) * ROWS)
        gates_ref[here, :] = jax.nn.sigmoid(gap)
        rival_ref[here, :] = jax.nn.sigmoid(-gap)
        other_ref[here, :] = column(meta[3:4])

    rows_x = x_ref[...]
    for f in range(0, units, tile):
        now = slice(f, f + tile)
        gate_pre = dot(rows_x, gate_ref[0, :, now], ((1,), (0,)))
        up_pre = dot(rows_x, up_ref[0, :, now], ((1,), (0,)))
        sigma = jax.nn.sigmoid(gate_pre)
        active = gate_pre * sigma
        active_ref[:, now] = active
        slope_ref[:, now] = sigma * (1.0 + gate_pre * (1.0 - sigma)) * up_pre
        hid_ref[:, now] = (active * up_pre).astype(BF16)
    hidden = hid_ref[...]
    fetch.wait()
    for f in range(0, model, 512):
        now = slice(f, f + 512)
        total[:, now] = gates_ref[...] * dot(hidden, down_ref[0, :, now], ((1,), (0,)))

    def emit(side, k, features):
        for q in range(groups):
            rows = total[q * ROWS : (q + 1) * ROWS, features]
            if side == 0:
                keep_ref[k, q] = rows
            else:
                give_ref[k, q] = rows.astype(BF16)

    visit(groups, hops, width, relative, emit)


def backward_kernel(relative, groups, hops, *refs):
    inputs = 2
    x_ref, active_ref, slope_ref, hid_ref, gates_ref, rival_ref, other_ref, down_ref = refs[inputs : inputs + 8]
    d_ref, dgate_ref, dup_ref, keep_ref, give_ref, scratch = refs[inputs + 8 :]
    experts, width = keep_ref.shape[1:]
    units = hid_ref.shape[1]
    tile = min(units, 256)

    def place(side, k, features):
        for q in range(groups):
            rows = gates_ref[q * ROWS : q * ROWS + CAP, :] * refs[side][q, k].astype(F32)
            rows = jnp.concatenate([rows, jnp.zeros((META, width), F32)], axis=0)
            d_ref[q * ROWS : (q + 1) * ROWS, features] = rows.astype(BF16)

    visit(groups, hops, width, relative, place)
    rows_d = d_ref[...]
    dots = jnp.zeros((rows_d.shape[0], 1), F32)
    for f in range(0, units, tile):
        now = slice(f, f + tile)
        d_hidden = dot(rows_d, down_ref[0, now, :], ((1,), (1,)))
        dgate_ref[:, now] = (d_hidden * slope_ref[:, now]).astype(BF16)
        dup_ref[:, now] = (d_hidden * active_ref[:, now]).astype(BF16)
        dots += jnp.sum(hid_ref[:, now].astype(F32) * d_hidden, axis=1, keepdims=True)
    weight = dots * rival_ref[...]
    lane = lax.broadcasted_iota(jnp.int32, (weight.shape[0], experts), 1)
    signed = jnp.where(lane == lax.axis_index("expert"), weight, 0.0) - jnp.where(
        lane == other_ref[...].astype(jnp.int32), weight, 0.0
    )
    router = jnp.zeros((experts, x_ref.shape[1]), F32)
    for piece in split3(signed):
        router = router + dot(piece.astype(BF16), x_ref[...], ((0,), (0,)))
    scratch[...] = router

    def emit(side, k, features):
        rows = scratch[:, features]
        if side == 0:
            keep_ref[k] = rows
        else:
            give_ref[k] = halves(rows).astype(BF16)

    visit(groups, hops, width, relative, emit)


def halves(rows):
    top = rows.astype(BF16).astype(F32)
    return jnp.concatenate([top, rows - top], axis=0)


def merge_kernel(keep_ref, got_ref, rkeep_ref, rgot_ref, *out_refs):
    experts = rkeep_ref.shape[1]
    hops = keep_ref.shape[0]
    for k in range(hops):
        got = rgot_ref[k].astype(F32)
        router = halves(rkeep_ref[k] + got[:experts] + got[experts:])
        put(out_refs[k], keep_ref[k] + got_ref[k].astype(F32), router)


def pass_kernel(block_ref, *refs):
    refs[-1][...] = block_ref[...]


def put(out_ref, blocks, router):
    groups, height, width = out_ref.shape
    spare = height - CAP - router.shape[0]
    for q in range(groups):
        rows = [blocks[q][:CAP], router]
        if spare:
            rows.append(jnp.zeros((spare, width), F32))
        out_ref[q] = jnp.concatenate(rows, axis=0).astype(BF16)


def grads_kernel(x_ref, d_ref, dgate_ref, dup_ref, hid_ref, _, gate_ref, up_ref, down_ref, mark_ref):
    rows_x = x_ref[...]
    first = ((0,), (0,))
    gate_ref[0] = dot(rows_x, dgate_ref[...], first).astype(BF16)
    up_ref[0] = dot(rows_x, dup_ref[...], first).astype(BF16)
    down_ref[0] = dot(hid_ref[...], d_ref[...], first).astype(BF16)
    mark_ref[...] = jnp.zeros(mark_ref.shape, F32)


def add_blocks(experts, parts, sends):
    router = None
    for q, send in enumerate(sends):
        block = parts[0][q].astype(F32)
        for ref in parts[1:]:
            block = block + ref[q].astype(F32)
        if router is None:
            router = halves(block[CAP : CAP + experts] + block[CAP + experts : CAP + 2 * experts])
        height, width = send.shape
        rows = [block[:CAP], router]
        if height > CAP + 2 * experts:
            rows.append(jnp.zeros((height - CAP - 2 * experts, width), F32))
        send[...] = jnp.concatenate(rows, axis=0).astype(BF16)


def sum_kernel(experts, groups, *refs):
    add_blocks(experts, refs[: len(refs) - groups - 1], refs[len(refs) - groups :])


def combine_kernel(groups, pos_ref, *refs):
    backs, mixed_ref, router_ref = refs[:groups], refs[groups], refs[groups + 1]
    experts, width = router_ref.shape
    blocks = []
    router = jnp.zeros((2 * experts, width), F32)
    for ref in backs:
        block = ref[...].astype(F32)
        router = router + block[CAP : CAP + 2 * experts]
        blocks.append(block[:CAP])
        blocks.append(jnp.zeros((ROWS - CAP, width), F32))
    rows = jnp.concatenate(blocks, axis=0).astype(BF16)
    merged = chosen(pos_ref[...], experts)
    mixed_ref[...] = dot(merged, rows, ((0,), (0,))).astype(BF16)
    router_ref[...] = (router[:experts] + router[experts:]).astype(BF16)


def swap(block, axis, bits):
    size = lax.axis_size(axis)
    return lax.ppermute(block, axis, [(i, i ^ bits) for i in range(size)])


def shards(tokens, expert_ids, live_tokens, replicated, w_router, w_gate, w_up, w_down, cotangent):
    groups = lax.axis_size("expert")
    hops = lax.axis_size("z")
    experts = w_router.shape[1]
    count, width = tokens.shape
    _, model, units = w_gate.shape
    rows = groups * ROWS
    height = -(-(CAP + 2 * experts) // 16) * 16
    relative = width % LANES == 0 and hops <= 4
    whole = pl.BlockSpec(memory_space=pltpu.VMEM)
    anywhere = pl.BlockSpec(memory_space=pl.ANY)
    fixed = pl.BlockSpec(memory_space=pltpu.HBM)
    shape = jax.ShapeDtypeStruct

    def call(kernel, args, outs, name, scratch=(), loose=(), cost=None, limit=4 * MIB):
        args = [pltpu.with_memory_space_constraint(a, pltpu.HBM) if i in loose else a for i, a in enumerate(args)]
        return pl.pallas_call(
            kernel,
            out_shape=tuple(outs),
            in_specs=[fixed if i in loose else whole for i in range(len(args))],
            out_specs=(whole,) * len(outs),
            scratch_shapes=list(scratch),
            compiler_params=pltpu.CompilerParams(vmem_limit_bytes=limit),
            cost_estimate=cost,
            name=name,
        )(*args)

    position, handed, *sends = call(
        functools.partial(pack_kernel, experts),
        (live_tokens, replicated, expert_ids.T, w_router.T, tokens, cotangent),
        [shape((1, 2 * count), jnp.int32), shape(cotangent.shape, BF16)] + [shape((ROWS, width), BF16)] * experts,
        "pack",
        scratch=[
            pltpu.SMEM(live_tokens.shape, jnp.int32),
            pltpu.SMEM(replicated.shape, jnp.int32),
            pltpu.VMEM((2, count), jnp.int32),
            pltpu.VMEM((experts, width), BF16),
            pltpu.VMEM((count, width), BF16),
            pltpu.SemaphoreType.DMA((6,)),
        ],
        loose=range(6),
    )
    def load(weight, name):
        return call(
            load_kernel,
            (weight,),
            [pltpu.VMEM(weight.shape, BF16), shape((8, LANES), F32)],
            name,
            scratch=[pltpu.SemaphoreType.DMA],
            loose=(0,),
            cost=pl.CostEstimate(flops=0, bytes_accessed=2 * 2 * model * units, transcendentals=0),
            limit=8 * MIB,
        )

    gate_w, gate_mark = load(w_gate, "load_gate")
    up_w, up_mark = load(w_up, "load_up")
    def gather(block, forward):
        if not relative:
            return [lax.all_gather(block, "z", axis=0, tiled=False)]
        blocks = [block]
        if hops > 2:
            second = swap(block, "z", 2)
        if hops > 1:
            blocks.append(swap(block, "z", 1))
        if hops > 2:
            blocks += [second, swap(forward(second, blocks[1]), "z", 1)]
        return blocks

    arrived = [sends[0]] + [swap(sends[q], "expert", q) for q in range(1, groups)]
    slices = gather(handed, lambda second, near: second)
    picked = call(
        functools.partial(pick_kernel, relative, experts, hops),
        (position, *slices),
        [shape((hops, CAP, width), BF16)] * experts,
        "pick",
    )
    (stacked,) = call(
        functools.partial(stack_kernel, groups),
        (*arrived, gate_mark, up_mark),
        [shape((groups, ROWS, width), BF16)],
        "stack",
    )

    def relay(second, near):
        return call(pass_kernel, (second, near), [shape(second.shape, BF16)], "relay")[0]

    blocks = gather(stacked, relay)
    blocks = blocks + [swap(block, "core", 1) for block in blocks]
    blocks_d = [picked[0]] + [swap(picked[q], "expert", q) for q in range(1, groups)]

    cost = 2 * rows * model * units
    rows_x, hidden, active, slope, gates, rival, others, keep, give, down_w = call(
        functools.partial(forward_kernel, relative, groups, hops),
        (*blocks, gate_w, up_w, blocks_d[1 if groups > 1 else 0], w_down),
        [
            shape((rows, model), BF16),
            shape((rows, units), BF16),
            shape((rows, units), F32),
            shape((rows, units), F32),
            shape((rows, 1), F32),
            shape((rows, 1), F32),
            shape((rows, 1), F32),
            shape((hops, groups, ROWS, width), F32),
            shape((hops, groups, ROWS, width), BF16),
            pltpu.VMEM(w_down.shape, BF16),
        ],
        "forward",
        scratch=[pltpu.VMEM((rows, model), F32), pltpu.SemaphoreType.DMA],
        loose=(len(blocks) + 3,),
        cost=pl.CostEstimate(flops=3 * cost, bytes_accessed=6 * model * units, transcendentals=rows * units),
        limit=16 * MIB,
    )
    got = swap(give, "core", 1)
    (own_d,) = call(
        functools.partial(stack_kernel, groups),
        (*blocks_d, gates),
        [shape((groups, hops, CAP, width), BF16)],
        "stack_d",
    )
    far_d = swap(own_d, "core", 1)
    rows_d, d_gate, d_up, router_keep, router_give = call(
        functools.partial(backward_kernel, relative, groups, hops),
        (own_d, far_d, rows_x, active, slope, hidden, gates, rival, others, down_w),
        [
            shape((rows, model), BF16),
            shape((rows, units), BF16),
            shape((rows, units), BF16),
            shape((hops, experts, width), F32),
            shape((hops, 2 * experts, width), BF16),
        ],
        "backward",
        scratch=[pltpu.VMEM((experts, model), F32)],
        cost=pl.CostEstimate(flops=cost, bytes_accessed=2 * model * units, transcendentals=0),
        limit=14 * MIB,
    )
    router_got = swap(router_give, "core", 1)
    merged = call(
        merge_kernel,
        (keep, got, router_keep, router_got),
        [shape((groups, height, width), BF16)] * hops,
        "merge",
    )
    if relative:
        outs = [merged[0]] + [swap(merged[k], "z", k) for k in range(1, hops)]
    else:
        outs = lax.all_to_all(jnp.stack(merged), "z", split_axis=0, concat_axis=0, tiled=True)
        outs = [outs[k] for k in range(hops)]

    parts = 8
    once = lambda *shape: pl.BlockSpec(shape, lambda i: (0,) * len(shape))
    strip = max(units // parts, LANES)
    at = lambda i: i if units >= LANES * parts else 0
    grad_gate, grad_up, grad_down, mark = pl.pallas_call(
        grads_kernel,
        grid=(parts,),
        out_shape=(
            shape(w_gate.shape, BF16),
            shape(w_up.shape, BF16),
            shape(w_down.shape, BF16),
            shape((8, LANES), F32),
        ),
        in_specs=[
            pl.BlockSpec((rows, model // parts), lambda i: (0, i)),
            once(rows, model),
            once(rows, units),
            once(rows, units),
            pl.BlockSpec((rows, strip), lambda i: (0, at(i))),
            anywhere,
        ],
        out_specs=(
            pl.BlockSpec((1, model // parts, units), lambda i: (0, i, 0)),
            pl.BlockSpec((1, model // parts, units), lambda i: (0, i, 0)),
            pl.BlockSpec((1, strip, model), lambda i: (0, at(i), 0)),
            once(8, LANES),
        ),
        compiler_params=pltpu.CompilerParams(vmem_limit_bytes=24 * MIB),
        cost_estimate=pl.CostEstimate(flops=3 * cost, bytes_accessed=6 * model * units, transcendentals=0),
        name="grads",
    )(rows_x, rows_d, d_gate, d_up, hidden, merged[0])

    backs = call(
        functools.partial(sum_kernel, experts, groups),
        (*outs, mark),
        [shape((height, width), BF16)] * groups,
        "total",
    )
    backs = [backs[0]] + [swap(backs[q], "expert", q) for q in range(1, groups)]
    mixed, grad_router = call(
        functools.partial(combine_kernel, groups),
        (position, *backs),
        [shape((count, width), BF16), shape((experts, width), BF16)],
        "combine",
    )
    return (mixed, grad_gate, grad_up, grad_down, grad_router.T)


def solution(mesh):
    groups, etp = mesh.devices.shape
    inner = Mesh(mesh.devices.reshape(groups, etp // 2, 2), ("expert", "z", "core"))
    etp = ("z", "core")
    in_specs = (
        P("expert", etp),
        P("expert", None),
        P(),
        P(),
        P(etp, None),
        P("expert", None, etp),
        P("expert", None, etp),
        P("expert", etp, None),
        P("expert", etp),
    )
    out_specs = (
        P("expert", etp),
        P("expert", None, etp),
        P("expert", None, etp),
        P("expert", etp, None),
        P(etp, None),
    )
    return jax.shard_map(shards, mesh=inner, in_specs=in_specs, out_specs=out_specs, check_vma=False)
```

```python
import functools

import jax
import jax.numpy as jnp
from jax import lax
from jax.experimental import pallas as pl
from jax.experimental.pallas import tpu as pltpu
from jax.sharding import Mesh, PartitionSpec as P

CAPG = 32
RCAP = 8
CAP = CAPG + RCAP
META = 8
ROWS = CAP + META
MIB = 1024 * 1024
LANES = 128

F32 = jnp.float32
BF16 = jnp.bfloat16


def dot(a, b, dims):
    return lax.dot_general(a, b, (dims, ((), ())), preferred_element_type=F32)


def split3(value):
    hi = value.astype(BF16).astype(F32)
    rest = value - hi
    mid = rest.astype(BF16).astype(F32)
    return hi, mid, rest - mid


def chosen(position, experts):
    count = position.shape[1] // 2
    slots = lax.broadcasted_iota(jnp.int32, (experts * ROWS, 2 * count), 0)
    select = (slots == position).astype(F32)
    return (select[:, :count] + select[:, count:]).astype(BF16)


def pack_kernel(experts, *refs):
    sources, pos_ref, pass_ref, send_refs = refs[:6], refs[6], refs[7], refs[8 : 8 + experts]
    held, sems = [*refs[8 + experts : 13 + experts], pass_ref], refs[13 + experts]
    copies = [pltpu.make_async_copy(a, b, sems.at[i]) for i, (a, b) in enumerate(zip(sources, held))]
    for copy in copies:
        copy.start()
    for copy in copies:
        copy.wait()
    live_ref, flags_ref, ids_ref, router_ref, tok_ref, _ = held
    count, width = tok_ref.shape
    both = 2 * count
    lanes = max(experts, 8)
    group = lax.axis_index("expert")
    live = live_ref[group]
    ids = ids_ref[...]
    first, second = ids[0:1, :], ids[1:2, :]
    order = jnp.concatenate([first, second], axis=1)
    other = jnp.concatenate([second, first], axis=1)
    lane = lax.broadcasted_iota(jnp.int32, (1, both), 1)
    token = jnp.where(lane < count, lane, lane - count)
    alive = token < live
    expert_rows = lax.broadcasted_iota(jnp.int32, (lanes, both), 0)
    onehot = ((expert_rows == order) & alive).astype(F32)
    earlier = lax.broadcasted_iota(jnp.int32, (both, both), 0)
    later = lax.broadcasted_iota(jnp.int32, (both, both), 1)
    before = dot(onehot.astype(BF16), (earlier < later).astype(BF16), ((1,), (0,)))
    slot = jnp.sum(onehot * before, axis=0, keepdims=True).astype(jnp.int32)
    limit = jnp.full((1, both), CAPG, jnp.int32)
    for e in range(experts):
        limit = jnp.where(order == e, CAPG + RCAP * flags_ref[e], limit)
    kept = alive & (slot < limit)
    position = jnp.where(kept, (order ^ group) * ROWS + slot, -1)
    pos_ref[...] = position

    merged = chosen(position, experts)
    rows_x = dot(merged, tok_ref[...], ((1,), (0,)))

    logits = dot(router_ref[...], tok_ref[...], ((1,), (1,)))
    pick = lax.broadcasted_iota(jnp.int32, (experts, count), 0)
    gap = jnp.sum(
        jnp.where(pick == first, logits, 0.0) - jnp.where(pick == second, logits, 0.0),
        axis=0,
        keepdims=True,
    )
    hi, mid, low = split3(jnp.concatenate([gap, -gap], axis=1))
    meta_row = lax.broadcasted_iota(jnp.int32, (META, both), 0)
    meta = jnp.where(
        meta_row == 0,
        hi,
        jnp.where(
            meta_row == 1,
            mid,
            jnp.where(meta_row == 2, low, jnp.where(meta_row == 3, other.astype(F32), 0.0)),
        ),
    ).astype(BF16)
    span = min(width, LANES)
    near = lax.broadcasted_iota(jnp.int32, (span, both), 0)
    for e in range(experts):
        mine = ((near + e * ROWS == position) & (near < CAP)).astype(F32).astype(BF16)
        block = dot(meta, mine, ((1,), (1,)))
        if width > span:
            block = jnp.concatenate([block, jnp.zeros((META, width - span), F32)], axis=1)
        base = e * ROWS
        send_refs[e][...] = jnp.concatenate([rows_x[base : base + CAP], block], axis=0).astype(BF16)


def stack_kernel(count, *refs):
    for q in range(count):
        refs[-1][q] = refs[q][...]


def pick_kernel(relative, experts, hops, pos_ref, *refs):
    sources, sends = refs[: len(refs) - experts], refs[len(refs) - experts :]
    merged = chosen(pos_ref[...], experts)
    for k in range(hops):
        rows = dot(merged, sources[k][...] if relative else sources[0][k], ((1,), (0,)))
        for q in range(experts):
            sends[q][k] = rows[q * ROWS : q * ROWS + CAP].astype(BF16)


def column(row):
    size = row.shape[1]
    down = lax.broadcasted_iota(jnp.int32, (size, size), 0)
    across = lax.broadcasted_iota(jnp.int32, (size, size), 1)
    return jnp.sum(jnp.where(down == across, row, 0.0), axis=1, keepdims=True)


def visit(groups, hops, width, relative, body):
    core = lax.axis_index("core")
    z = lax.axis_index("z")
    if width % LANES == 0:
        for side in range(2):
            for k in range(hops):
                at = ((z ^ k if relative else k) * 2 + (core ^ side)) * width
                body(side, k, pl.ds(pl.multiple_of(at, LANES), width))
        return
    for here in range(2):

        @pl.when(core == here)
        def _():
            for side in range(2):
                for k in range(hops):
                    at = (k * 2 + (here ^ side)) * width
                    body(side, k, pl.ds(at, width))


def load_kernel(source, out, mark, sem):
    mark[...] = jnp.zeros(mark.shape, F32)
    copy = pltpu.make_async_copy(source, out, sem)
    copy.start()
    copy.wait()


def reader(relative, hops, refs):
    if relative:
        return lambda side, q, k: refs[2 * side + k // 3][k % 3, q]
    return lambda side, q, k: refs[side][k, q]


def forward_kernel(relative, groups, hops, *refs):
    inputs = 4 if relative else 2
    take = reader(relative, hops, refs[:inputs])
    gate_ref, up_ref, down_ref, _ = refs[inputs : inputs + 4]
    x_ref, hid_ref, active_ref, slope_ref, gates_ref, rival_ref, other_ref, keep_ref, give_ref, total = refs[
        inputs + 4 :
    ]
    width = keep_ref.shape[-1]
    model = x_ref.shape[1]
    units = hid_ref.shape[1]
    tile = min(units, 256)

    def place(side, k, features):
        for q in range(groups):
            x_ref[q * ROWS : (q + 1) * ROWS, features] = take(side, q, k)

    visit(groups, hops, width, relative, place)
    for q in range(groups):
        logit = jnp.zeros((META, ROWS), F32)
        for k in range(hops):
            for side in range(2):
                meta = take(side, q, k).astype(F32)[CAP:, :ROWS]
                logit = logit + meta
        gap = column(logit[0:1] + logit[1:2] + logit[2:3])
        here = slice(q * ROWS, (q + 1) * ROWS)
        gates_ref[here, :] = jax.nn.sigmoid(gap)
        rival_ref[here, :] = jax.nn.sigmoid(-gap)
        other_ref[here, :] = column(meta[3:4])

    rows_x = x_ref[...]
    for f in range(0, units, tile):
        now = slice(f, f + tile)
        gate_pre = dot(rows_x, gate_ref[0, :, now], ((1,), (0,)))
        up_pre = dot(rows_x, up_ref[0, :, now], ((1,), (0,)))
        sigma = jax.nn.sigmoid(gate_pre)
        active = gate_pre * sigma
        active_ref[:, now] = active
        slope_ref[:, now] = sigma * (1.0 + gate_pre * (1.0 - sigma)) * up_pre
        hid_ref[:, now] = (active * up_pre).astype(BF16)
    hidden = hid_ref[...]
    for f in range(0, model, 512):
        now = slice(f, f + 512)
        total[:, now] = gates_ref[...] * dot(hidden, down_ref[0, :, now], ((1,), (0,)))

    def emit(side, k, features):
        for q in range(groups):
            rows = total[q * ROWS : (q + 1) * ROWS, features]
            if side == 0:
                keep_ref[k, q] = rows
            else:
                give_ref[k, q] = rows.astype(BF16)

    visit(groups, hops, width, relative, emit)


def backward_kernel(relative, groups, hops, *refs):
    inputs = 2
    x_ref, active_ref, slope_ref, hid_ref, gates_ref, rival_ref, other_ref, down_ref = refs[inputs : inputs + 8]
    d_ref, dgate_ref, dup_ref, keep_ref, give_ref, scratch = refs[inputs + 8 :]
    experts, width = keep_ref.shape[1:]
    units = hid_ref.shape[1]
    tile = min(units, 256)

    def place(side, k, features):
        for q in range(groups):
            rows = gates_ref[q * ROWS : q * ROWS + CAP, :] * refs[side][q, k].astype(F32)
            rows = jnp.concatenate([rows, jnp.zeros((META, width), F32)], axis=0)
            d_ref[q * ROWS : (q + 1) * ROWS, features] = rows.astype(BF16)

    visit(groups, hops, width, relative, place)
    rows_d = d_ref[...]
    dots = jnp.zeros((rows_d.shape[0], 1), F32)
    for f in range(0, units, tile):
        now = slice(f, f + tile)
        d_hidden = dot(rows_d, down_ref[0, now, :], ((1,), (1,)))
        dgate_ref[:, now] = (d_hidden * slope_ref[:, now]).astype(BF16)
        dup_ref[:, now] = (d_hidden * active_ref[:, now]).astype(BF16)
        dots += jnp.sum(hid_ref[:, now].astype(F32) * d_hidden, axis=1, keepdims=True)
    weight = dots * rival_ref[...]
    lane = lax.broadcasted_iota(jnp.int32, (weight.shape[0], experts), 1)
    signed = jnp.where(lane == lax.axis_index("expert"), weight, 0.0) - jnp.where(
        lane == other_ref[...].astype(jnp.int32), weight, 0.0
    )
    router = jnp.zeros((experts, x_ref.shape[1]), F32)
    for piece in split3(signed):
        router = router + dot(piece.astype(BF16), x_ref[...], ((0,), (0,)))
    scratch[...] = router

    def emit(side, k, features):
        rows = scratch[:, features]
        if side == 0:
            keep_ref[k] = rows
        else:
            give_ref[k] = halves(rows).astype(BF16)

    visit(groups, hops, width, relative, emit)


def halves(rows):
    top = rows.astype(BF16).astype(F32)
    return jnp.concatenate([top, rows - top], axis=0)


def merge_kernel(keep_ref, got_ref, rkeep_ref, rgot_ref, *out_refs):
    experts = rkeep_ref.shape[1]
    hops = keep_ref.shape[0]
    for k in range(hops):
        got = rgot_ref[k].astype(F32)
        router = halves(rkeep_ref[k] + got[:experts] + got[experts:])
        put(out_refs[k], keep_ref[k] + got_ref[k].astype(F32), router)


def relay_kernel(own_ref, near_ref, second_ref, _, __, ___, three_ref, relay_ref):
    three_ref[0] = own_ref[...]
    three_ref[1] = near_ref[...]
    three_ref[2] = second_ref[...]
    relay_ref[...] = second_ref[...]


def put(out_ref, blocks, router):
    groups, height, width = out_ref.shape
    spare = height - CAP - router.shape[0]
    for q in range(groups):
        rows = [blocks[q][:CAP], router]
        if spare:
            rows.append(jnp.zeros((spare, width), F32))
        out_ref[q] = jnp.concatenate(rows, axis=0).astype(BF16)


def grads_kernel(x_ref, d_ref, dgate_ref, dup_ref, hid_ref, _, gate_ref, up_ref, down_ref, mark_ref):
    rows_x = x_ref[...]
    first = ((0,), (0,))
    gate_ref[0] = dot(rows_x, dgate_ref[...], first).astype(BF16)
    up_ref[0] = dot(rows_x, dup_ref[...], first).astype(BF16)
    down_ref[0] = dot(hid_ref[...], d_ref[...], first).astype(BF16)
    mark_ref[...] = jnp.zeros(mark_ref.shape, F32)


def add_blocks(experts, parts, sends):
    router = None
    for q, send in enumerate(sends):
        block = parts[0][q].astype(F32)
        for ref in parts[1:]:
            block = block + ref[q].astype(F32)
        if router is None:
            router = halves(block[CAP : CAP + experts] + block[CAP + experts : CAP + 2 * experts])
        height, width = send.shape
        rows = [block[:CAP], router]
        if height > CAP + 2 * experts:
            rows.append(jnp.zeros((height - CAP - 2 * experts, width), F32))
        send[...] = jnp.concatenate(rows, axis=0).astype(BF16)


def sum_kernel(experts, groups, *refs):
    add_blocks(experts, refs[: len(refs) - groups - 1], refs[len(refs) - groups :])


def combine_kernel(groups, pos_ref, *refs):
    backs, mixed_ref, router_ref = refs[:groups], refs[groups], refs[groups + 1]
    experts, width = router_ref.shape
    blocks = []
    router = jnp.zeros((2 * experts, width), F32)
    for ref in backs:
        block = ref[...].astype(F32)
        router = router + block[CAP : CAP + 2 * experts]
        blocks.append(block[:CAP])
        blocks.append(jnp.zeros((ROWS - CAP, width), F32))
    rows = jnp.concatenate(blocks, axis=0).astype(BF16)
    merged = chosen(pos_ref[...], experts)
    mixed_ref[...] = dot(merged, rows, ((0,), (0,))).astype(BF16)
    router_ref[...] = (router[:experts] + router[experts:]).astype(BF16)


def swap(block, axis, bits):
    size = lax.axis_size(axis)
    return lax.ppermute(block, axis, [(i, i ^ bits) for i in range(size)])


def shards(tokens, expert_ids, live_tokens, replicated, w_router, w_gate, w_up, w_down, cotangent):
    groups = lax.axis_size("expert")
    hops = lax.axis_size("z")
    experts = w_router.shape[1]
    count, width = tokens.shape
    _, model, units = w_gate.shape
    rows = groups * ROWS
    height = -(-(CAP + 2 * experts) // 16) * 16
    relative = width % LANES == 0 and hops == 4
    whole = pl.BlockSpec(memory_space=pltpu.VMEM)
    anywhere = pl.BlockSpec(memory_space=pl.ANY)
    fixed = pl.BlockSpec(memory_space=pltpu.HBM)
    shape = jax.ShapeDtypeStruct

    def call(kernel, args, outs, name, scratch=(), loose=(), cost=None, limit=4 * MIB):
        args = [pltpu.with_memory_space_constraint(a, pltpu.HBM) if i in loose else a for i, a in enumerate(args)]
        return pl.pallas_call(
            kernel,
            out_shape=tuple(outs),
            in_specs=[fixed if i in loose else whole for i in range(len(args))],
            out_specs=(whole,) * len(outs),
            scratch_shapes=list(scratch),
            compiler_params=pltpu.CompilerParams(vmem_limit_bytes=limit),
            cost_estimate=cost,
            name=name,
        )(*args)

    position, handed, *sends = call(
        functools.partial(pack_kernel, experts),
        (live_tokens, replicated, expert_ids.T, w_router.T, tokens, cotangent),
        [shape((1, 2 * count), jnp.int32), shape(cotangent.shape, BF16)] + [shape((ROWS, width), BF16)] * experts,
        "pack",
        scratch=[
            pltpu.SMEM(live_tokens.shape, jnp.int32),
            pltpu.SMEM(replicated.shape, jnp.int32),
            pltpu.VMEM((2, count), jnp.int32),
            pltpu.VMEM((experts, width), BF16),
            pltpu.VMEM((count, width), BF16),
            pltpu.SemaphoreType.DMA((6,)),
        ],
        loose=range(6),
    )
    def load(weight, name):
        return call(
            load_kernel,
            (weight,),
            [pltpu.VMEM(weight.shape, BF16), shape((8, LANES), F32)],
            name,
            scratch=[pltpu.SemaphoreType.DMA],
            loose=(0,),
            cost=pl.CostEstimate(flops=0, bytes_accessed=2 * 2 * model * units, transcendentals=0),
            limit=8 * MIB,
        )

    gate_w, gate_mark = load(w_gate, "load_gate")
    up_w, up_mark = load(w_up, "load_up")
    down_w, down_mark = load(w_down, "load_down")
    def gather(block):
        if relative:
            second = swap(block, "z", 2)
            return [block, swap(block, "z", 1), second, swap(second, "z", 1)]
        return [lax.all_gather(block, "z", axis=0, tiled=False)]

    arrived = [sends[0]] + [swap(sends[q], "expert", q) for q in range(1, groups)]
    slices = gather(handed)
    picked = call(
        functools.partial(pick_kernel, relative, experts, hops),
        (position, *slices),
        [shape((hops, CAP, width), BF16)] * experts,
        "pick",
    )
    (stacked,) = call(
        functools.partial(stack_kernel, groups),
        (*arrived, gate_mark, *slices[1:3]),
        [shape((groups, ROWS, width), BF16)],
        "stack",
    )
    if relative:
        near, second = swap(stacked, "z", 1), swap(stacked, "z", 2)
        three, relay = call(
            relay_kernel,
            (stacked, near, second, up_mark, down_mark, picked[0]),
            [shape((3, *stacked.shape), BF16), shape(stacked.shape, BF16)],
            "relay",
        )
        blocks = [three, swap(relay, "z", 1)[None]]
    else:
        blocks = gather(stacked)
    blocks = blocks + [swap(block, "core", 1) for block in blocks]
    blocks_d = [picked[0]] + [swap(picked[q], "expert", q) for q in range(1, groups)]

    cost = 2 * rows * model * units
    rows_x, hidden, active, slope, gates, rival, others, keep, give = call(
        functools.partial(forward_kernel, relative, groups, hops),
        (*blocks, gate_w, up_w, down_w, picked[0]),
        [
            shape((rows, model), BF16),
            shape((rows, units), BF16),
            shape((rows, units), F32),
            shape((rows, units), F32),
            shape((rows, 1), F32),
            shape((rows, 1), F32),
            shape((rows, 1), F32),
            shape((hops, groups, ROWS, width), F32),
            shape((hops, groups, ROWS, width), BF16),
        ],
        "forward",
        scratch=[pltpu.VMEM((rows, model), F32)],
        cost=pl.CostEstimate(flops=3 * cost, bytes_accessed=6 * model * units, transcendentals=rows * units),
        limit=16 * MIB,
    )
    got = swap(give, "core", 1)
    (own_d,) = call(
        functools.partial(stack_kernel, groups),
        (*blocks_d, gates),
        [shape((groups, hops, CAP, width), BF16)],
        "stack_d",
    )
    far_d = swap(own_d, "core", 1)
    rows_d, d_gate, d_up, router_keep, router_give = call(
        functools.partial(backward_kernel, relative, groups, hops),
        (own_d, far_d, rows_x, active, slope, hidden, gates, rival, others, down_w),
        [
            shape((rows, model), BF16),
            shape((rows, units), BF16),
            shape((rows, units), BF16),
            shape((hops, experts, width), F32),
            shape((hops, 2 * experts, width), BF16),
        ],
        "backward",
        scratch=[pltpu.VMEM((experts, model), F32)],
        cost=pl.CostEstimate(flops=cost, bytes_accessed=2 * model * units, transcendentals=0),
        limit=14 * MIB,
    )
    router_got = swap(router_give, "core", 1)
    merged = call(
        merge_kernel,
        (keep, got, router_keep, router_got),
        [shape((groups, height, width), BF16)] * hops,
        "merge",
    )
    if relative:
        outs = [merged[0]] + [swap(merged[k], "z", k) for k in range(1, hops)]
    else:
        outs = lax.all_to_all(jnp.stack(merged), "z", split_axis=0, concat_axis=0, tiled=True)
        outs = [outs[k] for k in range(hops)]

    parts = 8
    once = lambda *shape: pl.BlockSpec(shape, lambda i: (0,) * len(shape))
    strip = max(units // parts, LANES)
    at = lambda i: i if units >= LANES * parts else 0
    grad_gate, grad_up, grad_down, mark = pl.pallas_call(
        grads_kernel,
        grid=(parts,),
        out_shape=(
            shape(w_gate.shape, BF16),
            shape(w_up.shape, BF16),
            shape(w_down.shape, BF16),
            shape((8, LANES), F32),
        ),
        in_specs=[
            pl.BlockSpec((rows, model // parts), lambda i: (0, i)),
            once(rows, model),
            once(rows, units),
            once(rows, units),
            pl.BlockSpec((rows, strip), lambda i: (0, at(i))),
            anywhere,
        ],
        out_specs=(
            pl.BlockSpec((1, model // parts, units), lambda i: (0, i, 0)),
            pl.BlockSpec((1, model // parts, units), lambda i: (0, i, 0)),
            pl.BlockSpec((1, strip, model), lambda i: (0, at(i), 0)),
            once(8, LANES),
        ),
        compiler_params=pltpu.CompilerParams(vmem_limit_bytes=24 * MIB),
        cost_estimate=pl.CostEstimate(flops=3 * cost, bytes_accessed=6 * model * units, transcendentals=0),
        name="grads",
    )(rows_x, rows_d, d_gate, d_up, hidden, merged[0])

    backs = call(
        functools.partial(sum_kernel, experts, groups),
        (*outs, mark),
        [shape((height, width), BF16)] * groups,
        "total",
    )
    backs = [backs[0]] + [swap(backs[q], "expert", q) for q in range(1, groups)]
    mixed, grad_router = call(
        functools.partial(combine_kernel, groups),
        (position, *backs),
        [shape((count, width), BF16), shape((experts, width), BF16)],
        "combine",
    )
    return (mixed, grad_gate, grad_up, grad_down, grad_router.T)


def solution(mesh):
    groups, etp = mesh.devices.shape
    inner = Mesh(mesh.devices.reshape(groups, etp // 2, 2), ("expert", "z", "core"))
    etp = ("z", "core")
    in_specs = (
        P("expert", etp),
        P("expert", None),
        P(),
        P(),
        P(etp, None),
        P("expert", None, etp),
        P("expert", None, etp),
        P("expert", etp, None),
        P("expert", etp),
    )
    out_specs = (
        P("expert", etp),
        P("expert", None, etp),
        P("expert", None, etp),
        P("expert", etp, None),
        P(etp, None),
    )
    return jax.shard_map(shards, mesh=inner, in_specs=in_specs, out_specs=out_specs, check_vma=False)
```

```python
import functools

import jax
import jax.numpy as jnp
from jax import lax
from jax.experimental import pallas as pl
from jax.experimental.pallas import tpu as pltpu
from jax.sharding import Mesh, PartitionSpec as P

CAPG = 32
RCAP = 8
CAP = CAPG + RCAP
META = 8
ROWS = CAP + META
MIB = 1024 * 1024
LANES = 128

F32 = jnp.float32
BF16 = jnp.bfloat16


def dot(a, b, dims):
    return lax.dot_general(a, b, (dims, ((), ())), preferred_element_type=F32)


def split3(value):
    hi = value.astype(BF16).astype(F32)
    rest = value - hi
    mid = rest.astype(BF16).astype(F32)
    return hi, mid, rest - mid


def chosen(position, experts):
    count = position.shape[1] // 2
    slots = lax.broadcasted_iota(jnp.int32, (experts * ROWS, 2 * count), 0)
    select = (slots == position).astype(F32)
    return (select[:, :count] + select[:, count:]).astype(BF16)


def pack_kernel(experts, *refs):
    sources, pos_ref, pass_ref, send_refs = refs[:6], refs[6], refs[7], refs[8 : 8 + experts]
    held, sems = [*refs[8 + experts : 13 + experts], pass_ref], refs[13 + experts]
    copies = [pltpu.make_async_copy(a, b, sems.at[i]) for i, (a, b) in enumerate(zip(sources, held))]
    for copy in copies:
        copy.start()
    for copy in copies:
        copy.wait()
    live_ref, flags_ref, ids_ref, router_ref, tok_ref, _ = held
    count, width = tok_ref.shape
    both = 2 * count
    lanes = max(experts, 8)
    group = lax.axis_index("expert")
    live = live_ref[group]
    ids = ids_ref[...]
    first, second = ids[0:1, :], ids[1:2, :]
    order = jnp.concatenate([first, second], axis=1)
    other = jnp.concatenate([second, first], axis=1)
    lane = lax.broadcasted_iota(jnp.int32, (1, both), 1)
    token = jnp.where(lane < count, lane, lane - count)
    alive = token < live
    expert_rows = lax.broadcasted_iota(jnp.int32, (lanes, both), 0)
    onehot = ((expert_rows == order) & alive).astype(F32)
    earlier = lax.broadcasted_iota(jnp.int32, (both, both), 0)
    later = lax.broadcasted_iota(jnp.int32, (both, both), 1)
    before = dot(onehot.astype(BF16), (earlier < later).astype(BF16), ((1,), (0,)))
    slot = jnp.sum(onehot * before, axis=0, keepdims=True).astype(jnp.int32)
    limit = jnp.full((1, both), CAPG, jnp.int32)
    for e in range(experts):
        limit = jnp.where(order == e, CAPG + RCAP * flags_ref[e], limit)
    kept = alive & (slot < limit)
    position = jnp.where(kept, (order ^ group) * ROWS + slot, -1)
    pos_ref[...] = position

    merged = chosen(position, experts)
    rows_x = dot(merged, tok_ref[...], ((1,), (0,)))

    logits = dot(router_ref[...], tok_ref[...], ((1,), (1,)))
    pick = lax.broadcasted_iota(jnp.int32, (experts, count), 0)
    gap = jnp.sum(
        jnp.where(pick == first, logits, 0.0) - jnp.where(pick == second, logits, 0.0),
        axis=0,
        keepdims=True,
    )
    hi, mid, low = split3(jnp.concatenate([gap, -gap], axis=1))
    meta_row = lax.broadcasted_iota(jnp.int32, (META, both), 0)
    meta = jnp.where(
        meta_row == 0,
        hi,
        jnp.where(
            meta_row == 1,
            mid,
            jnp.where(meta_row == 2, low, jnp.where(meta_row == 3, other.astype(F32), 0.0)),
        ),
    ).astype(BF16)
    span = min(width, LANES)
    near = lax.broadcasted_iota(jnp.int32, (span, both), 0)
    for e in range(experts):
        mine = ((near + e * ROWS == position) & (near < CAP)).astype(F32).astype(BF16)
        block = dot(meta, mine, ((1,), (1,)))
        if width > span:
            block = jnp.concatenate([block, jnp.zeros((META, width - span), F32)], axis=1)
        base = e * ROWS
        send_refs[e][...] = jnp.concatenate([rows_x[base : base + CAP], block], axis=0).astype(BF16)


def stack_kernel(count, *refs):
    for q in range(count):
        refs[-1][q] = refs[q][...]


def join_kernel(groups, _, __, *refs):
    blocks_d, blocks_x, own_x, own_d = refs[:groups], refs[groups:-2], refs[-2], refs[-1]
    for q in range(groups):
        own_d[q] = blocks_d[q][...]
    if len(blocks_x) == 1:
        own_x[...] = blocks_x[0][...]
    else:
        for k in range(len(blocks_x)):
            own_x[k] = blocks_x[k][...]


def pick_kernel(relative, experts, hops, pos_ref, *refs):
    sources, sends = refs[: len(refs) - experts], refs[len(refs) - experts :]
    merged = chosen(pos_ref[...], experts)
    for k in range(hops):
        rows = dot(merged, sources[k][...] if relative else sources[0][k], ((1,), (0,)))
        for q in range(experts):
            sends[q][k] = rows[q * ROWS : q * ROWS + CAP].astype(BF16)


def column(row):
    size = row.shape[1]
    down = lax.broadcasted_iota(jnp.int32, (size, size), 0)
    across = lax.broadcasted_iota(jnp.int32, (size, size), 1)
    return jnp.sum(jnp.where(down == across, row, 0.0), axis=1, keepdims=True)


def visit(groups, hops, width, relative, body):
    core = lax.axis_index("core")
    z = lax.axis_index("z")
    if width % LANES == 0:
        for side in range(2):
            for k in range(hops):
                at = ((z ^ k if relative else k) * 2 + (core ^ side)) * width
                body(side, k, pl.ds(pl.multiple_of(at, LANES), width))
        return
    for here in range(2):

        @pl.when(core == here)
        def _():
            for side in range(2):
                for k in range(hops):
                    at = (k * 2 + (here ^ side)) * width
                    body(side, k, pl.ds(at, width))


def load_kernel(source, out, mark, sem):
    mark[...] = jnp.zeros(mark.shape, F32)
    copy = pltpu.make_async_copy(source, out, sem)
    copy.start()
    copy.wait()


def forward_kernel(relative, groups, hops, *refs):
    sides, (gate_ref, up_ref, down_ref) = refs[:2], refs[2:5]
    x_ref, hid_ref, active_ref, slope_ref, gates_ref, rival_ref, other_ref, keep_ref, give_ref, total = refs[
        5:
    ]
    width = keep_ref.shape[-1]
    model = x_ref.shape[1]
    units = hid_ref.shape[1]
    tile = min(units, 256)

    def place(side, k, features):
        for q in range(groups):
            x_ref[q * ROWS : (q + 1) * ROWS, features] = sides[side][k, q]

    visit(groups, hops, width, relative, place)
    for q in range(groups):
        logit = jnp.zeros((META, ROWS), F32)
        for k in range(hops):
            for side in range(2):
                meta = sides[side][k, q].astype(F32)[CAP:, :ROWS]
                logit = logit + meta
        gap = column(logit[0:1] + logit[1:2] + logit[2:3])
        here = slice(q * ROWS, (q + 1) * ROWS)
        gates_ref[here, :] = jax.nn.sigmoid(gap)
        rival_ref[here, :] = jax.nn.sigmoid(-gap)
        other_ref[here, :] = column(meta[3:4])

    rows_x = x_ref[...]
    for f in range(0, units, tile):
        now = slice(f, f + tile)
        gate_pre = dot(rows_x, gate_ref[0, :, now], ((1,), (0,)))
        up_pre = dot(rows_x, up_ref[0, :, now], ((1,), (0,)))
        sigma = jax.nn.sigmoid(gate_pre)
        active = gate_pre * sigma
        active_ref[:, now] = active
        slope_ref[:, now] = sigma * (1.0 + gate_pre * (1.0 - sigma)) * up_pre
        hid_ref[:, now] = (active * up_pre).astype(BF16)
    hidden = hid_ref[...]
    for f in range(0, model, 512):
        now = slice(f, f + 512)
        total[:, now] = gates_ref[...] * dot(hidden, down_ref[0, :, now], ((1,), (0,)))

    def emit(side, k, features):
        for q in range(groups):
            rows = total[q * ROWS : (q + 1) * ROWS, features]
            if side == 0:
                keep_ref[k, q] = rows
            else:
                give_ref[k, q] = rows.astype(BF16)

    visit(groups, hops, width, relative, emit)


def backward_kernel(relative, groups, hops, *refs):
    inputs = 2
    x_ref, active_ref, slope_ref, hid_ref, gates_ref, rival_ref, other_ref, down_ref = refs[inputs : inputs + 8]
    d_ref, dgate_ref, dup_ref, keep_ref, give_ref, scratch = refs[inputs + 8 :]
    experts, width = keep_ref.shape[1:]
    units = hid_ref.shape[1]
    tile = min(units, 256)

    def place(side, k, features):
        for q in range(groups):
            rows = gates_ref[q * ROWS : q * ROWS + CAP, :] * refs[side][q, k].astype(F32)
            rows = jnp.concatenate([rows, jnp.zeros((META, width), F32)], axis=0)
            d_ref[q * ROWS : (q + 1) * ROWS, features] = rows.astype(BF16)

    visit(groups, hops, width, relative, place)
    rows_d = d_ref[...]
    dots = jnp.zeros((rows_d.shape[0], 1), F32)
    for f in range(0, units, tile):
        now = slice(f, f + tile)
        d_hidden = dot(rows_d, down_ref[0, now, :], ((1,), (1,)))
        dgate_ref[:, now] = (d_hidden * slope_ref[:, now]).astype(BF16)
        dup_ref[:, now] = (d_hidden * active_ref[:, now]).astype(BF16)
        dots += jnp.sum(hid_ref[:, now].astype(F32) * d_hidden, axis=1, keepdims=True)
    weight = dots * rival_ref[...]
    lane = lax.broadcasted_iota(jnp.int32, (weight.shape[0], experts), 1)
    signed = jnp.where(lane == lax.axis_index("expert"), weight, 0.0) - jnp.where(
        lane == other_ref[...].astype(jnp.int32), weight, 0.0
    )
    router = jnp.zeros((experts, x_ref.shape[1]), F32)
    for piece in split3(signed):
        router = router + dot(piece.astype(BF16), x_ref[...], ((0,), (0,)))
    scratch[...] = router

    def emit(side, k, features):
        rows = scratch[:, features]
        if side == 0:
            keep_ref[k] = rows
        else:
            give_ref[k] = halves(rows).astype(BF16)

    visit(groups, hops, width, relative, emit)


def halves(rows):
    top = rows.astype(BF16).astype(F32)
    return jnp.concatenate([top, rows - top], axis=0)


def merge_kernel(keep_ref, got_ref, rkeep_ref, rgot_ref, *out_refs):
    experts = rkeep_ref.shape[1]
    hops = keep_ref.shape[0]
    for k in range(hops):
        got = rgot_ref[k].astype(F32)
        router = halves(rkeep_ref[k] + got[:experts] + got[experts:])
        put(out_refs[k], keep_ref[k] + got_ref[k].astype(F32), router)


def put(out_ref, blocks, router):
    groups, height, width = out_ref.shape
    spare = height - CAP - router.shape[0]
    for q in range(groups):
        rows = [blocks[q][:CAP], router]
        if spare:
            rows.append(jnp.zeros((spare, width), F32))
        out_ref[q] = jnp.concatenate(rows, axis=0).astype(BF16)


def grads_kernel(x_ref, d_ref, dgate_ref, dup_ref, hid_ref, _, gate_ref, up_ref, down_ref, mark_ref):
    rows_x = x_ref[...]
    first = ((0,), (0,))
    gate_ref[0] = dot(rows_x, dgate_ref[...], first).astype(BF16)
    up_ref[0] = dot(rows_x, dup_ref[...], first).astype(BF16)
    down_ref[0] = dot(hid_ref[...], d_ref[...], first).astype(BF16)
    mark_ref[...] = jnp.zeros(mark_ref.shape, F32)


def add_blocks(experts, parts, sends):
    router = None
    for q, send in enumerate(sends):
        block = parts[0][q].astype(F32)
        for ref in parts[1:]:
            block = block + ref[q].astype(F32)
        if router is None:
            router = halves(block[CAP : CAP + experts] + block[CAP + experts : CAP + 2 * experts])
        height, width = send.shape
        rows = [block[:CAP], router]
        if height > CAP + 2 * experts:
            rows.append(jnp.zeros((height - CAP - 2 * experts, width), F32))
        send[...] = jnp.concatenate(rows, axis=0).astype(BF16)


def sum_kernel(experts, groups, *refs):
    add_blocks(experts, refs[: len(refs) - groups - 1], refs[len(refs) - groups :])


def combine_kernel(groups, pos_ref, *refs):
    backs, mixed_ref, router_ref = refs[:groups], refs[groups], refs[groups + 1]
    experts, width = router_ref.shape
    blocks = []
    router = jnp.zeros((2 * experts, width), F32)
    for ref in backs:
        block = ref[...].astype(F32)
        router = router + block[CAP : CAP + 2 * experts]
        blocks.append(block[:CAP])
        blocks.append(jnp.zeros((ROWS - CAP, width), F32))
    rows = jnp.concatenate(blocks, axis=0).astype(BF16)
    merged = chosen(pos_ref[...], experts)
    mixed_ref[...] = dot(merged, rows, ((0,), (0,))).astype(BF16)
    router_ref[...] = (router[:experts] + router[experts:]).astype(BF16)


def swap(block, axis, bits):
    size = lax.axis_size(axis)
    return lax.ppermute(block, axis, [(i, i ^ bits) for i in range(size)])


def shards(tokens, expert_ids, live_tokens, replicated, w_router, w_gate, w_up, w_down, cotangent):
    groups = lax.axis_size("expert")
    hops = lax.axis_size("z")
    experts = w_router.shape[1]
    count, width = tokens.shape
    _, model, units = w_gate.shape
    rows = groups * ROWS
    height = -(-(CAP + 2 * experts) // 16) * 16
    relative = width % LANES == 0 and hops == 4
    whole = pl.BlockSpec(memory_space=pltpu.VMEM)
    anywhere = pl.BlockSpec(memory_space=pl.ANY)
    fixed = pl.BlockSpec(memory_space=pltpu.HBM)
    shape = jax.ShapeDtypeStruct

    def call(kernel, args, outs, name, scratch=(), loose=(), cost=None, limit=4 * MIB):
        args = [pltpu.with_memory_space_constraint(a, pltpu.HBM) if i in loose else a for i, a in enumerate(args)]
        return pl.pallas_call(
            kernel,
            out_shape=tuple(outs),
            in_specs=[fixed if i in loose else whole for i in range(len(args))],
            out_specs=(whole,) * len(outs),
            scratch_shapes=list(scratch),
            compiler_params=pltpu.CompilerParams(vmem_limit_bytes=limit),
            cost_estimate=cost,
            name=name,
        )(*args)

    position, handed, *sends = call(
        functools.partial(pack_kernel, experts),
        (live_tokens, replicated, expert_ids.T, w_router.T, tokens, cotangent),
        [shape((1, 2 * count), jnp.int32), shape(cotangent.shape, BF16)] + [shape((ROWS, width), BF16)] * experts,
        "pack",
        scratch=[
            pltpu.SMEM(live_tokens.shape, jnp.int32),
            pltpu.SMEM(replicated.shape, jnp.int32),
            pltpu.VMEM((2, count), jnp.int32),
            pltpu.VMEM((experts, width), BF16),
            pltpu.VMEM((count, width), BF16),
            pltpu.SemaphoreType.DMA((6,)),
        ],
        loose=range(6),
    )
    def load(weight, name):
        return call(
            load_kernel,
            (weight,),
            [pltpu.VMEM(weight.shape, BF16), shape((8, LANES), F32)],
            name,
            scratch=[pltpu.SemaphoreType.DMA],
            loose=(0,),
            cost=pl.CostEstimate(flops=0, bytes_accessed=2 * 2 * model * units, transcendentals=0),
            limit=8 * MIB,
        )

    gate_w, gate_mark = load(w_gate, "load_gate")
    up_w, up_mark = load(w_up, "load_up")
    down_w, down_mark = load(w_down, "load_down")
    def gather(block):
        if relative:
            second = swap(block, "z", 2)
            return [block, swap(block, "z", 1), second, swap(second, "z", 1)]
        return [lax.all_gather(block, "z", axis=0, tiled=False)]

    arrived = [sends[0]] + [swap(sends[q], "expert", q) for q in range(1, groups)]
    slices = gather(handed)
    picked = call(
        functools.partial(pick_kernel, relative, experts, hops),
        (position, *slices),
        [shape((hops, CAP, width), BF16)] * experts,
        "pick",
    )
    (stacked,) = call(
        functools.partial(stack_kernel, groups),
        (*arrived, gate_mark, *slices[1:3]),
        [shape((groups, ROWS, width), BF16)],
        "stack",
    )
    blocks_x = [stacked] + [swap(stacked, "z", k) for k in range(1, hops)] if relative else gather(stacked)
    blocks_d = [picked[0]] + [swap(picked[q], "expert", q) for q in range(1, groups)]
    own_x, own_d = call(
        functools.partial(join_kernel, groups),
        (up_mark, down_mark, *blocks_d, *blocks_x),
        [shape((hops, *stacked.shape), BF16), shape((groups, *picked[0].shape), BF16)],
        "join",
    )
    far_x = swap(own_x, "core", 1)
    far_d = swap(own_d, "core", 1)

    cost = 2 * rows * model * units
    rows_x, hidden, active, slope, gates, rival, others, keep, give = call(
        functools.partial(forward_kernel, relative, groups, hops),
        (own_x, far_x, gate_w, up_w, down_w),
        [
            shape((rows, model), BF16),
            shape((rows, units), BF16),
            shape((rows, units), F32),
            shape((rows, units), F32),
            shape((rows, 1), F32),
            shape((rows, 1), F32),
            shape((rows, 1), F32),
            shape((hops, groups, ROWS, width), F32),
            shape((hops, groups, ROWS, width), BF16),
        ],
        "forward",
        scratch=[pltpu.VMEM((rows, model), F32)],
        cost=pl.CostEstimate(flops=3 * cost, bytes_accessed=6 * model * units, transcendentals=rows * units),
        limit=16 * MIB,
    )
    got = swap(give, "core", 1)
    rows_d, d_gate, d_up, router_keep, router_give = call(
        functools.partial(backward_kernel, relative, groups, hops),
        (own_d, far_d, rows_x, active, slope, hidden, gates, rival, others, down_w),
        [
            shape((rows, model), BF16),
            shape((rows, units), BF16),
            shape((rows, units), BF16),
            shape((hops, experts, width), F32),
            shape((hops, 2 * experts, width), BF16),
        ],
        "backward",
        scratch=[pltpu.VMEM((experts, model), F32)],
        cost=pl.CostEstimate(flops=cost, bytes_accessed=2 * model * units, transcendentals=0),
        limit=14 * MIB,
    )
    router_got = swap(router_give, "core", 1)
    merged = call(
        merge_kernel,
        (keep, got, router_keep, router_got),
        [shape((groups, height, width), BF16)] * hops,
        "merge",
    )
    if relative:
        outs = [merged[0]] + [swap(merged[k], "z", k) for k in range(hops - 1, 0, -1)]
    else:
        outs = lax.all_to_all(jnp.stack(merged), "z", split_axis=0, concat_axis=0, tiled=True)
        outs = [outs[k] for k in range(hops)]

    parts = 8
    once = lambda *shape: pl.BlockSpec(shape, lambda i: (0,) * len(shape))
    strip = max(units // parts, LANES)
    at = lambda i: i if units >= LANES * parts else 0
    grad_gate, grad_up, grad_down, mark = pl.pallas_call(
        grads_kernel,
        grid=(parts,),
        out_shape=(
            shape(w_gate.shape, BF16),
            shape(w_up.shape, BF16),
            shape(w_down.shape, BF16),
            shape((8, LANES), F32),
        ),
        in_specs=[
            pl.BlockSpec((rows, model // parts), lambda i: (0, i)),
            once(rows, model),
            once(rows, units),
            once(rows, units),
            pl.BlockSpec((rows, strip), lambda i: (0, at(i))),
            anywhere,
        ],
        out_specs=(
            pl.BlockSpec((1, model // parts, units), lambda i: (0, i, 0)),
            pl.BlockSpec((1, model // parts, units), lambda i: (0, i, 0)),
            pl.BlockSpec((1, strip, model), lambda i: (0, at(i), 0)),
            once(8, LANES),
        ),
        compiler_params=pltpu.CompilerParams(vmem_limit_bytes=24 * MIB),
        cost_estimate=pl.CostEstimate(flops=3 * cost, bytes_accessed=6 * model * units, transcendentals=0),
        name="grads",
    )(rows_x, rows_d, d_gate, d_up, hidden, merged[0])

    backs = call(
        functools.partial(sum_kernel, experts, groups),
        (*outs, mark),
        [shape((height, width), BF16)] * groups,
        "total",
    )
    backs = [backs[0]] + [swap(backs[q], "expert", q) for q in range(1, groups)]
    mixed, grad_router = call(
        functools.partial(combine_kernel, groups),
        (position, *backs),
        [shape((count, width), BF16), shape((experts, width), BF16)],
        "combine",
    )
    return (mixed, grad_gate, grad_up, grad_down, grad_router.T)


def solution(mesh):
    groups, etp = mesh.devices.shape
    inner = Mesh(mesh.devices.reshape(groups, etp // 2, 2), ("expert", "z", "core"))
    etp = ("z", "core")
    in_specs = (
        P("expert", etp),
        P("expert", None),
        P(),
        P(),
        P(etp, None),
        P("expert", None, etp),
        P("expert", None, etp),
        P("expert", etp, None),
        P("expert", etp),
    )
    out_specs = (
        P("expert", etp),
        P("expert", None, etp),
        P("expert", None, etp),
        P("expert", etp, None),
        P(etp, None),
    )
    return jax.shard_map(shards, mesh=inner, in_specs=in_specs, out_specs=out_specs, check_vma=False)
```

```python
import functools

import jax
import jax.numpy as jnp
from jax import lax
from jax.experimental import pallas as pl
from jax.experimental.pallas import tpu as pltpu
from jax.sharding import Mesh, PartitionSpec as P

CAPG = 32
RCAP = 8
CAP = CAPG + RCAP
META = 8
ROWS = CAP + META
MIB = 1024 * 1024
LANES = 128
PARTS = 4

F32 = jnp.float32
BF16 = jnp.bfloat16


def dot(a, b, dims):
    return lax.dot_general(a, b, (dims, ((), ())), preferred_element_type=F32)


def split3(value):
    hi = value.astype(BF16).astype(F32)
    rest = value - hi
    mid = rest.astype(BF16).astype(F32)
    return hi, mid, rest - mid


def chosen(position, experts):
    count = position.shape[1] // 2
    slots = lax.broadcasted_iota(jnp.int32, (experts * ROWS, 2 * count), 0)
    select = (slots == position).astype(F32)
    return (select[:, :count] + select[:, count:]).astype(BF16)


def pack_kernel(experts, *refs):
    sources, pos_ref, pass_ref, send_refs = refs[:6], refs[6], refs[7], refs[8 : 8 + experts]
    held, sems = [*refs[8 + experts : 13 + experts], pass_ref], refs[13 + experts]
    copies = [pltpu.make_async_copy(a, b, sems.at[i]) for i, (a, b) in enumerate(zip(sources, held))]
    for copy in copies:
        copy.start()
    for copy in copies:
        copy.wait()
    live_ref, flags_ref, ids_ref, router_ref, tok_ref, _ = held
    count, width = tok_ref.shape
    both = 2 * count
    lanes = max(experts, 8)
    group = lax.axis_index("expert")
    live = live_ref[group]
    ids = ids_ref[...]
    first, second = ids[0:1, :], ids[1:2, :]
    order = jnp.concatenate([first, second], axis=1)
    other = jnp.concatenate([second, first], axis=1)
    lane = lax.broadcasted_iota(jnp.int32, (1, both), 1)
    token = jnp.where(lane < count, lane, lane - count)
    alive = token < live
    expert_rows = lax.broadcasted_iota(jnp.int32, (lanes, both), 0)
    onehot = ((expert_rows == order) & alive).astype(F32)
    earlier = lax.broadcasted_iota(jnp.int32, (both, both), 0)
    later = lax.broadcasted_iota(jnp.int32, (both, both), 1)
    before = dot(onehot.astype(BF16), (earlier < later).astype(BF16), ((1,), (0,)))
    slot = jnp.sum(onehot * before, axis=0, keepdims=True).astype(jnp.int32)
    limit = jnp.full((1, both), CAPG, jnp.int32)
    for e in range(experts):
        limit = jnp.where(order == e, CAPG + RCAP * flags_ref[e], limit)
    kept = alive & (slot < limit)
    position = jnp.where(kept, (order ^ group) * ROWS + slot, -1)
    pos_ref[...] = position

    merged = chosen(position, experts)
    rows_x = dot(merged, tok_ref[...], ((1,), (0,)))

    logits = dot(router_ref[...], tok_ref[...], ((1,), (1,)))
    pick = lax.broadcasted_iota(jnp.int32, (experts, count), 0)
    gap = jnp.sum(
        jnp.where(pick == first, logits, 0.0) - jnp.where(pick == second, logits, 0.0),
        axis=0,
        keepdims=True,
    )
    hi, mid, low = split3(jnp.concatenate([gap, -gap], axis=1))
    meta_row = lax.broadcasted_iota(jnp.int32, (META, both), 0)
    meta = jnp.where(
        meta_row == 0,
        hi,
        jnp.where(
            meta_row == 1,
            mid,
            jnp.where(meta_row == 2, low, jnp.where(meta_row == 3, other.astype(F32), 0.0)),
        ),
    ).astype(BF16)
    span = min(width, LANES)
    near = lax.broadcasted_iota(jnp.int32, (span, both), 0)
    for e in range(experts):
        mine = ((near + e * ROWS == position) & (near < CAP)).astype(F32).astype(BF16)
        block = dot(meta, mine, ((1,), (1,)))
        if width > span:
            block = jnp.concatenate([block, jnp.zeros((META, width - span), F32)], axis=1)
        base = e * ROWS
        send_refs[e][...] = jnp.concatenate([rows_x[base : base + CAP], block], axis=0).astype(BF16)


def stack_kernel(count, *refs):
    for q in range(count):
        refs[-1][q] = refs[q][...]


def join_kernel(*refs):
    blocks, out_ref = refs[:-2], refs[-1]
    if len(blocks) == 1:
        out_ref[...] = blocks[0][...]
    else:
        for k, block in enumerate(blocks):
            out_ref[k] = block[...]


def pick_kernel(relative, experts, hops, pos_ref, *refs):
    sources, sends = refs[: len(refs) - experts - 2], refs[len(refs) - experts :]
    merged = chosen(pos_ref[...], experts)
    for k in range(hops):
        rows = dot(merged, sources[k][...] if relative else sources[0][k], ((1,), (0,)))
        for q in range(experts):
            sends[q][k] = rows[q * ROWS : q * ROWS + CAP].astype(BF16)


def column(row):
    size = row.shape[1]
    down = lax.broadcasted_iota(jnp.int32, (size, size), 0)
    across = lax.broadcasted_iota(jnp.int32, (size, size), 1)
    return jnp.sum(jnp.where(down == across, row, 0.0), axis=1, keepdims=True)


def visit(groups, hops, width, relative, body):
    core = lax.axis_index("core")
    z = lax.axis_index("z")
    if width % LANES == 0:
        for side in range(2):
            for k in range(hops):
                at = ((z ^ k if relative else k) * 2 + (core ^ side)) * width
                body(side, k, pl.ds(pl.multiple_of(at, LANES), width))
        return
    for here in range(2):

        @pl.when(core == here)
        def _():
            for side in range(2):
                for k in range(hops):
                    at = (k * 2 + (here ^ side)) * width
                    body(side, k, pl.ds(at, width))


def load_kernel(start, source, out, mark, sems):
    mark[...] = jnp.zeros(mark.shape, F32)
    copies = []
    part = out.shape[0] // PARTS
    for n in range(PARTS):
        there = source.at[0, pl.ds(start + n * part, part)]
        copies.append(pltpu.make_async_copy(there, out.at[pl.ds(n * part, part)], sems.at[n]))
        copies[-1].start()
    for copy in copies:
        copy.wait()


def forward_kernel(relative, groups, hops, *refs):
    sides, (gate_ref, up_a_ref, up_b_ref, down_ref) = refs[:2], refs[2:6]
    x_ref, hid_ref, active_ref, slope_ref, gates_ref, rival_ref, other_ref, keep_ref, give_ref, total = refs[
        7:
    ]
    width = keep_ref.shape[-1]
    model = x_ref.shape[1]
    units = hid_ref.shape[1]
    tile = min(units, 256)

    def place(side, k, features):
        for q in range(groups):
            x_ref[q * ROWS : (q + 1) * ROWS, features] = sides[side][k, q]

    visit(groups, hops, width, relative, place)
    for q in range(groups):
        logit = jnp.zeros((META, ROWS), F32)
        for k in range(hops):
            for side in range(2):
                meta = sides[side][k, q].astype(F32)[CAP:, :ROWS]
                logit = logit + meta
        gap = column(logit[0:1] + logit[1:2] + logit[2:3])
        here = slice(q * ROWS, (q + 1) * ROWS)
        gates_ref[here, :] = jax.nn.sigmoid(gap)
        rival_ref[here, :] = jax.nn.sigmoid(-gap)
        other_ref[here, :] = column(meta[3:4])

    rows_x = x_ref[...]
    half = up_a_ref.shape[0]
    for f in range(0, units, tile):
        now = slice(f, f + tile)
        gate_pre = dot(rows_x, gate_ref[:, now], ((1,), (0,)))
        up_pre = dot(rows_x[:, :half], up_a_ref[:, now], ((1,), (0,)))
        up_pre = up_pre + dot(rows_x[:, half:], up_b_ref[:, now], ((1,), (0,)))
        sigma = jax.nn.sigmoid(gate_pre)
        active = gate_pre * sigma
        active_ref[:, now] = active
        slope_ref[:, now] = sigma * (1.0 + gate_pre * (1.0 - sigma)) * up_pre
        hid_ref[:, now] = (active * up_pre).astype(BF16)
    hidden = hid_ref[...]
    for f in range(0, model, 512):
        now = slice(f, f + 512)
        total[:, now] = gates_ref[...] * dot(hidden, down_ref[:, now], ((1,), (0,)))

    def emit(side, k, features):
        for q in range(groups):
            rows = total[q * ROWS : (q + 1) * ROWS, features]
            if side == 0:
                keep_ref[k, q] = rows
            else:
                give_ref[k, q] = rows.astype(BF16)

    visit(groups, hops, width, relative, emit)


def backward_kernel(relative, groups, hops, *refs):
    inputs = 2
    x_ref, active_ref, slope_ref, hid_ref, gates_ref, rival_ref, other_ref, down_ref = refs[inputs : inputs + 8]
    d_ref, dgate_ref, dup_ref, keep_ref, give_ref, scratch = refs[inputs + 8 :]
    experts, width = keep_ref.shape[1:]
    units = hid_ref.shape[1]
    tile = min(units, 256)

    def place(side, k, features):
        for q in range(groups):
            rows = gates_ref[q * ROWS : q * ROWS + CAP, :] * refs[side][q, k].astype(F32)
            rows = jnp.concatenate([rows, jnp.zeros((META, width), F32)], axis=0)
            d_ref[q * ROWS : (q + 1) * ROWS, features] = rows.astype(BF16)

    visit(groups, hops, width, relative, place)
    rows_d = d_ref[...]
    dots = jnp.zeros((rows_d.shape[0], 1), F32)
    for f in range(0, units, tile):
        now = slice(f, f + tile)
        d_hidden = dot(rows_d, down_ref[now, :], ((1,), (1,)))
        dgate_ref[:, now] = (d_hidden * slope_ref[:, now]).astype(BF16)
        dup_ref[:, now] = (d_hidden * active_ref[:, now]).astype(BF16)
        dots += jnp.sum(hid_ref[:, now].astype(F32) * d_hidden, axis=1, keepdims=True)
    weight = dots * rival_ref[...]
    lane = lax.broadcasted_iota(jnp.int32, (weight.shape[0], experts), 1)
    signed = jnp.where(lane == lax.axis_index("expert"), weight, 0.0) - jnp.where(
        lane == other_ref[...].astype(jnp.int32), weight, 0.0
    )
    router = jnp.zeros((experts, x_ref.shape[1]), F32)
    for piece in split3(signed):
        router = router + dot(piece.astype(BF16), x_ref[...], ((0,), (0,)))
    scratch[...] = router

    def emit(side, k, features):
        rows = scratch[:, features]
        if side == 0:
            keep_ref[k] = rows
        else:
            give_ref[k] = halves(rows).astype(BF16)

    visit(groups, hops, width, relative, emit)


def halves(rows):
    top = rows.astype(BF16).astype(F32)
    return jnp.concatenate([top, rows - top], axis=0)


def merge_kernel(keep_ref, got_ref, rkeep_ref, rgot_ref, *out_refs):
    experts = rkeep_ref.shape[1]
    hops = keep_ref.shape[0]
    for k in range(hops):
        got = rgot_ref[k].astype(F32)
        router = halves(rkeep_ref[k] + got[:experts] + got[experts:])
        put(out_refs[k], keep_ref[k] + got_ref[k].astype(F32), router)


def put(out_ref, blocks, router):
    groups, height, width = out_ref.shape
    spare = height - CAP - router.shape[0]
    for q in range(groups):
        rows = [blocks[q][:CAP], router]
        if spare:
            rows.append(jnp.zeros((spare, width), F32))
        out_ref[q] = jnp.concatenate(rows, axis=0).astype(BF16)


def grads_kernel(x_ref, d_ref, dgate_ref, dup_ref, hid_ref, _, gate_ref, up_ref, down_ref, mark_ref):
    rows_x = x_ref[...]
    first = ((0,), (0,))
    gate_ref[0] = dot(rows_x, dgate_ref[...], first).astype(BF16)
    up_ref[0] = dot(rows_x, dup_ref[...], first).astype(BF16)
    down_ref[0] = dot(hid_ref[...], d_ref[...], first).astype(BF16)
    mark_ref[...] = jnp.zeros(mark_ref.shape, F32)


def add_blocks(experts, parts, sends):
    router = None
    for q, send in enumerate(sends):
        block = parts[0][q].astype(F32)
        for ref in parts[1:]:
            block = block + ref[q].astype(F32)
        if router is None:
            router = halves(block[CAP : CAP + experts] + block[CAP + experts : CAP + 2 * experts])
        height, width = send.shape
        rows = [block[:CAP], router]
        if height > CAP + 2 * experts:
            rows.append(jnp.zeros((height - CAP - 2 * experts, width), F32))
        send[...] = jnp.concatenate(rows, axis=0).astype(BF16)


def sum_kernel(experts, groups, *refs):
    add_blocks(experts, refs[: len(refs) - groups - 1], refs[len(refs) - groups :])


def combine_kernel(groups, pos_ref, *refs):
    backs, mixed_ref, router_ref = refs[:groups], refs[groups], refs[groups + 1]
    experts, width = router_ref.shape
    blocks = []
    router = jnp.zeros((2 * experts, width), F32)
    for ref in backs:
        block = ref[...].astype(F32)
        router = router + block[CAP : CAP + 2 * experts]
        blocks.append(block[:CAP])
        blocks.append(jnp.zeros((ROWS - CAP, width), F32))
    rows = jnp.concatenate(blocks, axis=0).astype(BF16)
    merged = chosen(pos_ref[...], experts)
    mixed_ref[...] = dot(merged, rows, ((0,), (0,))).astype(BF16)
    router_ref[...] = (router[:experts] + router[experts:]).astype(BF16)


def swap(block, axis, bits):
    size = lax.axis_size(axis)
    return lax.ppermute(block, axis, [(i, i ^ bits) for i in range(size)])


def shards(tokens, expert_ids, live_tokens, replicated, w_router, w_gate, w_up, w_down, cotangent):
    groups = lax.axis_size("expert")
    hops = lax.axis_size("z")
    experts = w_router.shape[1]
    count, width = tokens.shape
    _, model, units = w_gate.shape
    rows = groups * ROWS
    height = -(-(CAP + 2 * experts) // 16) * 16
    relative = width % LANES == 0 and hops == 4
    whole = pl.BlockSpec(memory_space=pltpu.VMEM)
    anywhere = pl.BlockSpec(memory_space=pl.ANY)
    fixed = pl.BlockSpec(memory_space=pltpu.HBM)
    shape = jax.ShapeDtypeStruct

    def call(kernel, args, outs, name, scratch=(), loose=(), cost=None, limit=4 * MIB):
        args = [pltpu.with_memory_space_constraint(a, pltpu.HBM) if i in loose else a for i, a in enumerate(args)]
        return pl.pallas_call(
            kernel,
            out_shape=tuple(outs),
            in_specs=[fixed if i in loose else whole for i in range(len(args))],
            out_specs=(whole,) * len(outs),
            scratch_shapes=list(scratch),
            compiler_params=pltpu.CompilerParams(vmem_limit_bytes=limit),
            cost_estimate=cost,
            name=name,
        )(*args)

    position, handed, *sends = call(
        functools.partial(pack_kernel, experts),
        (live_tokens, replicated, expert_ids.T, w_router.T, tokens, cotangent),
        [shape((1, 2 * count), jnp.int32), shape(cotangent.shape, BF16)] + [shape((ROWS, width), BF16)] * experts,
        "pack",
        scratch=[
            pltpu.SMEM(live_tokens.shape, jnp.int32),
            pltpu.SMEM(replicated.shape, jnp.int32),
            pltpu.VMEM((2, count), jnp.int32),
            pltpu.VMEM((experts, width), BF16),
            pltpu.VMEM((count, width), BF16),
            pltpu.SemaphoreType.DMA((6,)),
        ],
        loose=range(6),
    )
    def load(weight, name, start=0, size=None):
        height, length = size or weight.shape[1], weight.shape[2]
        return call(
            functools.partial(load_kernel, start),
            (weight,),
            [pltpu.VMEM((height, length), BF16), shape((8, LANES), F32)],
            name,
            scratch=[pltpu.SemaphoreType.DMA((PARTS,))],
            loose=(0,),
            cost=pl.CostEstimate(flops=0, bytes_accessed=4 * height * length, transcendentals=0),
            limit=8 * MIB,
        )

    half = model // 2
    gate_w, gate_mark = load(w_gate, "load_gate")
    up_a, up_mark = load(w_up, "load_up_a", 0, half)
    up_b, late_mark = load(w_up, "load_up_b", half, half)
    down_w, down_mark = load(w_down, "load_down")
    def gather(block, relayed=False):
        if relative and relayed:
            second = swap(block, "z", 2)
            return [block, swap(block, "z", 1), second, swap(second, "z", 1)]
        if relative:
            return [block] + [swap(block, "z", k) for k in range(1, hops)]
        return [lax.all_gather(block, "z", axis=0, tiled=False)]

    arrived = [sends[0]] + [swap(sends[q], "expert", q) for q in range(1, groups)]
    slices = gather(handed, True)
    picked = call(
        functools.partial(pick_kernel, relative, experts, hops),
        (position, *slices, late_mark, down_mark),
        [shape((hops, CAP, width), BF16)] * experts,
        "pick",
    )
    (stacked,) = call(
        functools.partial(stack_kernel, groups),
        (*arrived, gate_mark, up_mark, *slices[1:3]),
        [shape((groups, ROWS, width), BF16)],
        "stack",
    )
    blocks_x = gather(stacked)
    blocks_d = [picked[0]] + [swap(picked[q], "expert", q) for q in range(1, groups)]
    (own_x,) = call(
        join_kernel,
        (*blocks_x, picked[0]),
        [shape((hops, *stacked.shape), BF16)],
        "join",
    )
    far_x = swap(own_x, "core", 1)

    cost = 2 * rows * model * units
    rows_x, hidden, active, slope, gates, rival, others, keep, give = call(
        functools.partial(forward_kernel, relative, groups, hops),
        (own_x, far_x, gate_w, up_a, up_b, down_w, picked[0]),
        [
            shape((rows, model), BF16),
            shape((rows, units), BF16),
            shape((rows, units), F32),
            shape((rows, units), F32),
            shape((rows, 1), F32),
            shape((rows, 1), F32),
            shape((rows, 1), F32),
            shape((hops, groups, ROWS, width), F32),
            shape((hops, groups, ROWS, width), BF16),
        ],
        "forward",
        scratch=[pltpu.VMEM((rows, model), F32)],
        cost=pl.CostEstimate(flops=3 * cost, bytes_accessed=6 * model * units, transcendentals=rows * units),
        limit=16 * MIB,
    )
    got = swap(give, "core", 1)
    (own_d,) = call(
        functools.partial(stack_kernel, groups),
        (*blocks_d, gates),
        [shape((groups, hops, CAP, width), BF16)],
        "stack_d",
    )
    far_d = swap(own_d, "core", 1)
    rows_d, d_gate, d_up, router_keep, router_give = call(
        functools.partial(backward_kernel, relative, groups, hops),
        (own_d, far_d, rows_x, active, slope, hidden, gates, rival, others, down_w),
        [
            shape((rows, model), BF16),
            shape((rows, units), BF16),
            shape((rows, units), BF16),
            shape((hops, experts, width), F32),
            shape((hops, 2 * experts, width), BF16),
        ],
        "backward",
        scratch=[pltpu.VMEM((experts, model), F32)],
        cost=pl.CostEstimate(flops=cost, bytes_accessed=2 * model * units, transcendentals=0),
        limit=14 * MIB,
    )
    router_got = swap(router_give, "core", 1)
    merged = call(
        merge_kernel,
        (keep, got, router_keep, router_got),
        [shape((groups, height, width), BF16)] * hops,
        "merge",
    )
    if relative:
        outs = [merged[0]] + [swap(merged[k], "z", k) for k in range(hops - 1, 0, -1)]
    else:
        outs = lax.all_to_all(jnp.stack(merged), "z", split_axis=0, concat_axis=0, tiled=True)
        outs = [outs[k] for k in range(hops)]

    parts = 8
    once = lambda *shape: pl.BlockSpec(shape, lambda i: (0,) * len(shape))
    strip = max(units // parts, LANES)
    at = lambda i: i if units >= LANES * parts else 0
    grad_gate, grad_up, grad_down, mark = pl.pallas_call(
        grads_kernel,
        grid=(parts,),
        out_shape=(
            shape(w_gate.shape, BF16),
            shape(w_up.shape, BF16),
            shape(w_down.shape, BF16),
            shape((8, LANES), F32),
        ),
        in_specs=[
            pl.BlockSpec((rows, model // parts), lambda i: (0, i)),
            once(rows, model),
            once(rows, units),
            once(rows, units),
            pl.BlockSpec((rows, strip), lambda i: (0, at(i))),
            anywhere,
        ],
        out_specs=(
            pl.BlockSpec((1, model // parts, units), lambda i: (0, i, 0)),
            pl.BlockSpec((1, model // parts, units), lambda i: (0, i, 0)),
            pl.BlockSpec((1, strip, model), lambda i: (0, at(i), 0)),
            once(8, LANES),
        ),
        compiler_params=pltpu.CompilerParams(vmem_limit_bytes=24 * MIB),
        cost_estimate=pl.CostEstimate(flops=3 * cost, bytes_accessed=6 * model * units, transcendentals=0),
        name="grads",
    )(rows_x, rows_d, d_gate, d_up, hidden, merged[0])

    backs = call(
        functools.partial(sum_kernel, experts, groups),
        (*outs, mark),
        [shape((height, width), BF16)] * groups,
        "total",
    )
    backs = [backs[0]] + [swap(backs[q], "expert", q) for q in range(1, groups)]
    mixed, grad_router = call(
        functools.partial(combine_kernel, groups),
        (position, *backs),
        [shape((count, width), BF16), shape((experts, width), BF16)],
        "combine",
    )
    return (mixed, grad_gate, grad_up, grad_down, grad_router.T)


def solution(mesh):
    groups, etp = mesh.devices.shape
    inner = Mesh(mesh.devices.reshape(groups, etp // 2, 2), ("expert", "z", "core"))
    etp = ("z", "core")
    in_specs = (
        P("expert", etp),
        P("expert", None),
        P(),
        P(),
        P(etp, None),
        P("expert", None, etp),
        P("expert", None, etp),
        P("expert", etp, None),
        P("expert", etp),
    )
    out_specs = (
        P("expert", etp),
        P("expert", None, etp),
        P("expert", None, etp),
        P("expert", etp, None),
        P(etp, None),
    )
    return jax.shard_map(shards, mesh=inner, in_specs=in_specs, out_specs=out_specs, check_vma=False)
```

```python
import functools

import jax
import jax.numpy as jnp
from jax import lax
from jax.experimental import pallas as pl
from jax.experimental.pallas import tpu as pltpu
from jax.sharding import Mesh, PartitionSpec as P

CAPG = 32
RCAP = 8
CAP = CAPG + RCAP
META = 8
ROWS = CAP + META
MIB = 1024 * 1024
LANES = 128

F32 = jnp.float32
BF16 = jnp.bfloat16


def dot(a, b, dims):
    return lax.dot_general(a, b, (dims, ((), ())), preferred_element_type=F32)


def split3(value):
    hi = value.astype(BF16).astype(F32)
    rest = value - hi
    mid = rest.astype(BF16).astype(F32)
    return hi, mid, rest - mid


def chosen(position, experts):
    count = position.shape[1] // 2
    slots = lax.broadcasted_iota(jnp.int32, (experts * ROWS, 2 * count), 0)
    select = (slots == position).astype(F32)
    return (select[:, :count] + select[:, count:]).astype(BF16)


def pack_kernel(experts, *refs):
    sources, pos_ref, pass_ref, send_refs = refs[:6], refs[6], refs[7], refs[8 : 8 + experts]
    held, sems = [*refs[8 + experts : 13 + experts], pass_ref], refs[13 + experts]
    copies = [pltpu.make_async_copy(a, b, sems.at[i]) for i, (a, b) in enumerate(zip(sources, held))]
    for copy in copies:
        copy.start()
    for copy in copies:
        copy.wait()
    live_ref, flags_ref, ids_ref, router_ref, tok_ref, _ = held
    count, width = tok_ref.shape
    both = 2 * count
    lanes = max(experts, 8)
    group = lax.axis_index("expert")
    live = live_ref[group]
    ids = ids_ref[...]
    first, second = ids[0:1, :], ids[1:2, :]
    order = jnp.concatenate([first, second], axis=1)
    other = jnp.concatenate([second, first], axis=1)
    lane = lax.broadcasted_iota(jnp.int32, (1, both), 1)
    token = jnp.where(lane < count, lane, lane - count)
    alive = token < live
    expert_rows = lax.broadcasted_iota(jnp.int32, (lanes, both), 0)
    onehot = ((expert_rows == order) & alive).astype(F32)
    earlier = lax.broadcasted_iota(jnp.int32, (both, both), 0)
    later = lax.broadcasted_iota(jnp.int32, (both, both), 1)
    before = dot(onehot.astype(BF16), (earlier < later).astype(BF16), ((1,), (0,)))
    slot = jnp.sum(onehot * before, axis=0, keepdims=True).astype(jnp.int32)
    limit = jnp.full((1, both), CAPG, jnp.int32)
    for e in range(experts):
        limit = jnp.where(order == e, CAPG + RCAP * flags_ref[e], limit)
    kept = alive & (slot < limit)
    position = jnp.where(kept, (order ^ group) * ROWS + slot, -1)
    pos_ref[...] = position

    merged = chosen(position, experts)
    rows_x = dot(merged, tok_ref[...], ((1,), (0,)))

    logits = dot(router_ref[...], tok_ref[...], ((1,), (1,)))
    pick = lax.broadcasted_iota(jnp.int32, (experts, count), 0)
    gap = jnp.sum(
        jnp.where(pick == first, logits, 0.0) - jnp.where(pick == second, logits, 0.0),
        axis=0,
        keepdims=True,
    )
    hi, mid, low = split3(jnp.concatenate([gap, -gap], axis=1))
    meta_row = lax.broadcasted_iota(jnp.int32, (META, both), 0)
    meta = jnp.where(
        meta_row == 0,
        hi,
        jnp.where(
            meta_row == 1,
            mid,
            jnp.where(meta_row == 2, low, jnp.where(meta_row == 3, other.astype(F32), 0.0)),
        ),
    ).astype(BF16)
    span = min(width, LANES)
    near = lax.broadcasted_iota(jnp.int32, (span, both), 0)
    for e in range(experts):
        mine = ((near + e * ROWS == position) & (near < CAP)).astype(F32).astype(BF16)
        block = dot(meta, mine, ((1,), (1,)))
        if width > span:
            block = jnp.concatenate([block, jnp.zeros((META, width - span), F32)], axis=1)
        base = e * ROWS
        send_refs[e][...] = jnp.concatenate([rows_x[base : base + CAP], block], axis=0).astype(BF16)


def stack_kernel(count, *refs):
    for q in range(count):
        refs[-1][q] = refs[q][...]


def join_kernel(groups, _, __, *refs):
    blocks_d, blocks_x, own_x, own_d = refs[:groups], refs[groups:-2], refs[-2], refs[-1]
    for q in range(groups):
        own_d[q] = blocks_d[q][...]
    if len(blocks_x) == 1:
        own_x[...] = blocks_x[0][...]
    else:
        for k in range(len(blocks_x)):
            own_x[k] = blocks_x[k][...]


def pick_kernel(relative, experts, hops, pos_ref, *refs):
    sources, sends = refs[: len(refs) - experts - 1], refs[len(refs) - experts :]
    merged = chosen(pos_ref[...], experts)
    for k in range(hops):
        rows = dot(merged, sources[k][...] if relative else sources[0][k], ((1,), (0,)))
        for q in range(experts):
            sends[q][k] = rows[q * ROWS : q * ROWS + CAP].astype(BF16)


def column(row):
    size = row.shape[1]
    down = lax.broadcasted_iota(jnp.int32, (size, size), 0)
    across = lax.broadcasted_iota(jnp.int32, (size, size), 1)
    return jnp.sum(jnp.where(down == across, row, 0.0), axis=1, keepdims=True)


def visit(groups, hops, width, relative, body):
    core = lax.axis_index("core")
    z = lax.axis_index("z")
    if width % LANES == 0:
        for side in range(2):
            for k in range(hops):
                at = ((z ^ k if relative else k) * 2 + (core ^ side)) * width
                body(side, k, pl.ds(pl.multiple_of(at, LANES), width))
        return
    for here in range(2):

        @pl.when(core == here)
        def _():
            for side in range(2):
                for k in range(hops):
                    at = (k * 2 + (here ^ side)) * width
                    body(side, k, pl.ds(at, width))


def load_kernel(start, source, out, mark, sem):
    mark[...] = jnp.zeros(mark.shape, F32)
    copy = pltpu.make_async_copy(source.at[0, pl.ds(start, out.shape[0])], out, sem)
    copy.start()
    copy.wait()


def forward_kernel(relative, groups, hops, *refs):
    sides, (gate_ref, up_a_ref, up_b_ref, down_ref) = refs[:2], refs[2:6]
    x_ref, hid_ref, active_ref, slope_ref, gates_ref, rival_ref, other_ref, keep_ref, give_ref, total = refs[
        6:
    ]
    width = keep_ref.shape[-1]
    model = x_ref.shape[1]
    units = hid_ref.shape[1]
    tile = min(units, 256)

    def place(side, k, features):
        for q in range(groups):
            x_ref[q * ROWS : (q + 1) * ROWS, features] = sides[side][k, q]

    visit(groups, hops, width, relative, place)
    for q in range(groups):
        logit = jnp.zeros((META, ROWS), F32)
        for k in range(hops):
            for side in range(2):
                meta = sides[side][k, q].astype(F32)[CAP:, :ROWS]
                logit = logit + meta
        gap = column(logit[0:1] + logit[1:2] + logit[2:3])
        here = slice(q * ROWS, (q + 1) * ROWS)
        gates_ref[here, :] = jax.nn.sigmoid(gap)
        rival_ref[here, :] = jax.nn.sigmoid(-gap)
        other_ref[here, :] = column(meta[3:4])

    rows_x = x_ref[...]
    half = up_a_ref.shape[0]
    for f in range(0, units, tile):
        now = slice(f, f + tile)
        gate_pre = dot(rows_x, gate_ref[:, now], ((1,), (0,)))
        up_pre = dot(rows_x[:, :half], up_a_ref[:, now], ((1,), (0,)))
        up_pre = up_pre + dot(rows_x[:, half:], up_b_ref[:, now], ((1,), (0,)))
        sigma = jax.nn.sigmoid(gate_pre)
        active = gate_pre * sigma
        active_ref[:, now] = active
        slope_ref[:, now] = sigma * (1.0 + gate_pre * (1.0 - sigma)) * up_pre
        hid_ref[:, now] = (active * up_pre).astype(BF16)
    hidden = hid_ref[...]
    for f in range(0, model, 512):
        now = slice(f, f + 512)
        total[:, now] = gates_ref[...] * dot(hidden, down_ref[:, now], ((1,), (0,)))

    def emit(side, k, features):
        for q in range(groups):
            rows = total[q * ROWS : (q + 1) * ROWS, features]
            if side == 0:
                keep_ref[k, q] = rows
            else:
                give_ref[k, q] = rows.astype(BF16)

    visit(groups, hops, width, relative, emit)


def backward_kernel(relative, groups, hops, *refs):
    inputs = 2
    x_ref, active_ref, slope_ref, hid_ref, gates_ref, rival_ref, other_ref, down_ref = refs[inputs : inputs + 8]
    d_ref, dgate_ref, dup_ref, keep_ref, give_ref, scratch = refs[inputs + 8 :]
    experts, width = keep_ref.shape[1:]
    units = hid_ref.shape[1]
    tile = min(units, 256)

    def place(side, k, features):
        for q in range(groups):
            rows = gates_ref[q * ROWS : q * ROWS + CAP, :] * refs[side][q, k].astype(F32)
            rows = jnp.concatenate([rows, jnp.zeros((META, width), F32)], axis=0)
            d_ref[q * ROWS : (q + 1) * ROWS, features] = rows.astype(BF16)

    visit(groups, hops, width, relative, place)
    rows_d = d_ref[...]
    dots = jnp.zeros((rows_d.shape[0], 1), F32)
    for f in range(0, units, tile):
        now = slice(f, f + tile)
        d_hidden = dot(rows_d, down_ref[now, :], ((1,), (1,)))
        dgate_ref[:, now] = (d_hidden * slope_ref[:, now]).astype(BF16)
        dup_ref[:, now] = (d_hidden * active_ref[:, now]).astype(BF16)
        dots += jnp.sum(hid_ref[:, now].astype(F32) * d_hidden, axis=1, keepdims=True)
    weight = dots * rival_ref[...]
    lane = lax.broadcasted_iota(jnp.int32, (weight.shape[0], experts), 1)
    signed = jnp.where(lane == lax.axis_index("expert"), weight, 0.0) - jnp.where(
        lane == other_ref[...].astype(jnp.int32), weight, 0.0
    )
    router = jnp.zeros((experts, x_ref.shape[1]), F32)
    for piece in split3(signed):
        router = router + dot(piece.astype(BF16), x_ref[...], ((0,), (0,)))
    scratch[...] = router

    def emit(side, k, features):
        rows = scratch[:, features]
        if side == 0:
            keep_ref[k] = rows
        else:
            give_ref[k] = halves(rows).astype(BF16)

    visit(groups, hops, width, relative, emit)


def halves(rows):
    top = rows.astype(BF16).astype(F32)
    return jnp.concatenate([top, rows - top], axis=0)


def merge_kernel(keep_ref, got_ref, rkeep_ref, rgot_ref, *out_refs):
    experts = rkeep_ref.shape[1]
    hops = keep_ref.shape[0]
    for k in range(hops):
        got = rgot_ref[k].astype(F32)
        router = halves(rkeep_ref[k] + got[:experts] + got[experts:])
        put(out_refs[k], keep_ref[k] + got_ref[k].astype(F32), router)


def pass_kernel(block_ref, _, out_ref):
    out_ref[...] = block_ref[...]


def put(out_ref, blocks, router):
    groups, height, width = out_ref.shape
    spare = height - CAP - router.shape[0]
    for q in range(groups):
        rows = [blocks[q][:CAP], router]
        if spare:
            rows.append(jnp.zeros((spare, width), F32))
        out_ref[q] = jnp.concatenate(rows, axis=0).astype(BF16)


def grads_kernel(x_ref, d_ref, dgate_ref, dup_ref, hid_ref, _, gate_ref, up_ref, down_ref, mark_ref):
    rows_x = x_ref[...]
    first = ((0,), (0,))
    gate_ref[0] = dot(rows_x, dgate_ref[...], first).astype(BF16)
    up_ref[0] = dot(rows_x, dup_ref[...], first).astype(BF16)
    down_ref[0] = dot(hid_ref[...], d_ref[...], first).astype(BF16)
    mark_ref[...] = jnp.zeros(mark_ref.shape, F32)


def add_blocks(experts, parts, sends):
    router = None
    for q, send in enumerate(sends):
        block = parts[0][q].astype(F32)
        for ref in parts[1:]:
            block = block + ref[q].astype(F32)
        if router is None:
            router = halves(block[CAP : CAP + experts] + block[CAP + experts : CAP + 2 * experts])
        height, width = send.shape
        rows = [block[:CAP], router]
        if height > CAP + 2 * experts:
            rows.append(jnp.zeros((height - CAP - 2 * experts, width), F32))
        send[...] = jnp.concatenate(rows, axis=0).astype(BF16)


def sum_kernel(experts, groups, *refs):
    add_blocks(experts, refs[: len(refs) - groups - 1], refs[len(refs) - groups :])


def combine_kernel(groups, pos_ref, *refs):
    backs, mixed_ref, router_ref = refs[:groups], refs[groups], refs[groups + 1]
    experts, width = router_ref.shape
    blocks = []
    router = jnp.zeros((2 * experts, width), F32)
    for ref in backs:
        block = ref[...].astype(F32)
        router = router + block[CAP : CAP + 2 * experts]
        blocks.append(block[:CAP])
        blocks.append(jnp.zeros((ROWS - CAP, width), F32))
    rows = jnp.concatenate(blocks, axis=0).astype(BF16)
    merged = chosen(pos_ref[...], experts)
    mixed_ref[...] = dot(merged, rows, ((0,), (0,))).astype(BF16)
    router_ref[...] = (router[:experts] + router[experts:]).astype(BF16)


def swap(block, axis, bits):
    size = lax.axis_size(axis)
    return lax.ppermute(block, axis, [(i, i ^ bits) for i in range(size)])


def shards(tokens, expert_ids, live_tokens, replicated, w_router, w_gate, w_up, w_down, cotangent):
    groups = lax.axis_size("expert")
    hops = lax.axis_size("z")
    experts = w_router.shape[1]
    count, width = tokens.shape
    _, model, units = w_gate.shape
    rows = groups * ROWS
    height = -(-(CAP + 2 * experts) // 16) * 16
    relative = width % LANES == 0 and hops == 4
    whole = pl.BlockSpec(memory_space=pltpu.VMEM)
    anywhere = pl.BlockSpec(memory_space=pl.ANY)
    fixed = pl.BlockSpec(memory_space=pltpu.HBM)
    shape = jax.ShapeDtypeStruct

    def call(kernel, args, outs, name, scratch=(), loose=(), cost=None, limit=4 * MIB):
        args = [pltpu.with_memory_space_constraint(a, pltpu.HBM) if i in loose else a for i, a in enumerate(args)]
        return pl.pallas_call(
            kernel,
            out_shape=tuple(outs),
            in_specs=[fixed if i in loose else whole for i in range(len(args))],
            out_specs=(whole,) * len(outs),
            scratch_shapes=list(scratch),
            compiler_params=pltpu.CompilerParams(vmem_limit_bytes=limit),
            cost_estimate=cost,
            name=name,
        )(*args)

    position, handed, *sends = call(
        functools.partial(pack_kernel, experts),
        (live_tokens, replicated, expert_ids.T, w_router.T, tokens, cotangent),
        [shape((1, 2 * count), jnp.int32), shape(cotangent.shape, BF16)] + [shape((ROWS, width), BF16)] * experts,
        "pack",
        scratch=[
            pltpu.SMEM(live_tokens.shape, jnp.int32),
            pltpu.SMEM(replicated.shape, jnp.int32),
            pltpu.VMEM((2, count), jnp.int32),
            pltpu.VMEM((experts, width), BF16),
            pltpu.VMEM((count, width), BF16),
            pltpu.SemaphoreType.DMA((6,)),
        ],
        loose=range(6),
    )
    def load(weight, name, start=0, size=None):
        height, length = size or weight.shape[1], weight.shape[2]
        return call(
            functools.partial(load_kernel, start),
            (weight,),
            [pltpu.VMEM((height, length), BF16), shape((8, LANES), F32)],
            name,
            scratch=[pltpu.SemaphoreType.DMA],
            loose=(0,),
            cost=pl.CostEstimate(flops=0, bytes_accessed=4 * height * length, transcendentals=0),
            limit=8 * MIB,
        )

    half = model // 2
    gate_w, gate_mark = load(w_gate, "load_gate")
    up_a, up_mark = load(w_up, "load_up_a", 0, half)
    up_b, late_mark = load(w_up, "load_up_b", half, half)
    down_w, down_mark = load(w_down, "load_down")
    def gather(block):
        if relative:
            second = swap(block, "z", 2)
            (held,) = call(pass_kernel, (second, gate_mark), [shape(block.shape, BF16)], "relay")
            return [block, swap(block, "z", 1), second, swap(held, "z", 1)]
        return [lax.all_gather(block, "z", axis=0, tiled=False)]

    arrived = [sends[0]] + [swap(sends[q], "expert", q) for q in range(1, groups)]
    slices = gather(handed)
    (stacked,) = call(
        functools.partial(stack_kernel, groups),
        (*arrived, gate_mark, up_mark, *slices[1:]),
        [shape((groups, ROWS, width), BF16)],
        "stack",
    )
    picked = call(
        functools.partial(pick_kernel, relative, experts, hops),
        (position, *slices, stacked),
        [shape((hops, CAP, width), BF16)] * experts,
        "pick",
    )
    blocks_x = [stacked] + [swap(stacked, "z", k) for k in range(1, hops)] if relative else gather(stacked)
    blocks_d = [picked[0]] + [swap(picked[q], "expert", q) for q in range(1, groups)]
    own_x, own_d = call(
        functools.partial(join_kernel, groups),
        (late_mark, down_mark, *blocks_d, *blocks_x),
        [shape((hops, *stacked.shape), BF16), shape((groups, *picked[0].shape), BF16)],
        "join",
    )
    far_x = swap(own_x, "core", 1)
    far_d = swap(own_d, "core", 1)

    cost = 2 * rows * model * units
    rows_x, hidden, active, slope, gates, rival, others, keep, give = call(
        functools.partial(forward_kernel, relative, groups, hops),
        (own_x, far_x, gate_w, up_a, up_b, down_w),
        [
            shape((rows, model), BF16),
            shape((rows, units), BF16),
            shape((rows, units), F32),
            shape((rows, units), F32),
            shape((rows, 1), F32),
            shape((rows, 1), F32),
            shape((rows, 1), F32),
            shape((hops, groups, ROWS, width), F32),
            shape((hops, groups, ROWS, width), BF16),
        ],
        "forward",
        scratch=[pltpu.VMEM((rows, model), F32)],
        cost=pl.CostEstimate(flops=3 * cost, bytes_accessed=6 * model * units, transcendentals=rows * units),
        limit=16 * MIB,
    )
    got = swap(give, "core", 1)
    rows_d, d_gate, d_up, router_keep, router_give = call(
        functools.partial(backward_kernel, relative, groups, hops),
        (own_d, far_d, rows_x, active, slope, hidden, gates, rival, others, down_w),
        [
            shape((rows, model), BF16),
            shape((rows, units), BF16),
            shape((rows, units), BF16),
            shape((hops, experts, width), F32),
            shape((hops, 2 * experts, width), BF16),
        ],
        "backward",
        scratch=[pltpu.VMEM((experts, model), F32)],
        cost=pl.CostEstimate(flops=cost, bytes_accessed=2 * model * units, transcendentals=0),
        limit=14 * MIB,
    )
    router_got = swap(router_give, "core", 1)
    merged = call(
        merge_kernel,
        (keep, got, router_keep, router_got),
        [shape((groups, height, width), BF16)] * hops,
        "merge",
    )
    if relative:
        outs = [merged[0]] + [swap(merged[k], "z", k) for k in range(hops - 1, 0, -1)]
    else:
        outs = lax.all_to_all(jnp.stack(merged), "z", split_axis=0, concat_axis=0, tiled=True)
        outs = [outs[k] for k in range(hops)]

    parts = 8
    once = lambda *shape: pl.BlockSpec(shape, lambda i: (0,) * len(shape))
    strip = max(units // parts, LANES)
    at = lambda i: i if units >= LANES * parts else 0
    grad_gate, grad_up, grad_down, mark = pl.pallas_call(
        grads_kernel,
        grid=(parts,),
        out_shape=(
            shape(w_gate.shape, BF16),
            shape(w_up.shape, BF16),
            shape(w_down.shape, BF16),
            shape((8, LANES), F32),
        ),
        in_specs=[
            pl.BlockSpec((rows, model // parts), lambda i: (0, i)),
            once(rows, model),
            once(rows, units),
            once(rows, units),
            pl.BlockSpec((rows, strip), lambda i: (0, at(i))),
            anywhere,
        ],
        out_specs=(
            pl.BlockSpec((1, model // parts, units), lambda i: (0, i, 0)),
            pl.BlockSpec((1, model // parts, units), lambda i: (0, i, 0)),
            pl.BlockSpec((1, strip, model), lambda i: (0, at(i), 0)),
            once(8, LANES),
        ),
        compiler_params=pltpu.CompilerParams(vmem_limit_bytes=24 * MIB),
        cost_estimate=pl.CostEstimate(flops=3 * cost, bytes_accessed=6 * model * units, transcendentals=0),
        name="grads",
    )(rows_x, rows_d, d_gate, d_up, hidden, merged[0])

    backs = call(
        functools.partial(sum_kernel, experts, groups),
        (*outs, mark),
        [shape((height, width), BF16)] * groups,
        "total",
    )
    backs = [backs[0]] + [swap(backs[q], "expert", q) for q in range(1, groups)]
    mixed, grad_router = call(
        functools.partial(combine_kernel, groups),
        (position, *backs),
        [shape((count, width), BF16), shape((experts, width), BF16)],
        "combine",
    )
    return (mixed, grad_gate, grad_up, grad_down, grad_router.T)


def solution(mesh):
    groups, etp = mesh.devices.shape
    inner = Mesh(mesh.devices.reshape(groups, etp // 2, 2), ("expert", "z", "core"))
    etp = ("z", "core")
    in_specs = (
        P("expert", etp),
        P("expert", None),
        P(),
        P(),
        P(etp, None),
        P("expert", None, etp),
        P("expert", None, etp),
        P("expert", etp, None),
        P("expert", etp),
    )
    out_specs = (
        P("expert", etp),
        P("expert", None, etp),
        P("expert", None, etp),
        P("expert", etp, None),
        P(etp, None),
    )
    return jax.shard_map(shards, mesh=inner, in_specs=in_specs, out_specs=out_specs, check_vma=False)
```

```python
import functools

import jax
import jax.numpy as jnp
from jax import lax
from jax.experimental import pallas as pl
from jax.experimental.pallas import tpu as pltpu
from jax.sharding import Mesh, PartitionSpec as P

CAPG = 32
RCAP = 8
CAP = CAPG + RCAP
META = 8
ROWS = CAP + META
MIB = 1024 * 1024
LANES = 128

F32 = jnp.float32
BF16 = jnp.bfloat16


def dot(a, b, dims):
    return lax.dot_general(a, b, (dims, ((), ())), preferred_element_type=F32)


def split3(value):
    hi = value.astype(BF16).astype(F32)
    rest = value - hi
    mid = rest.astype(BF16).astype(F32)
    return hi, mid, rest - mid


def pack_kernel(experts, *refs):
    sources, pos_ref, send_refs = refs[:6], refs[6], refs[7 : 7 + experts]
    held, sems = refs[7 + experts : 13 + experts], refs[13 + experts]
    copies = [pltpu.make_async_copy(a, b, sems.at[i]) for i, (a, b) in enumerate(zip(sources, held))]
    for copy in copies:
        copy.start()
    for copy in copies:
        copy.wait()
    live_ref, flags_ref, ids_ref, router_ref, tok_ref, cot_ref = held
    count, width = tok_ref.shape
    both = 2 * count
    lanes = max(experts, 8)
    group = lax.axis_index("expert")
    live = live_ref[group]
    ids = ids_ref[...]
    first, second = ids[0:1, :], ids[1:2, :]
    order = jnp.concatenate([first, second], axis=1)
    other = jnp.concatenate([second, first], axis=1)
    lane = lax.broadcasted_iota(jnp.int32, (1, both), 1)
    token = jnp.where(lane < count, lane, lane - count)
    alive = token < live
    expert_rows = lax.broadcasted_iota(jnp.int32, (lanes, both), 0)
    onehot = ((expert_rows == order) & alive).astype(F32)
    earlier = lax.broadcasted_iota(jnp.int32, (both, both), 0)
    later = lax.broadcasted_iota(jnp.int32, (both, both), 1)
    before = dot(onehot.astype(BF16), (earlier < later).astype(BF16), ((1,), (0,)))
    slot = jnp.sum(onehot * before, axis=0, keepdims=True).astype(jnp.int32)
    limit = jnp.full((1, both), CAPG, jnp.int32)
    for e in range(experts):
        limit = jnp.where(order == e, CAPG + RCAP * flags_ref[e], limit)
    kept = alive & (slot < limit)
    position = jnp.where(kept, (order ^ group) * ROWS + slot, -1)
    pos_ref[...] = position

    slots = lax.broadcasted_iota(jnp.int32, (experts * ROWS, both), 0)
    select = (slots == position).astype(F32)
    merged = (select[:, :count] + select[:, count:]).astype(BF16)
    rows_x = dot(merged, tok_ref[...], ((1,), (0,)))
    rows_d = dot(merged, cot_ref[...], ((1,), (0,)))

    logits = dot(router_ref[...], tok_ref[...], ((1,), (1,)))
    pick = lax.broadcasted_iota(jnp.int32, (experts, count), 0)
    gap = jnp.sum(
        jnp.where(pick == first, logits, 0.0) - jnp.where(pick == second, logits, 0.0),
        axis=0,
        keepdims=True,
    )
    hi, mid, low = split3(jnp.concatenate([gap, -gap], axis=1))
    meta_row = lax.broadcasted_iota(jnp.int32, (META, both), 0)
    meta = jnp.where(
        meta_row == 0,
        hi,
        jnp.where(
            meta_row == 1,
            mid,
            jnp.where(meta_row == 2, low, jnp.where(meta_row == 3, other.astype(F32), 0.0)),
        ),
    ).astype(BF16)
    span = min(width, LANES)
    near = lax.broadcasted_iota(jnp.int32, (span, both), 0)
    for e in range(experts):
        mine = ((near + e * ROWS == position) & (near < CAP)).astype(F32).astype(BF16)
        block = dot(meta, mine, ((1,), (1,)))
        if width > span:
            block = jnp.concatenate([block, jnp.zeros((META, width - span), F32)], axis=1)
        base = e * ROWS
        send_refs[e][:ROWS] = jnp.concatenate([rows_x[base : base + CAP], block], axis=0).astype(BF16)
        send_refs[e][ROWS:] = rows_d[base : base + CAP].astype(BF16)


def stack_kernel(count, lo, hi, *refs):
    for q in range(count):
        refs[-1][q] = refs[q][lo:hi]


def column(row):
    size = row.shape[1]
    down = lax.broadcasted_iota(jnp.int32, (size, size), 0)
    across = lax.broadcasted_iota(jnp.int32, (size, size), 1)
    return jnp.sum(jnp.where(down == across, row, 0.0), axis=1, keepdims=True)


def visit(groups, hops, width, relative, body):
    core = lax.axis_index("core")
    z = lax.axis_index("z")
    if width % LANES == 0:
        for side in range(2):
            for k in range(hops):
                at = ((z ^ k if relative else k) * 2 + (core ^ side)) * width
                body(side, k, pl.ds(pl.multiple_of(at, LANES), width))
        return
    for here in range(2):

        @pl.when(core == here)
        def _():
            for side in range(2):
                for k in range(hops):
                    at = (k * 2 + (here ^ side)) * width
                    body(side, k, pl.ds(at, width))


def load_kernel(source, out, mark, sem):
    mark[...] = jnp.zeros(mark.shape, F32)
    copy = pltpu.make_async_copy(source, out, sem)
    copy.start()
    copy.wait()


def reader(relative, hops, refs):
    if relative:
        return lambda side, q, k: refs[side * hops + k][q]
    return lambda side, q, k: refs[side][k, q]


def forward_kernel(relative, groups, hops, *refs):
    inputs = 2 * hops if relative else 2
    take = reader(relative, hops, refs[:inputs])
    gate_ref, up_ref, down_ref = refs[inputs : inputs + 3]
    x_ref, hid_ref, active_ref, slope_ref, gates_ref, rival_ref, other_ref, keep_ref, give_ref, total = refs[
        inputs + 3 :
    ]
    width = keep_ref.shape[-1]
    model = x_ref.shape[1]
    units = hid_ref.shape[1]
    tile = min(units, 256)

    def place(side, k, features):
        for q in range(groups):
            x_ref[q * ROWS : (q + 1) * ROWS, features] = take(side, q, k)[:ROWS]

    visit(groups, hops, width, relative, place)
    for q in range(groups):
        logit = jnp.zeros((META, ROWS), F32)
        for k in range(hops):
            for side in range(2):
                meta = take(side, q, k)[:ROWS].astype(F32)[CAP:, :ROWS]
                logit = logit + meta
        gap = column(logit[0:1] + logit[1:2] + logit[2:3])
        here = slice(q * ROWS, (q + 1) * ROWS)
        gates_ref[here, :] = jax.nn.sigmoid(gap)
        rival_ref[here, :] = jax.nn.sigmoid(-gap)
        other_ref[here, :] = column(meta[3:4])

    rows_x = x_ref[...]
    for f in range(0, units, tile):
        now = slice(f, f + tile)
        gate_pre = dot(rows_x, gate_ref[0, :, now], ((1,), (0,)))
        up_pre = dot(rows_x, up_ref[0, :, now], ((1,), (0,)))
        sigma = jax.nn.sigmoid(gate_pre)
        active = gate_pre * sigma
        active_ref[:, now] = active
        slope_ref[:, now] = sigma * (1.0 + gate_pre * (1.0 - sigma)) * up_pre
        hid_ref[:, now] = (active * up_pre).astype(BF16)
    hidden = hid_ref[...]
    for f in range(0, model, 512):
        now = slice(f, f + 512)
        total[:, now] = gates_ref[...] * dot(hidden, down_ref[0, :, now], ((1,), (0,)))

    def emit(side, k, features):
        for q in range(groups):
            rows = total[q * ROWS : (q + 1) * ROWS, features]
            if side == 0:
                keep_ref[k, q] = rows
            else:
                give_ref[k, q] = rows.astype(BF16)

    visit(groups, hops, width, relative, emit)


def backward_kernel(relative, groups, hops, *refs):
    inputs = 2 * hops if relative else 2
    take = reader(relative, hops, refs[:inputs])
    x_ref, active_ref, slope_ref, hid_ref, gates_ref, rival_ref, other_ref, down_ref = refs[inputs : inputs + 8]
    d_ref, dgate_ref, dup_ref, keep_ref, give_ref, scratch = refs[inputs + 8 :]
    experts, width = keep_ref.shape[1:]
    units = hid_ref.shape[1]
    tile = min(units, 256)

    def place(side, k, features):
        for q in range(groups):
            rows = gates_ref[q * ROWS : q * ROWS + CAP, :] * take(side, q, k)[ROWS:].astype(F32)
            rows = jnp.concatenate([rows, jnp.zeros((META, width), F32)], axis=0)
            d_ref[q * ROWS : (q + 1) * ROWS, features] = rows.astype(BF16)

    visit(groups, hops, width, relative, place)
    rows_d = d_ref[...]
    dots = jnp.zeros((rows_d.shape[0], 1), F32)
    for f in range(0, units, tile):
        now = slice(f, f + tile)
        d_hidden = dot(rows_d, down_ref[0, now, :], ((1,), (1,)))
        dgate_ref[:, now] = (d_hidden * slope_ref[:, now]).astype(BF16)
        dup_ref[:, now] = (d_hidden * active_ref[:, now]).astype(BF16)
        dots += jnp.sum(hid_ref[:, now].astype(F32) * d_hidden, axis=1, keepdims=True)
    weight = dots * rival_ref[...]
    lane = lax.broadcasted_iota(jnp.int32, (weight.shape[0], experts), 1)
    signed = jnp.where(lane == lax.axis_index("expert"), weight, 0.0) - jnp.where(
        lane == other_ref[...].astype(jnp.int32), weight, 0.0
    )
    router = jnp.zeros((experts, x_ref.shape[1]), F32)
    for piece in split3(signed):
        router = router + dot(piece.astype(BF16), x_ref[...], ((0,), (0,)))
    scratch[...] = router

    def emit(side, k, features):
        rows = scratch[:, features]
        if side == 0:
            keep_ref[k] = rows
        else:
            give_ref[k] = halves(rows).astype(BF16)

    visit(groups, hops, width, relative, emit)


def halves(rows):
    top = rows.astype(BF16).astype(F32)
    return jnp.concatenate([top, rows - top], axis=0)


def merge_kernel(keep_ref, got_ref, rkeep_ref, rgot_ref, *out_refs):
    experts = rkeep_ref.shape[1]
    hops = keep_ref.shape[0]
    for k in range(hops):
        got = rgot_ref[k].astype(F32)
        router = halves(rkeep_ref[k] + got[:experts] + got[experts:])
        put(out_refs[k], keep_ref[k] + got_ref[k].astype(F32), router)


def pass_kernel(block_ref, _, __, out_ref):
    out_ref[...] = block_ref[...]


def put(out_ref, blocks, router):
    rows = [blocks[q, :CAP] for q in range(blocks.shape[0])]
    out_ref[...] = jnp.concatenate([*rows, router], axis=0).astype(BF16)


def grads_kernel(x_ref, d_ref, dgate_ref, dup_ref, hid_ref, _, gate_ref, up_ref, down_ref, mark_ref):
    rows_x = x_ref[...]
    first = ((0,), (0,))
    gate_ref[0] = dot(rows_x, dgate_ref[...], first).astype(BF16)
    up_ref[0] = dot(rows_x, dup_ref[...], first).astype(BF16)
    down_ref[0] = dot(hid_ref[...], d_ref[...], first).astype(BF16)
    mark_ref[...] = jnp.zeros(mark_ref.shape, F32)


def sum_kernel(experts, groups, *refs):
    parts, sends = refs[: len(refs) - groups - 1], refs[len(refs) - groups :]
    total = parts[0][...].astype(F32)
    for ref in parts[1:]:
        total = total + ref[...].astype(F32)
    router = total[groups * CAP :]
    router = halves(router[:experts] + router[experts:])
    height, width = sends[0].shape
    for q, send in enumerate(sends):
        rows = [total[q * CAP : (q + 1) * CAP], router]
        if height > CAP + 2 * experts:
            rows.append(jnp.zeros((height - CAP - 2 * experts, width), F32))
        send[...] = jnp.concatenate(rows, axis=0).astype(BF16)


def combine_kernel(groups, pos_ref, *refs):
    backs, mixed_ref, router_ref = refs[:groups], refs[groups], refs[groups + 1]
    experts, width = router_ref.shape
    count = mixed_ref.shape[0]
    blocks = []
    router = jnp.zeros((2 * experts, width), F32)
    for ref in backs:
        block = ref[...].astype(F32)
        router = router + block[CAP : CAP + 2 * experts]
        blocks.append(block[:CAP])
        blocks.append(jnp.zeros((ROWS - CAP, width), F32))
    rows = jnp.concatenate(blocks, axis=0).astype(BF16)
    slots = lax.broadcasted_iota(jnp.int32, (experts * ROWS, 2 * count), 0)
    select = (slots == pos_ref[...]).astype(F32)
    merged = (select[:, :count] + select[:, count:]).astype(BF16)
    mixed_ref[...] = dot(merged, rows, ((0,), (0,))).astype(BF16)
    router_ref[...] = (router[:experts] + router[experts:]).astype(BF16)


def swap(block, axis, bits):
    size = lax.axis_size(axis)
    return lax.ppermute(block, axis, [(i, i ^ bits) for i in range(size)])


def shards(tokens, expert_ids, live_tokens, replicated, w_router, w_gate, w_up, w_down, cotangent):
    groups = lax.axis_size("expert")
    hops = lax.axis_size("z")
    experts = w_router.shape[1]
    count, width = tokens.shape
    _, model, units = w_gate.shape
    rows = groups * ROWS
    height = -(-(CAP + 2 * experts) // 16) * 16
    relative = width % LANES == 0 and hops <= 4
    whole = pl.BlockSpec(memory_space=pltpu.VMEM)
    anywhere = pl.BlockSpec(memory_space=pl.ANY)
    fixed = pl.BlockSpec(memory_space=pltpu.HBM)
    shape = jax.ShapeDtypeStruct

    def call(kernel, args, outs, name, scratch=(), loose=(), cost=None, limit=4 * MIB):
        args = [pltpu.with_memory_space_constraint(a, pltpu.HBM) if i in loose else a for i, a in enumerate(args)]
        return pl.pallas_call(
            kernel,
            out_shape=tuple(outs),
            in_specs=[fixed if i in loose else whole for i in range(len(args))],
            out_specs=(whole,) * len(outs),
            scratch_shapes=list(scratch),
            compiler_params=pltpu.CompilerParams(vmem_limit_bytes=limit),
            cost_estimate=cost,
            name=name,
        )(*args)

    position, *sends = call(
        functools.partial(pack_kernel, experts),
        (live_tokens, replicated, expert_ids.T, w_router.T, tokens, cotangent),
        [shape((1, 2 * count), jnp.int32)] + [shape((ROWS + CAP, width), BF16)] * experts,
        "pack",
        scratch=[
            pltpu.SMEM(live_tokens.shape, jnp.int32),
            pltpu.SMEM(replicated.shape, jnp.int32),
            pltpu.VMEM((2, count), jnp.int32),
            pltpu.VMEM((experts, width), BF16),
            pltpu.VMEM((count, width), BF16),
            pltpu.VMEM((count, width), BF16),
            pltpu.SemaphoreType.DMA((6,)),
        ],
        loose=range(6),
    )
    arrived = [sends[0]] + [swap(sends[q], "expert", q) for q in range(1, groups)]
    def load(weight, name):
        return call(
            load_kernel,
            (weight,),
            [pltpu.VMEM(weight.shape, BF16), shape((8, LANES), F32)],
            name,
            scratch=[pltpu.SemaphoreType.DMA],
            loose=(0,),
            cost=pl.CostEstimate(flops=0, bytes_accessed=2 * 2 * model * units, transcendentals=0),
            limit=8 * MIB,
        )

    gate_w, gate_mark = load(w_gate, "load_gate")
    up_w, up_mark = load(w_up, "load_up")
    down_w, down_mark = load(w_down, "load_down")
    (stacked,) = call(
        functools.partial(stack_kernel, groups, 0, ROWS + CAP),
        (*arrived, gate_mark, up_mark),
        [shape((groups, ROWS + CAP, width), BF16)],
        "stack",
    )
    if relative:
        blocks = [stacked]
        if hops > 2:
            second = swap(stacked, "z", 2)
        if hops > 1:
            blocks.append(swap(stacked, "z", 1))
        if hops > 2:
            (relay,) = call(pass_kernel, (second, blocks[1], down_mark), [shape(second.shape, BF16)], "relay")
            blocks += [second, swap(relay, "z", 1)]
    else:
        blocks = [lax.all_gather(stacked, "z", axis=0, tiled=False)]
    blocks = blocks + [swap(block, "core", 1) for block in blocks]

    cost = 2 * rows * model * units
    rows_x, hidden, active, slope, gates, rival, others, keep, give = call(
        functools.partial(forward_kernel, relative, groups, hops),
        (*blocks, gate_w, up_w, down_w),
        [
            shape((rows, model), BF16),
            shape((rows, units), BF16),
            shape((rows, units), F32),
            shape((rows, units), F32),
            shape((rows, 1), F32),
            shape((rows, 1), F32),
            shape((rows, 1), F32),
            shape((hops, groups, ROWS, width), F32),
            shape((hops, groups, ROWS, width), BF16),
        ],
        "forward",
        scratch=[pltpu.VMEM((rows, model), F32)],
        cost=pl.CostEstimate(flops=3 * cost, bytes_accessed=6 * model * units, transcendentals=rows * units),
        limit=16 * MIB,
    )
    got = swap(give, "core", 1)
    rows_d, d_gate, d_up, router_keep, router_give = call(
        functools.partial(backward_kernel, relative, groups, hops),
        (*blocks, rows_x, active, slope, hidden, gates, rival, others, down_w),
        [
            shape((rows, model), BF16),
            shape((rows, units), BF16),
            shape((rows, units), BF16),
            shape((hops, experts, width), F32),
            shape((hops, 2 * experts, width), BF16),
        ],
        "backward",
        scratch=[pltpu.VMEM((experts, model), F32)],
        cost=pl.CostEstimate(flops=cost, bytes_accessed=2 * model * units, transcendentals=0),
        limit=14 * MIB,
    )
    router_got = swap(router_give, "core", 1)
    merged = call(
        merge_kernel,
        (keep, got, router_keep, router_got),
        [shape((groups * CAP + 2 * experts, width), BF16)] * hops,
        "merge",
    )
    if relative:
        outs = [merged[0]] + [swap(merged[k], "z", k) for k in range(hops - 1, 0, -1)]
    else:
        outs = lax.all_to_all(jnp.stack(merged), "z", split_axis=0, concat_axis=0, tiled=True)
        outs = [outs[k] for k in range(hops)]

    parts = 8
    once = lambda *shape: pl.BlockSpec(shape, lambda i: (0,) * len(shape))
    strip = max(units // parts, LANES)
    at = lambda i: i if units >= LANES * parts else 0
    grad_gate, grad_up, grad_down, mark = pl.pallas_call(
        grads_kernel,
        grid=(parts,),
        out_shape=(
            shape(w_gate.shape, BF16),
            shape(w_up.shape, BF16),
            shape(w_down.shape, BF16),
            shape((8, LANES), F32),
        ),
        in_specs=[
            pl.BlockSpec((rows, model // parts), lambda i: (0, i)),
            once(rows, model),
            once(rows, units),
            once(rows, units),
            pl.BlockSpec((rows, strip), lambda i: (0, at(i))),
            anywhere,
        ],
        out_specs=(
            pl.BlockSpec((1, model // parts, units), lambda i: (0, i, 0)),
            pl.BlockSpec((1, model // parts, units), lambda i: (0, i, 0)),
            pl.BlockSpec((1, strip, model), lambda i: (0, at(i), 0)),
            once(8, LANES),
        ),
        compiler_params=pltpu.CompilerParams(vmem_limit_bytes=24 * MIB),
        cost_estimate=pl.CostEstimate(flops=3 * cost, bytes_accessed=6 * model * units, transcendentals=0),
        name="grads",
    )(rows_x, rows_d, d_gate, d_up, hidden, merged[0])

    backs = call(
        functools.partial(sum_kernel, experts, groups),
        (*outs, mark),
        [shape((height, width), BF16)] * groups,
        "total",
    )
    backs = [backs[0]] + [swap(backs[q], "expert", q) for q in range(1, groups)]
    mixed, grad_router = call(
        functools.partial(combine_kernel, groups),
        (position, *backs),
        [shape((count, width), BF16), shape((experts, width), BF16)],
        "combine",
    )
    return (mixed, grad_gate, grad_up, grad_down, grad_router.T)


def solution(mesh):
    groups, etp = mesh.devices.shape
    inner = Mesh(mesh.devices.reshape(groups, etp // 2, 2), ("expert", "z", "core"))
    etp = ("z", "core")
    in_specs = (
        P("expert", etp),
        P("expert", None),
        P(),
        P(),
        P(etp, None),
        P("expert", None, etp),
        P("expert", None, etp),
        P("expert", etp, None),
        P("expert", etp),
    )
    out_specs = (
        P("expert", etp),
        P("expert", None, etp),
        P("expert", None, etp),
        P("expert", etp, None),
        P(etp, None),
    )
    return jax.shard_map(shards, mesh=inner, in_specs=in_specs, out_specs=out_specs, check_vma=False)
```

```python
import functools

import jax
import jax.numpy as jnp
from jax import lax
from jax.experimental import pallas as pl
from jax.experimental.pallas import tpu as pltpu
from jax.sharding import Mesh, PartitionSpec as P

CAPG = 32
RCAP = 8
CAP = CAPG + RCAP
META = 8
ROWS = CAP + META
MIB = 1024 * 1024
LANES = 128

F32 = jnp.float32
BF16 = jnp.bfloat16


def dot(a, b, dims):
    return lax.dot_general(a, b, (dims, ((), ())), preferred_element_type=F32)


def split3(value):
    hi = value.astype(BF16).astype(F32)
    rest = value - hi
    mid = rest.astype(BF16).astype(F32)
    return hi, mid, rest - mid


def chosen(position, experts):
    count = position.shape[1] // 2
    slots = lax.broadcasted_iota(jnp.int32, (experts * ROWS, 2 * count), 0)
    select = (slots == position).astype(F32)
    return (select[:, :count] + select[:, count:]).astype(BF16)


def pack_kernel(experts, *refs):
    sources, pos_ref, pass_ref, send_refs = refs[:6], refs[6], refs[7], refs[8 : 8 + experts]
    held, sems = [*refs[8 + experts : 13 + experts], pass_ref], refs[13 + experts]
    copies = [pltpu.make_async_copy(a, b, sems.at[i]) for i, (a, b) in enumerate(zip(sources, held))]
    for copy in copies:
        copy.start()
    for copy in copies:
        copy.wait()
    live_ref, flags_ref, ids_ref, router_ref, tok_ref, _ = held
    count, width = tok_ref.shape
    both = 2 * count
    lanes = max(experts, 8)
    group = lax.axis_index("expert")
    live = live_ref[group]
    ids = ids_ref[...]
    first, second = ids[0:1, :], ids[1:2, :]
    order = jnp.concatenate([first, second], axis=1)
    other = jnp.concatenate([second, first], axis=1)
    lane = lax.broadcasted_iota(jnp.int32, (1, both), 1)
    token = jnp.where(lane < count, lane, lane - count)
    alive = token < live
    expert_rows = lax.broadcasted_iota(jnp.int32, (lanes, both), 0)
    onehot = ((expert_rows == order) & alive).astype(F32)
    earlier = lax.broadcasted_iota(jnp.int32, (both, both), 0)
    later = lax.broadcasted_iota(jnp.int32, (both, both), 1)
    before = dot(onehot.astype(BF16), (earlier < later).astype(BF16), ((1,), (0,)))
    slot = jnp.sum(onehot * before, axis=0, keepdims=True).astype(jnp.int32)
    limit = jnp.full((1, both), CAPG, jnp.int32)
    for e in range(experts):
        limit = jnp.where(order == e, CAPG + RCAP * flags_ref[e], limit)
    kept = alive & (slot < limit)
    position = jnp.where(kept, (order ^ group) * ROWS + slot, -1)
    pos_ref[...] = position

    merged = chosen(position, experts)
    rows_x = dot(merged, tok_ref[...], ((1,), (0,)))

    logits = dot(router_ref[...], tok_ref[...], ((1,), (1,)))
    pick = lax.broadcasted_iota(jnp.int32, (experts, count), 0)
    gap = jnp.sum(
        jnp.where(pick == first, logits, 0.0) - jnp.where(pick == second, logits, 0.0),
        axis=0,
        keepdims=True,
    )
    hi, mid, low = split3(jnp.concatenate([gap, -gap], axis=1))
    meta_row = lax.broadcasted_iota(jnp.int32, (META, both), 0)
    meta = jnp.where(
        meta_row == 0,
        hi,
        jnp.where(
            meta_row == 1,
            mid,
            jnp.where(meta_row == 2, low, jnp.where(meta_row == 3, other.astype(F32), 0.0)),
        ),
    ).astype(BF16)
    span = min(width, LANES)
    near = lax.broadcasted_iota(jnp.int32, (span, both), 0)
    for e in range(experts):
        mine = ((near + e * ROWS == position) & (near < CAP)).astype(F32).astype(BF16)
        block = dot(meta, mine, ((1,), (1,)))
        if width > span:
            block = jnp.concatenate([block, jnp.zeros((META, width - span), F32)], axis=1)
        base = e * ROWS
        send_refs[e][...] = jnp.concatenate([rows_x[base : base + CAP], block], axis=0).astype(BF16)


def stack_kernel(count, *refs):
    for q in range(count):
        refs[-1][q] = refs[q][...]


def join_kernel(groups, _, *refs):
    blocks_d, blocks_x, own_x, own_d = refs[:groups], refs[groups:-2], refs[-2], refs[-1]
    for q in range(groups):
        own_d[q] = blocks_d[q][...]
    if len(blocks_x) == 1:
        own_x[...] = blocks_x[0][...]
    else:
        for k in range(len(blocks_x)):
            own_x[k] = blocks_x[k][...]


def pick_kernel(relative, experts, hops, pos_ref, *refs):
    sources, sends = refs[: len(refs) - experts - 1], refs[len(refs) - experts :]
    merged = chosen(pos_ref[...], experts)
    for k in range(hops):
        rows = dot(merged, sources[k][...] if relative else sources[0][k], ((1,), (0,)))
        for q in range(experts):
            sends[q][k] = rows[q * ROWS : q * ROWS + CAP].astype(BF16)


def column(row):
    size = row.shape[1]
    down = lax.broadcasted_iota(jnp.int32, (size, size), 0)
    across = lax.broadcasted_iota(jnp.int32, (size, size), 1)
    return jnp.sum(jnp.where(down == across, row, 0.0), axis=1, keepdims=True)


def visit(groups, hops, width, relative, body):
    core = lax.axis_index("core")
    z = lax.axis_index("z")
    if width % LANES == 0:
        for side in range(2):
            for k in range(hops):
                at = ((z ^ k if relative else k) * 2 + (core ^ side)) * width
                body(side, k, pl.ds(pl.multiple_of(at, LANES), width))
        return
    for here in range(2):

        @pl.when(core == here)
        def _():
            for side in range(2):
                for k in range(hops):
                    at = (k * 2 + (here ^ side)) * width
                    body(side, k, pl.ds(at, width))


def load_kernel(source, out, mark, sem):
    mark[...] = jnp.zeros(mark.shape, F32)
    copy = pltpu.make_async_copy(source, out, sem)
    copy.start()
    copy.wait()


def forward_kernel(relative, groups, hops, *refs):
    sides, (gate_ref, up_ref, down_ref) = refs[:2], refs[2:5]
    x_ref, hid_ref, active_ref, slope_ref, gates_ref, rival_ref, other_ref, keep_ref, give_ref, total = refs[
        5:
    ]
    width = keep_ref.shape[-1]
    model = x_ref.shape[1]
    units = hid_ref.shape[1]
    tile = min(units, 256)

    def place(side, k, features):
        for q in range(groups):
            x_ref[q * ROWS : (q + 1) * ROWS, features] = sides[side][k, q]

    visit(groups, hops, width, relative, place)
    for q in range(groups):
        logit = jnp.zeros((META, ROWS), F32)
        for k in range(hops):
            for side in range(2):
                meta = sides[side][k, q].astype(F32)[CAP:, :ROWS]
                logit = logit + meta
        gap = column(logit[0:1] + logit[1:2] + logit[2:3])
        here = slice(q * ROWS, (q + 1) * ROWS)
        gates_ref[here, :] = jax.nn.sigmoid(gap)
        rival_ref[here, :] = jax.nn.sigmoid(-gap)
        other_ref[here, :] = column(meta[3:4])

    rows_x = x_ref[...]
    for f in range(0, units, tile):
        now = slice(f, f + tile)
        gate_pre = dot(rows_x, gate_ref[0, :, now], ((1,), (0,)))
        up_pre = dot(rows_x, up_ref[0, :, now], ((1,), (0,)))
        sigma = jax.nn.sigmoid(gate_pre)
        active = gate_pre * sigma
        active_ref[:, now] = active
        slope_ref[:, now] = sigma * (1.0 + gate_pre * (1.0 - sigma)) * up_pre
        hid_ref[:, now] = (active * up_pre).astype(BF16)
    hidden = hid_ref[...]
    for f in range(0, model, 512):
        now = slice(f, f + 512)
        total[:, now] = gates_ref[...] * dot(hidden, down_ref[0, :, now], ((1,), (0,)))

    def emit(side, k, features):
        for q in range(groups):
            rows = total[q * ROWS : (q + 1) * ROWS, features]
            if side == 0:
                keep_ref[k, q] = rows
            else:
                give_ref[k, q] = rows.astype(BF16)

    visit(groups, hops, width, relative, emit)


def backward_kernel(relative, groups, hops, *refs):
    inputs = 2
    x_ref, active_ref, slope_ref, hid_ref, gates_ref, rival_ref, other_ref, down_ref = refs[inputs : inputs + 8]
    d_ref, dgate_ref, dup_ref, keep_ref, give_ref, scratch = refs[inputs + 8 :]
    experts, width = keep_ref.shape[1:]
    units = hid_ref.shape[1]
    tile = min(units, 256)

    def place(side, k, features):
        for q in range(groups):
            rows = gates_ref[q * ROWS : q * ROWS + CAP, :] * refs[side][q, k].astype(F32)
            rows = jnp.concatenate([rows, jnp.zeros((META, width), F32)], axis=0)
            d_ref[q * ROWS : (q + 1) * ROWS, features] = rows.astype(BF16)

    visit(groups, hops, width, relative, place)
    rows_d = d_ref[...]
    dots = jnp.zeros((rows_d.shape[0], 1), F32)
    for f in range(0, units, tile):
        now = slice(f, f + tile)
        d_hidden = dot(rows_d, down_ref[0, now, :], ((1,), (1,)))
        dgate_ref[:, now] = (d_hidden * slope_ref[:, now]).astype(BF16)
        dup_ref[:, now] = (d_hidden * active_ref[:, now]).astype(BF16)
        dots += jnp.sum(hid_ref[:, now].astype(F32) * d_hidden, axis=1, keepdims=True)
    weight = dots * rival_ref[...]
    lane = lax.broadcasted_iota(jnp.int32, (weight.shape[0], experts), 1)
    signed = jnp.where(lane == lax.axis_index("expert"), weight, 0.0) - jnp.where(
        lane == other_ref[...].astype(jnp.int32), weight, 0.0
    )
    router = jnp.zeros((experts, x_ref.shape[1]), F32)
    for piece in split3(signed):
        router = router + dot(piece.astype(BF16), x_ref[...], ((0,), (0,)))
    scratch[...] = router

    def emit(side, k, features):
        rows = scratch[:, features]
        if side == 0:
            keep_ref[k] = rows
        else:
            give_ref[k] = halves(rows).astype(BF16)

    visit(groups, hops, width, relative, emit)


def halves(rows):
    top = rows.astype(BF16).astype(F32)
    return jnp.concatenate([top, rows - top], axis=0)


def merge_kernel(keep_ref, got_ref, rkeep_ref, rgot_ref, *out_refs):
    experts = rkeep_ref.shape[1]
    hops = keep_ref.shape[0]
    for k in range(hops):
        got = rgot_ref[k].astype(F32)
        router = halves(rkeep_ref[k] + got[:experts] + got[experts:])
        put(out_refs[k], keep_ref[k] + got_ref[k].astype(F32), router)


def put(out_ref, blocks, router):
    rows = [blocks[q, :CAP] for q in range(blocks.shape[0])]
    out_ref[...] = jnp.concatenate([*rows, router], axis=0).astype(BF16)


def grads_kernel(x_ref, dgate_ref, dup_ref, _, gate_ref, up_ref, mark_ref):
    rows_x = x_ref[...]
    first = ((0,), (0,))
    gate_ref[0] = dot(rows_x, dgate_ref[...], first).astype(BF16)
    up_ref[0] = dot(rows_x, dup_ref[...], first).astype(BF16)
    mark_ref[...] = jnp.zeros(mark_ref.shape, F32)


def grad_down_kernel(d_ref, hid_ref, _, down_ref, mark_ref):
    down_ref[0] = dot(hid_ref[...], d_ref[...], ((0,), (0,))).astype(BF16)
    mark_ref[...] = jnp.zeros(mark_ref.shape, F32)


def sum_kernel(experts, groups, *refs):
    parts, sends = refs[: len(refs) - groups - 1], refs[len(refs) - groups :]
    total = parts[0][...].astype(F32)
    for ref in parts[1:]:
        total = total + ref[...].astype(F32)
    router = total[groups * CAP :]
    router = halves(router[:experts] + router[experts:])
    height, width = sends[0].shape
    for q, send in enumerate(sends):
        rows = [total[q * CAP : (q + 1) * CAP], router]
        if height > CAP + 2 * experts:
            rows.append(jnp.zeros((height - CAP - 2 * experts, width), F32))
        send[...] = jnp.concatenate(rows, axis=0).astype(BF16)


def combine_kernel(groups, pos_ref, *refs):
    backs, mixed_ref, router_ref = refs[:groups], refs[groups + 1], refs[groups + 2]
    experts, width = router_ref.shape
    blocks = []
    router = jnp.zeros((2 * experts, width), F32)
    for ref in backs:
        block = ref[...].astype(F32)
        router = router + block[CAP : CAP + 2 * experts]
        blocks.append(block[:CAP])
        blocks.append(jnp.zeros((ROWS - CAP, width), F32))
    rows = jnp.concatenate(blocks, axis=0).astype(BF16)
    merged = chosen(pos_ref[...], experts)
    mixed_ref[...] = dot(merged, rows, ((0,), (0,))).astype(BF16)
    router_ref[...] = (router[:experts] + router[experts:]).astype(BF16)


def swap(block, axis, bits):
    size = lax.axis_size(axis)
    return lax.ppermute(block, axis, [(i, i ^ bits) for i in range(size)])


def shards(tokens, expert_ids, live_tokens, replicated, w_router, w_gate, w_up, w_down, cotangent):
    groups = lax.axis_size("expert")
    hops = lax.axis_size("z")
    experts = w_router.shape[1]
    count, width = tokens.shape
    _, model, units = w_gate.shape
    rows = groups * ROWS
    height = -(-(CAP + 2 * experts) // 16) * 16
    relative = width % LANES == 0 and hops == 4
    whole = pl.BlockSpec(memory_space=pltpu.VMEM)
    anywhere = pl.BlockSpec(memory_space=pl.ANY)
    fixed = pl.BlockSpec(memory_space=pltpu.HBM)
    shape = jax.ShapeDtypeStruct

    def call(kernel, args, outs, name, scratch=(), loose=(), cost=None, limit=4 * MIB):
        args = [pltpu.with_memory_space_constraint(a, pltpu.HBM) if i in loose else a for i, a in enumerate(args)]
        return pl.pallas_call(
            kernel,
            out_shape=tuple(outs),
            in_specs=[fixed if i in loose else whole for i in range(len(args))],
            out_specs=(whole,) * len(outs),
            scratch_shapes=list(scratch),
            compiler_params=pltpu.CompilerParams(vmem_limit_bytes=limit),
            cost_estimate=cost,
            name=name,
        )(*args)

    position, handed, *sends = call(
        functools.partial(pack_kernel, experts),
        (live_tokens, replicated, expert_ids.T, w_router.T, tokens, cotangent),
        [shape((1, 2 * count), jnp.int32), shape(cotangent.shape, BF16)] + [shape((ROWS, width), BF16)] * experts,
        "pack",
        scratch=[
            pltpu.SMEM(live_tokens.shape, jnp.int32),
            pltpu.SMEM(replicated.shape, jnp.int32),
            pltpu.VMEM((2, count), jnp.int32),
            pltpu.VMEM((experts, width), BF16),
            pltpu.VMEM((count, width), BF16),
            pltpu.SemaphoreType.DMA((6,)),
        ],
        loose=range(6),
    )
    def load(weight, name):
        return call(
            load_kernel,
            (weight,),
            [pltpu.VMEM(weight.shape, BF16), shape((8, LANES), F32)],
            name,
            scratch=[pltpu.SemaphoreType.DMA],
            loose=(0,),
            cost=pl.CostEstimate(flops=0, bytes_accessed=2 * 2 * model * units, transcendentals=0),
            limit=8 * MIB,
        )

    gate_w, gate_mark = load(w_gate, "load_gate")
    up_w, up_mark = load(w_up, "load_up")
    down_w, down_mark = load(w_down, "load_down")
    def gather(block):
        if relative:
            second = swap(block, "z", 2)
            return [block, swap(block, "z", 1), second, swap(second, "z", 1)]
        return [lax.all_gather(block, "z", axis=0, tiled=False)]

    arrived = [sends[0]] + [swap(sends[q], "expert", q) for q in range(1, groups)]
    slices = gather(handed)
    picked = call(
        functools.partial(pick_kernel, relative, experts, hops),
        (position, *slices, up_mark),
        [shape((hops, CAP, width), BF16)] * experts,
        "pick",
    )
    (stacked,) = call(
        functools.partial(stack_kernel, groups),
        (*arrived, gate_mark, *slices[1:3]),
        [shape((groups, ROWS, width), BF16)],
        "stack",
    )
    blocks_x = [stacked] + [swap(stacked, "z", k) for k in range(1, hops)] if relative else gather(stacked)
    blocks_d = [picked[0]] + [swap(picked[q], "expert", q) for q in range(1, groups)]
    own_x, own_d = call(
        functools.partial(join_kernel, groups),
        (down_mark, *blocks_d, *blocks_x),
        [shape((hops, *stacked.shape), BF16), shape((groups, *picked[0].shape), BF16)],
        "join",
    )
    far_x = swap(own_x, "core", 1)
    far_d = swap(own_d, "core", 1)

    cost = 2 * rows * model * units
    rows_x, hidden, active, slope, gates, rival, others, keep, give = call(
        functools.partial(forward_kernel, relative, groups, hops),
        (own_x, far_x, gate_w, up_w, down_w),
        [
            shape((rows, model), BF16),
            shape((rows, units), BF16),
            shape((rows, units), F32),
            shape((rows, units), F32),
            shape((rows, 1), F32),
            shape((rows, 1), F32),
            shape((rows, 1), F32),
            shape((hops, groups, ROWS, width), F32),
            shape((hops, groups, ROWS, width), BF16),
        ],
        "forward",
        scratch=[pltpu.VMEM((rows, model), F32)],
        cost=pl.CostEstimate(flops=3 * cost, bytes_accessed=6 * model * units, transcendentals=rows * units),
        limit=16 * MIB,
    )
    got = swap(give, "core", 1)
    rows_d, d_gate, d_up, router_keep, router_give = call(
        functools.partial(backward_kernel, relative, groups, hops),
        (own_d, far_d, rows_x, active, slope, hidden, gates, rival, others, down_w),
        [
            shape((rows, model), BF16),
            shape((rows, units), BF16),
            shape((rows, units), BF16),
            shape((hops, experts, width), F32),
            shape((hops, 2 * experts, width), BF16),
        ],
        "backward",
        scratch=[pltpu.VMEM((experts, model), F32)],
        cost=pl.CostEstimate(flops=cost, bytes_accessed=2 * model * units, transcendentals=0),
        limit=14 * MIB,
    )
    router_got = swap(router_give, "core", 1)
    merged = call(
        merge_kernel,
        (keep, got, router_keep, router_got),
        [shape((groups * CAP + 2 * experts, width), BF16)] * hops,
        "merge",
    )
    if relative:
        outs = [merged[0]] + [swap(merged[k], "z", k) for k in range(hops - 1, 0, -1)]
    else:
        outs = lax.all_to_all(jnp.stack(merged), "z", split_axis=0, concat_axis=0, tiled=True)
        outs = [outs[k] for k in range(hops)]

    parts = 8
    once = lambda *shape: pl.BlockSpec(shape, lambda i: (0,) * len(shape))
    strip = max(units // parts, LANES)
    marked = shape((8, LANES), F32)
    grad_gate, grad_up, mark = pl.pallas_call(
        grads_kernel,
        grid=(parts,),
        out_shape=(shape(w_gate.shape, BF16), shape(w_up.shape, BF16), marked),
        in_specs=[
            pl.BlockSpec((rows, model // parts), lambda i: (0, i)),
            once(rows, units),
            once(rows, units),
            anywhere,
        ],
        out_specs=(
            pl.BlockSpec((1, model // parts, units), lambda i: (0, i, 0)),
            pl.BlockSpec((1, model // parts, units), lambda i: (0, i, 0)),
            once(8, LANES),
        ),
        compiler_params=pltpu.CompilerParams(vmem_limit_bytes=20 * MIB),
        cost_estimate=pl.CostEstimate(flops=2 * cost, bytes_accessed=4 * model * units, transcendentals=0),
        name="grads",
    )(rows_x, d_gate, d_up, merged[0])

    backs = call(
        functools.partial(sum_kernel, experts, groups),
        (*outs, mark),
        [shape((height, width), BF16)] * groups,
        "total",
    )
    grad_down, last = pl.pallas_call(
        grad_down_kernel,
        grid=(units // strip,),
        out_shape=(shape(w_down.shape, BF16), marked),
        in_specs=[once(rows, model), pl.BlockSpec((rows, strip), lambda i: (0, i)), anywhere],
        out_specs=(pl.BlockSpec((1, strip, model), lambda i: (0, i, 0)), once(8, LANES)),
        compiler_params=pltpu.CompilerParams(vmem_limit_bytes=20 * MIB),
        cost_estimate=pl.CostEstimate(flops=cost, bytes_accessed=2 * model * units, transcendentals=0),
        name="grad_down",
    )(rows_d, hidden, backs[0])
    backs = [backs[0]] + [swap(backs[q], "expert", q) for q in range(1, groups)]
    mixed, grad_router = call(
        functools.partial(combine_kernel, groups),
        (position, *backs, last),
        [shape((count, width), BF16), shape((experts, width), BF16)],
        "combine",
    )
    return (mixed, grad_gate, grad_up, grad_down, grad_router.T)


def solution(mesh):
    groups, etp = mesh.devices.shape
    inner = Mesh(mesh.devices.reshape(groups, etp // 2, 2), ("expert", "z", "core"))
    etp = ("z", "core")
    in_specs = (
        P("expert", etp),
        P("expert", None),
        P(),
        P(),
        P(etp, None),
        P("expert", None, etp),
        P("expert", None, etp),
        P("expert", etp, None),
        P("expert", etp),
    )
    out_specs = (
        P("expert", etp),
        P("expert", None, etp),
        P("expert", None, etp),
        P("expert", etp, None),
        P(etp, None),
    )
    return jax.shard_map(shards, mesh=inner, in_specs=in_specs, out_specs=out_specs, check_vma=False)
```

```python
import functools

import jax
import jax.numpy as jnp
from jax import lax
from jax.experimental import pallas as pl
from jax.experimental.pallas import tpu as pltpu
from jax.sharding import Mesh, PartitionSpec as P

CAPG = 32
RCAP = 8
CAP = CAPG + RCAP
META = 8
ROWS = CAP + META
MIB = 1024 * 1024
LANES = 128

F32 = jnp.float32
BF16 = jnp.bfloat16


def dot(a, b, dims):
    return lax.dot_general(a, b, (dims, ((), ())), preferred_element_type=F32)


def split3(value):
    hi = value.astype(BF16).astype(F32)
    rest = value - hi
    mid = rest.astype(BF16).astype(F32)
    return hi, mid, rest - mid


def chosen(position, experts):
    count = position.shape[1] // 2
    slots = lax.broadcasted_iota(jnp.int32, (experts * ROWS, 2 * count), 0)
    select = (slots == position).astype(F32)
    return (select[:, :count] + select[:, count:]).astype(BF16)


def pack_kernel(experts, *refs):
    sources, pos_ref, pass_ref, send_refs = refs[:6], refs[6], refs[7], refs[8 : 8 + experts]
    held, sems = [*refs[8 + experts : 13 + experts], pass_ref], refs[13 + experts]
    copies = [pltpu.make_async_copy(a, b, sems.at[i]) for i, (a, b) in enumerate(zip(sources, held))]
    for copy in copies:
        copy.start()
    for copy in copies:
        copy.wait()
    live_ref, flags_ref, ids_ref, router_ref, tok_ref, _ = held
    count, width = tok_ref.shape
    both = 2 * count
    lanes = max(experts, 8)
    group = lax.axis_index("expert")
    live = live_ref[group]
    ids = ids_ref[...]
    first, second = ids[0:1, :], ids[1:2, :]
    order = jnp.concatenate([first, second], axis=1)
    other = jnp.concatenate([second, first], axis=1)
    lane = lax.broadcasted_iota(jnp.int32, (1, both), 1)
    token = jnp.where(lane < count, lane, lane - count)
    alive = token < live
    expert_rows = lax.broadcasted_iota(jnp.int32, (lanes, both), 0)
    onehot = ((expert_rows == order) & alive).astype(F32)
    earlier = lax.broadcasted_iota(jnp.int32, (both, both), 0)
    later = lax.broadcasted_iota(jnp.int32, (both, both), 1)
    before = dot(onehot.astype(BF16), (earlier < later).astype(BF16), ((1,), (0,)))
    slot = jnp.sum(onehot * before, axis=0, keepdims=True).astype(jnp.int32)
    limit = jnp.full((1, both), CAPG, jnp.int32)
    for e in range(experts):
        limit = jnp.where(order == e, CAPG + RCAP * flags_ref[e], limit)
    kept = alive & (slot < limit)
    position = jnp.where(kept, (order ^ group) * ROWS + slot, -1)
    pos_ref[...] = position

    merged = chosen(position, experts)
    rows_x = dot(merged, tok_ref[...], ((1,), (0,)))

    logits = dot(router_ref[...], tok_ref[...], ((1,), (1,)))
    pick = lax.broadcasted_iota(jnp.int32, (experts, count), 0)
    gap = jnp.sum(
        jnp.where(pick == first, logits, 0.0) - jnp.where(pick == second, logits, 0.0),
        axis=0,
        keepdims=True,
    )
    hi, mid, low = split3(jnp.concatenate([gap, -gap], axis=1))
    meta_row = lax.broadcasted_iota(jnp.int32, (META, both), 0)
    meta = jnp.where(
        meta_row == 0,
        hi,
        jnp.where(
            meta_row == 1,
            mid,
            jnp.where(meta_row == 2, low, jnp.where(meta_row == 3, other.astype(F32), 0.0)),
        ),
    ).astype(BF16)
    span = min(width, LANES)
    near = lax.broadcasted_iota(jnp.int32, (span, both), 0)
    for e in range(experts):
        mine = ((near + e * ROWS == position) & (near < CAP)).astype(F32).astype(BF16)
        block = dot(meta, mine, ((1,), (1,)))
        if width > span:
            block = jnp.concatenate([block, jnp.zeros((META, width - span), F32)], axis=1)
        base = e * ROWS
        send_refs[e][...] = jnp.concatenate([rows_x[base : base + CAP], block], axis=0).astype(BF16)


def stack_kernel(count, *refs):
    for q in range(count):
        refs[-1][q] = refs[q][...]


def join_kernel(groups, _, *refs):
    blocks_d, blocks_x, own_x, own_d = refs[:groups], refs[groups:-2], refs[-2], refs[-1]
    for q in range(groups):
        own_d[q] = blocks_d[q][...]
    if len(blocks_x) == 1:
        own_x[...] = blocks_x[0][...]
    else:
        for k in range(len(blocks_x)):
            own_x[k] = blocks_x[k][...]


def pick_kernel(relative, experts, hops, pos_ref, *refs):
    sources, sends = refs[: len(refs) - experts - 1], refs[len(refs) - experts :]
    merged = chosen(pos_ref[...], experts)
    for k in range(hops):
        rows = dot(merged, sources[k][...] if relative else sources[0][k], ((1,), (0,)))
        for q in range(experts):
            sends[q][k] = rows[q * ROWS : q * ROWS + CAP].astype(BF16)


def column(row):
    size = row.shape[1]
    down = lax.broadcasted_iota(jnp.int32, (size, size), 0)
    across = lax.broadcasted_iota(jnp.int32, (size, size), 1)
    return jnp.sum(jnp.where(down == across, row, 0.0), axis=1, keepdims=True)


def visit(groups, hops, width, relative, body):
    core = lax.axis_index("core")
    z = lax.axis_index("z")
    if width % LANES == 0:
        for side in range(2):
            for k in range(hops):
                at = ((z ^ k if relative else k) * 2 + (core ^ side)) * width
                body(side, k, pl.ds(pl.multiple_of(at, LANES), width))
        return
    for here in range(2):

        @pl.when(core == here)
        def _():
            for side in range(2):
                for k in range(hops):
                    at = (k * 2 + (here ^ side)) * width
                    body(side, k, pl.ds(at, width))


def load_kernel(source, out, mark, sem):
    mark[...] = jnp.zeros(mark.shape, F32)
    copy = pltpu.make_async_copy(source, out, sem)
    copy.start()
    copy.wait()


def forward_kernel(relative, groups, hops, *refs):
    sides, (gate_ref, up_ref, down_ref) = refs[:2], refs[2:5]
    x_ref, hid_ref, active_ref, slope_ref, gates_ref, rival_ref, other_ref, keep_ref, give_ref, total = refs[
        5:
    ]
    width = keep_ref.shape[-1]
    model = x_ref.shape[1]
    units = hid_ref.shape[1]
    tile = min(units, 256)

    def place(side, k, features):
        for q in range(groups):
            x_ref[q * ROWS : (q + 1) * ROWS, features] = sides[side][k, q]

    visit(groups, hops, width, relative, place)
    for q in range(groups):
        logit = jnp.zeros((META, ROWS), F32)
        for k in range(hops):
            for side in range(2):
                meta = sides[side][k, q].astype(F32)[CAP:, :ROWS]
                logit = logit + meta
        gap = column(logit[0:1] + logit[1:2] + logit[2:3])
        here = slice(q * ROWS, (q + 1) * ROWS)
        gates_ref[here, :] = jax.nn.sigmoid(gap)
        rival_ref[here, :] = jax.nn.sigmoid(-gap)
        other_ref[here, :] = column(meta[3:4])

    rows_x = x_ref[...]
    for f in range(0, units, tile):
        now = slice(f, f + tile)
        gate_pre = dot(rows_x, gate_ref[0, :, now], ((1,), (0,)))
        up_pre = dot(rows_x, up_ref[0, :, now], ((1,), (0,)))
        sigma = jax.nn.sigmoid(gate_pre)
        active = gate_pre * sigma
        active_ref[:, now] = active
        slope_ref[:, now] = sigma * (1.0 + gate_pre * (1.0 - sigma)) * up_pre
        hid_ref[:, now] = (active * up_pre).astype(BF16)
    hidden = hid_ref[...]
    for f in range(0, model, 512):
        now = slice(f, f + 512)
        total[:, now] = gates_ref[...] * dot(hidden, down_ref[0, :, now], ((1,), (0,)))

    def emit(side, k, features):
        for q in range(groups):
            rows = total[q * ROWS : (q + 1) * ROWS, features]
            if side == 0:
                keep_ref[k, q] = rows
            else:
                give_ref[k, q] = rows.astype(BF16)

    visit(groups, hops, width, relative, emit)


def backward_kernel(relative, groups, hops, *refs):
    inputs = 2
    x_ref, active_ref, slope_ref, hid_ref, gates_ref, rival_ref, other_ref, down_ref = refs[inputs : inputs + 8]
    d_ref, dgate_ref, dup_ref, keep_ref, give_ref, scratch = refs[inputs + 8 :]
    experts, width = keep_ref.shape[1:]
    units = hid_ref.shape[1]
    tile = min(units, 256)

    def place(side, k, features):
        for q in range(groups):
            rows = gates_ref[q * ROWS : q * ROWS + CAP, :] * refs[side][q, k].astype(F32)
            rows = jnp.concatenate([rows, jnp.zeros((META, width), F32)], axis=0)
            d_ref[q * ROWS : (q + 1) * ROWS, features] = rows.astype(BF16)

    visit(groups, hops, width, relative, place)
    rows_d = d_ref[...]
    dots = jnp.zeros((rows_d.shape[0], 1), F32)
    for f in range(0, units, tile):
        now = slice(f, f + tile)
        d_hidden = dot(rows_d, down_ref[0, now, :], ((1,), (1,)))
        dgate_ref[:, now] = (d_hidden * slope_ref[:, now]).astype(BF16)
        dup_ref[:, now] = (d_hidden * active_ref[:, now]).astype(BF16)
        dots += jnp.sum(hid_ref[:, now].astype(F32) * d_hidden, axis=1, keepdims=True)
    weight = dots * rival_ref[...]
    lane = lax.broadcasted_iota(jnp.int32, (weight.shape[0], experts), 1)
    signed = jnp.where(lane == lax.axis_index("expert"), weight, 0.0) - jnp.where(
        lane == other_ref[...].astype(jnp.int32), weight, 0.0
    )
    router = jnp.zeros((experts, x_ref.shape[1]), F32)
    for piece in split3(signed):
        router = router + dot(piece.astype(BF16), x_ref[...], ((0,), (0,)))
    scratch[...] = router

    def emit(side, k, features):
        rows = scratch[:, features]
        if side == 0:
            keep_ref[k] = rows
        else:
            give_ref[k] = halves(rows).astype(BF16)

    visit(groups, hops, width, relative, emit)


def halves(rows):
    top = rows.astype(BF16).astype(F32)
    return jnp.concatenate([top, rows - top], axis=0)


def merge_kernel(keep_ref, got_ref, rkeep_ref, rgot_ref, *out_refs):
    experts = rkeep_ref.shape[1]
    hops = keep_ref.shape[0]
    for k in range(hops):
        got = rgot_ref[k].astype(F32)
        router = halves(rkeep_ref[k] + got[:experts] + got[experts:])
        put(out_refs[k], keep_ref[k] + got_ref[k].astype(F32), router)


def put(out_ref, blocks, router):
    rows = [blocks[q, :CAP] for q in range(blocks.shape[0])]
    out_ref[...] = jnp.concatenate([*rows, router], axis=0).astype(BF16)


def grads_kernel(x_ref, d_ref, dgate_ref, dup_ref, hid_ref, _, gate_ref, up_ref, down_ref, mark_ref):
    rows_x = x_ref[...]
    first = ((0,), (0,))
    gate_ref[0] = dot(rows_x, dgate_ref[...], first).astype(BF16)
    up_ref[0] = dot(rows_x, dup_ref[...], first).astype(BF16)
    down_ref[0] = dot(hid_ref[...], d_ref[...], first).astype(BF16)
    mark_ref[...] = jnp.zeros(mark_ref.shape, F32)


def sum_kernel(experts, groups, *refs):
    parts, sends = refs[: len(refs) - groups - 1], refs[len(refs) - groups :]
    total = parts[0][...].astype(F32)
    for ref in parts[1:]:
        total = total + ref[...].astype(F32)
    router = total[groups * CAP :]
    router = halves(router[:experts] + router[experts:])
    height, width = sends[0].shape
    for q, send in enumerate(sends):
        rows = [total[q * CAP : (q + 1) * CAP], router]
        if height > CAP + 2 * experts:
            rows.append(jnp.zeros((height - CAP - 2 * experts, width), F32))
        send[...] = jnp.concatenate(rows, axis=0).astype(BF16)


def combine_kernel(groups, pos_ref, *refs):
    backs, mixed_ref, router_ref = refs[:groups], refs[groups], refs[groups + 1]
    experts, width = router_ref.shape
    blocks = []
    router = jnp.zeros((2 * experts, width), F32)
    for ref in backs:
        block = ref[...].astype(F32)
        router = router + block[CAP : CAP + 2 * experts]
        blocks.append(block[:CAP])
        blocks.append(jnp.zeros((ROWS - CAP, width), F32))
    rows = jnp.concatenate(blocks, axis=0).astype(BF16)
    merged = chosen(pos_ref[...], experts)
    mixed_ref[...] = dot(merged, rows, ((0,), (0,))).astype(BF16)
    router_ref[...] = (router[:experts] + router[experts:]).astype(BF16)


def swap(block, axis, bits):
    size = lax.axis_size(axis)
    return lax.ppermute(block, axis, [(i, i ^ bits) for i in range(size)])


def shards(tokens, expert_ids, live_tokens, replicated, w_router, w_gate, w_up, w_down, cotangent):
    groups = lax.axis_size("expert")
    hops = lax.axis_size("z")
    experts = w_router.shape[1]
    count, width = tokens.shape
    _, model, units = w_gate.shape
    rows = groups * ROWS
    height = -(-(CAP + 2 * experts) // 16) * 16
    relative = width % LANES == 0 and hops == 4
    whole = pl.BlockSpec(memory_space=pltpu.VMEM)
    anywhere = pl.BlockSpec(memory_space=pl.ANY)
    fixed = pl.BlockSpec(memory_space=pltpu.HBM)
    shape = jax.ShapeDtypeStruct

    def call(kernel, args, outs, name, scratch=(), loose=(), cost=None, limit=4 * MIB):
        args = [pltpu.with_memory_space_constraint(a, pltpu.HBM) if i in loose else a for i, a in enumerate(args)]
        return pl.pallas_call(
            kernel,
            out_shape=tuple(outs),
            in_specs=[fixed if i in loose else whole for i in range(len(args))],
            out_specs=(whole,) * len(outs),
            scratch_shapes=list(scratch),
            compiler_params=pltpu.CompilerParams(vmem_limit_bytes=limit),
            cost_estimate=cost,
            name=name,
        )(*args)

    position, handed, *sends = call(
        functools.partial(pack_kernel, experts),
        (live_tokens, replicated, expert_ids.T, w_router.T, tokens, cotangent),
        [shape((1, 2 * count), jnp.int32), shape(cotangent.shape, BF16)] + [shape((ROWS, width), BF16)] * experts,
        "pack",
        scratch=[
            pltpu.SMEM(live_tokens.shape, jnp.int32),
            pltpu.SMEM(replicated.shape, jnp.int32),
            pltpu.VMEM((2, count), jnp.int32),
            pltpu.VMEM((experts, width), BF16),
            pltpu.VMEM((count, width), BF16),
            pltpu.SemaphoreType.DMA((6,)),
        ],
        loose=range(6),
    )
    def load(weight, name):
        return call(
            load_kernel,
            (weight,),
            [pltpu.VMEM(weight.shape, BF16), shape((8, LANES), F32)],
            name,
            scratch=[pltpu.SemaphoreType.DMA],
            loose=(0,),
            cost=pl.CostEstimate(flops=0, bytes_accessed=2 * 2 * model * units, transcendentals=0),
            limit=8 * MIB,
        )

    gate_w, gate_mark = load(w_gate, "load_gate")
    up_w, up_mark = load(w_up, "load_up")
    down_w, down_mark = load(w_down, "load_down")
    def gather(block):
        if relative:
            second = swap(block, "z", 2)
            return [block, swap(block, "z", 1), second, swap(second, "z", 1)]
        return [lax.all_gather(block, "z", axis=0, tiled=False)]

    arrived = [sends[0]] + [swap(sends[q], "expert", q) for q in range(1, groups)]
    slices = gather(handed)
    picked = call(
        functools.partial(pick_kernel, relative, experts, hops),
        (position, *slices, up_mark),
        [shape((hops, CAP, width), BF16)] * experts,
        "pick",
    )
    (stacked,) = call(
        functools.partial(stack_kernel, groups),
        (*arrived, gate_mark, *slices[1:3]),
        [shape((groups, ROWS, width), BF16)],
        "stack",
    )
    blocks_x = [stacked] + [swap(stacked, "z", k) for k in range(1, hops)] if relative else gather(stacked)
    blocks_d = [picked[0]] + [swap(picked[q], "expert", q) for q in range(1, groups)]
    own_x, own_d = call(
        functools.partial(join_kernel, groups),
        (down_mark, *blocks_d, *blocks_x),
        [shape((hops, *stacked.shape), BF16), shape((groups, *picked[0].shape), BF16)],
        "join",
    )
    far_x = swap(own_x, "core", 1)
    far_d = swap(own_d, "core", 1)

    cost = 2 * rows * model * units
    rows_x, hidden, active, slope, gates, rival, others, keep, give = call(
        functools.partial(forward_kernel, relative, groups, hops),
        (own_x, far_x, gate_w, up_w, down_w),
        [
            shape((rows, model), BF16),
            shape((rows, units), BF16),
            shape((rows, units), F32),
            shape((rows, units), F32),
            shape((rows, 1), F32),
            shape((rows, 1), F32),
            shape((rows, 1), F32),
            shape((hops, groups, ROWS, width), F32),
            shape((hops, groups, ROWS, width), BF16),
        ],
        "forward",
        scratch=[pltpu.VMEM((rows, model), F32)],
        cost=pl.CostEstimate(flops=3 * cost, bytes_accessed=6 * model * units, transcendentals=rows * units),
        limit=16 * MIB,
    )
    got = swap(give, "core", 1)
    rows_d, d_gate, d_up, router_keep, router_give = call(
        functools.partial(backward_kernel, relative, groups, hops),
        (own_d, far_d, rows_x, active, slope, hidden, gates, rival, others, down_w),
        [
            shape((rows, model), BF16),
            shape((rows, units), BF16),
            shape((rows, units), BF16),
            shape((hops, experts, width), F32),
            shape((hops, 2 * experts, width), BF16),
        ],
        "backward",
        scratch=[pltpu.VMEM((experts, model), F32)],
        cost=pl.CostEstimate(flops=cost, bytes_accessed=2 * model * units, transcendentals=0),
        limit=14 * MIB,
    )
    router_got = swap(router_give, "core", 1)
    merged = call(
        merge_kernel,
        (keep, got, router_keep, router_got),
        [shape((groups * CAP + 2 * experts, width), BF16)] * hops,
        "merge",
    )
    if relative:
        outs = [merged[0]] + [swap(merged[k], "z", k) for k in range(hops - 1, 0, -1)]
    else:
        outs = lax.all_to_all(jnp.stack(merged), "z", split_axis=0, concat_axis=0, tiled=True)
        outs = [outs[k] for k in range(hops)]

    parts = 8
    once = lambda *shape: pl.BlockSpec(shape, lambda i: (0,) * len(shape))
    strip = max(units // parts, LANES)
    at = lambda i: i if units >= LANES * parts else 0
    grad_gate, grad_up, grad_down, mark = pl.pallas_call(
        grads_kernel,
        grid=(parts,),
        out_shape=(
            shape(w_gate.shape, BF16),
            shape(w_up.shape, BF16),
            shape(w_down.shape, BF16),
            shape((8, LANES), F32),
        ),
        in_specs=[
            pl.BlockSpec((rows, model // parts), lambda i: (0, i)),
            once(rows, model),
            once(rows, units),
            once(rows, units),
            pl.BlockSpec((rows, strip), lambda i: (0, at(i))),
            anywhere,
        ],
        out_specs=(
            pl.BlockSpec((1, model // parts, units), lambda i: (0, i, 0)),
            pl.BlockSpec((1, model // parts, units), lambda i: (0, i, 0)),
            pl.BlockSpec((1, strip, model), lambda i: (0, at(i), 0)),
            once(8, LANES),
        ),
        compiler_params=pltpu.CompilerParams(vmem_limit_bytes=24 * MIB),
        cost_estimate=pl.CostEstimate(flops=3 * cost, bytes_accessed=6 * model * units, transcendentals=0),
        name="grads",
    )(rows_x, rows_d, d_gate, d_up, hidden, merged[0])

    backs = call(
        functools.partial(sum_kernel, experts, groups),
        (*outs, mark),
        [shape((height, width), BF16)] * groups,
        "total",
    )
    backs = [backs[0]] + [swap(backs[q], "expert", q) for q in range(1, groups)]
    mixed, grad_router = call(
        functools.partial(combine_kernel, groups),
        (position, *backs),
        [shape((count, width), BF16), shape((experts, width), BF16)],
        "combine",
    )
    return (mixed, grad_gate, grad_up, grad_down, grad_router.T)


def solution(mesh):
    groups, etp = mesh.devices.shape
    inner = Mesh(mesh.devices.reshape(groups, etp // 2, 2), ("expert", "z", "core"))
    etp = ("z", "core")
    in_specs = (
        P("expert", etp),
        P("expert", None),
        P(),
        P(),
        P(etp, None),
        P("expert", None, etp),
        P("expert", None, etp),
        P("expert", etp, None),
        P("expert", etp),
    )
    out_specs = (
        P("expert", etp),
        P("expert", None, etp),
        P("expert", None, etp),
        P("expert", etp, None),
        P(etp, None),
    )
    return jax.shard_map(shards, mesh=inner, in_specs=in_specs, out_specs=out_specs, check_vma=False)
```

```python
import functools

import jax
import jax.numpy as jnp
from jax import lax
from jax.experimental import pallas as pl
from jax.experimental.pallas import tpu as pltpu
from jax.sharding import Mesh, PartitionSpec as P

CAPG = 32
RCAP = 8
CAP = CAPG + RCAP
META = 8
ROWS = CAP + META
MIB = 1024 * 1024
LANES = 128

F32 = jnp.float32
BF16 = jnp.bfloat16


def dot(a, b, dims):
    return lax.dot_general(a, b, (dims, ((), ())), preferred_element_type=F32)


def split3(value):
    hi = value.astype(BF16).astype(F32)
    rest = value - hi
    mid = rest.astype(BF16).astype(F32)
    return hi, mid, rest - mid


def chosen(position, experts):
    count = position.shape[1] // 2
    slots = lax.broadcasted_iota(jnp.int32, (experts * ROWS, 2 * count), 0)
    select = (slots == position).astype(F32)
    return (select[:, :count] + select[:, count:]).astype(BF16)


def pack_kernel(experts, *refs):
    sources, pos_ref, pass_ref, send_refs = refs[:6], refs[6], refs[7], refs[8 : 8 + experts]
    held, sems = [*refs[8 + experts : 13 + experts], pass_ref], refs[13 + experts]
    copies = [pltpu.make_async_copy(a, b, sems.at[i]) for i, (a, b) in enumerate(zip(sources, held))]
    for copy in copies:
        copy.start()
    for copy in copies:
        copy.wait()
    live_ref, flags_ref, ids_ref, router_ref, tok_ref, _ = held
    count, width = tok_ref.shape
    both = 2 * count
    lanes = max(experts, 8)
    group = lax.axis_index("expert")
    live = live_ref[group]
    ids = ids_ref[...]
    first, second = ids[0:1, :], ids[1:2, :]
    order = jnp.concatenate([first, second], axis=1)
    other = jnp.concatenate([second, first], axis=1)
    lane = lax.broadcasted_iota(jnp.int32, (1, both), 1)
    token = jnp.where(lane < count, lane, lane - count)
    alive = token < live
    expert_rows = lax.broadcasted_iota(jnp.int32, (lanes, both), 0)
    onehot = ((expert_rows == order) & alive).astype(F32)
    earlier = lax.broadcasted_iota(jnp.int32, (both, both), 0)
    later = lax.broadcasted_iota(jnp.int32, (both, both), 1)
    before = dot(onehot.astype(BF16), (earlier < later).astype(BF16), ((1,), (0,)))
    slot = jnp.sum(onehot * before, axis=0, keepdims=True).astype(jnp.int32)
    limit = jnp.full((1, both), CAPG, jnp.int32)
    for e in range(experts):
        limit = jnp.where(order == e, CAPG + RCAP * flags_ref[e], limit)
    kept = alive & (slot < limit)
    position = jnp.where(kept, (order ^ group) * ROWS + slot, -1)
    pos_ref[...] = position

    merged = chosen(position, experts)
    rows_x = dot(merged, tok_ref[...], ((1,), (0,)))

    logits = dot(router_ref[...], tok_ref[...], ((1,), (1,)))
    pick = lax.broadcasted_iota(jnp.int32, (experts, count), 0)
    gap = jnp.sum(
        jnp.where(pick == first, logits, 0.0) - jnp.where(pick == second, logits, 0.0),
        axis=0,
        keepdims=True,
    )
    hi, mid, low = split3(jnp.concatenate([gap, -gap], axis=1))
    meta_row = lax.broadcasted_iota(jnp.int32, (META, both), 0)
    meta = jnp.where(
        meta_row == 0,
        hi,
        jnp.where(
            meta_row == 1,
            mid,
            jnp.where(meta_row == 2, low, jnp.where(meta_row == 3, other.astype(F32), 0.0)),
        ),
    ).astype(BF16)
    span = min(width, LANES)
    near = lax.broadcasted_iota(jnp.int32, (span, both), 0)
    for e in range(experts):
        mine = ((near + e * ROWS == position) & (near < CAP)).astype(F32).astype(BF16)
        block = dot(meta, mine, ((1,), (1,)))
        if width > span:
            block = jnp.concatenate([block, jnp.zeros((META, width - span), F32)], axis=1)
        base = e * ROWS
        send_refs[e][...] = jnp.concatenate([rows_x[base : base + CAP], block], axis=0).astype(BF16)


def stack_kernel(count, *refs):
    for q in range(count):
        refs[-1][q] = refs[count - 1 - q][...]


def join_kernel(groups, _, *refs):
    blocks_d, blocks_x, own_x, own_d = refs[:groups], refs[groups:-2], refs[-2], refs[-1]
    for q in range(groups):
        own_d[q] = blocks_d[groups - 1 - q][...]
    if len(blocks_x) == 1:
        own_x[...] = blocks_x[0][...]
    else:
        for k in range(len(blocks_x)):
            own_x[k] = blocks_x[k][...]


def pick_kernel(relative, experts, hops, pos_ref, *refs):
    sources, sends = refs[: len(refs) - experts - 1], refs[len(refs) - experts :]
    merged = chosen(pos_ref[...], experts)
    for k in range(hops):
        rows = dot(merged, sources[k][...] if relative else sources[0][k], ((1,), (0,)))
        for q in range(experts):
            sends[q][k] = rows[q * ROWS : q * ROWS + CAP].astype(BF16)


def column(row):
    size = row.shape[1]
    down = lax.broadcasted_iota(jnp.int32, (size, size), 0)
    across = lax.broadcasted_iota(jnp.int32, (size, size), 1)
    return jnp.sum(jnp.where(down == across, row, 0.0), axis=1, keepdims=True)


def visit(groups, hops, width, relative, body):
    core = lax.axis_index("core")
    z = lax.axis_index("z")
    if width % LANES == 0:
        for side in range(2):
            for k in range(hops):
                at = ((z ^ k if relative else k) * 2 + (core ^ side)) * width
                body(side, k, pl.ds(pl.multiple_of(at, LANES), width))
        return
    for here in range(2):

        @pl.when(core == here)
        def _():
            for side in range(2):
                for k in range(hops):
                    at = (k * 2 + (here ^ side)) * width
                    body(side, k, pl.ds(at, width))


def load_kernel(source, out, mark, sem):
    mark[...] = jnp.zeros(mark.shape, F32)
    copy = pltpu.make_async_copy(source, out, sem)
    copy.start()
    copy.wait()


def forward_kernel(relative, groups, hops, *refs):
    sides, (gate_ref, up_ref, down_ref) = refs[:2], refs[2:5]
    x_ref, hid_ref, active_ref, slope_ref, gates_ref, rival_ref, other_ref, keep_ref, give_ref, total = refs[
        5:
    ]
    width = keep_ref.shape[-1]
    model = x_ref.shape[1]
    units = hid_ref.shape[1]
    tile = min(units, 256)

    def place(side, k, features):
        for q in range(groups):
            x_ref[q * ROWS : (q + 1) * ROWS, features] = sides[side][k, q]

    visit(groups, hops, width, relative, place)
    for q in range(groups):
        logit = jnp.zeros((META, ROWS), F32)
        for k in range(hops):
            for side in range(2):
                meta = sides[side][k, q].astype(F32)[CAP:, :ROWS]
                logit = logit + meta
        gap = column(logit[0:1] + logit[1:2] + logit[2:3])
        here = slice(q * ROWS, (q + 1) * ROWS)
        gates_ref[here, :] = jax.nn.sigmoid(gap)
        rival_ref[here, :] = jax.nn.sigmoid(-gap)
        other_ref[here, :] = column(meta[3:4])

    rows_x = x_ref[...]
    for f in range(0, units, tile):
        now = slice(f, f + tile)
        gate_pre = dot(rows_x, gate_ref[0, :, now], ((1,), (0,)))
        up_pre = dot(rows_x, up_ref[0, :, now], ((1,), (0,)))
        sigma = jax.nn.sigmoid(gate_pre)
        active = gate_pre * sigma
        active_ref[:, now] = active
        slope_ref[:, now] = sigma * (1.0 + gate_pre * (1.0 - sigma)) * up_pre
        hid_ref[:, now] = (active * up_pre).astype(BF16)
    hidden = hid_ref[...]
    for f in range(0, model, 512):
        now = slice(f, f + 512)
        total[:, now] = gates_ref[...] * dot(hidden, down_ref[0, :, now], ((1,), (0,)))

    def emit(side, k, features):
        for q in range(groups):
            rows = total[q * ROWS : (q + 1) * ROWS, features]
            if side == 0:
                keep_ref[k, q] = rows
            else:
                give_ref[k, q] = rows.astype(BF16)

    visit(groups, hops, width, relative, emit)


def backward_kernel(relative, groups, hops, *refs):
    inputs = 2
    x_ref, active_ref, slope_ref, hid_ref, gates_ref, rival_ref, other_ref, down_ref = refs[inputs : inputs + 8]
    d_ref, dgate_ref, dup_ref, keep_ref, give_ref, scratch = refs[inputs + 8 :]
    experts, width = keep_ref.shape[1:]
    units = hid_ref.shape[1]
    tile = min(units, 256)

    def place(side, k, features):
        for q in range(groups):
            rows = gates_ref[q * ROWS : q * ROWS + CAP, :] * refs[side][q, k].astype(F32)
            rows = jnp.concatenate([rows, jnp.zeros((META, width), F32)], axis=0)
            d_ref[q * ROWS : (q + 1) * ROWS, features] = rows.astype(BF16)

    visit(groups, hops, width, relative, place)
    rows_d = d_ref[...]
    dots = jnp.zeros((rows_d.shape[0], 1), F32)
    for f in range(0, units, tile):
        now = slice(f, f + tile)
        d_hidden = dot(rows_d, down_ref[0, now, :], ((1,), (1,)))
        dgate_ref[:, now] = (d_hidden * slope_ref[:, now]).astype(BF16)
        dup_ref[:, now] = (d_hidden * active_ref[:, now]).astype(BF16)
        dots += jnp.sum(hid_ref[:, now].astype(F32) * d_hidden, axis=1, keepdims=True)
    weight = dots * rival_ref[...]
    lane = lax.broadcasted_iota(jnp.int32, (weight.shape[0], experts), 1)
    signed = jnp.where(lane == lax.axis_index("expert"), weight, 0.0) - jnp.where(
        lane == other_ref[...].astype(jnp.int32), weight, 0.0
    )
    router = jnp.zeros((experts, x_ref.shape[1]), F32)
    for piece in split3(signed):
        router = router + dot(piece.astype(BF16), x_ref[...], ((0,), (0,)))
    scratch[...] = router

    def emit(side, k, features):
        rows = scratch[:, features]
        if side == 0:
            keep_ref[k] = rows
        else:
            give_ref[k] = halves(rows).astype(BF16)

    visit(groups, hops, width, relative, emit)


def halves(rows):
    top = rows.astype(BF16).astype(F32)
    return jnp.concatenate([top, rows - top], axis=0)


def merge_kernel(keep_ref, got_ref, rkeep_ref, rgot_ref, *out_refs):
    experts = rkeep_ref.shape[1]
    hops = keep_ref.shape[0]
    for k in range(hops):
        got = rgot_ref[k].astype(F32)
        router = halves(rkeep_ref[k] + got[:experts] + got[experts:])
        put(out_refs[k], keep_ref[k] + got_ref[k].astype(F32), router)


def put(out_ref, blocks, router):
    rows = [blocks[q, :CAP] for q in range(blocks.shape[0])]
    out_ref[...] = jnp.concatenate([*rows, router], axis=0).astype(BF16)


def grads_kernel(x_ref, d_ref, dgate_ref, dup_ref, hid_ref, _, gate_ref, up_ref, down_ref, mark_ref):
    rows_x = x_ref[...]
    first = ((0,), (0,))
    gate_ref[0] = dot(rows_x, dgate_ref[...], first).astype(BF16)
    up_ref[0] = dot(rows_x, dup_ref[...], first).astype(BF16)
    down_ref[0] = dot(hid_ref[...], d_ref[...], first).astype(BF16)
    mark_ref[...] = jnp.zeros(mark_ref.shape, F32)


def sum_kernel(experts, groups, *refs):
    parts, sends = refs[: len(refs) - groups - 1], refs[len(refs) - groups :]
    total = parts[0][...].astype(F32)
    for ref in parts[1:]:
        total = total + ref[...].astype(F32)
    router = total[groups * CAP :]
    router = halves(router[:experts] + router[experts:])
    height, width = sends[0].shape
    for q, send in enumerate(sends):
        rows = [total[q * CAP : (q + 1) * CAP], router]
        if height > CAP + 2 * experts:
            rows.append(jnp.zeros((height - CAP - 2 * experts, width), F32))
        send[...] = jnp.concatenate(rows, axis=0).astype(BF16)


def combine_kernel(groups, pos_ref, *refs):
    backs, mixed_ref, router_ref = refs[:groups], refs[groups], refs[groups + 1]
    experts, width = router_ref.shape
    blocks = []
    router = jnp.zeros((2 * experts, width), F32)
    for ref in reversed(backs):
        block = ref[...].astype(F32)
        router = router + block[CAP : CAP + 2 * experts]
        blocks.append(block[:CAP])
        blocks.append(jnp.zeros((ROWS - CAP, width), F32))
    rows = jnp.concatenate(blocks, axis=0).astype(BF16)
    merged = chosen(pos_ref[...], experts)
    mixed_ref[...] = dot(merged, rows, ((0,), (0,))).astype(BF16)
    router_ref[...] = (router[:experts] + router[experts:]).astype(BF16)


def swap(block, axis, bits):
    size = lax.axis_size(axis)
    return lax.ppermute(block, axis, [(i, i ^ bits) for i in range(size)])


def shards(tokens, expert_ids, live_tokens, replicated, w_router, w_gate, w_up, w_down, cotangent):
    groups = lax.axis_size("expert")
    hops = lax.axis_size("z")
    experts = w_router.shape[1]
    count, width = tokens.shape
    _, model, units = w_gate.shape
    rows = groups * ROWS
    height = -(-(CAP + 2 * experts) // 16) * 16
    relative = width % LANES == 0 and hops == 4
    whole = pl.BlockSpec(memory_space=pltpu.VMEM)
    anywhere = pl.BlockSpec(memory_space=pl.ANY)
    fixed = pl.BlockSpec(memory_space=pltpu.HBM)
    shape = jax.ShapeDtypeStruct

    def call(kernel, args, outs, name, scratch=(), loose=(), cost=None, limit=4 * MIB):
        args = [pltpu.with_memory_space_constraint(a, pltpu.HBM) if i in loose else a for i, a in enumerate(args)]
        return pl.pallas_call(
            kernel,
            out_shape=tuple(outs),
            in_specs=[fixed if i in loose else whole for i in range(len(args))],
            out_specs=(whole,) * len(outs),
            scratch_shapes=list(scratch),
            compiler_params=pltpu.CompilerParams(vmem_limit_bytes=limit),
            cost_estimate=cost,
            name=name,
        )(*args)

    position, handed, *sends = call(
        functools.partial(pack_kernel, experts),
        (live_tokens, replicated, expert_ids.T, w_router.T, tokens, cotangent),
        [shape((1, 2 * count), jnp.int32), shape(cotangent.shape, BF16)] + [shape((ROWS, width), BF16)] * experts,
        "pack",
        scratch=[
            pltpu.SMEM(live_tokens.shape, jnp.int32),
            pltpu.SMEM(replicated.shape, jnp.int32),
            pltpu.VMEM((2, count), jnp.int32),
            pltpu.VMEM((experts, width), BF16),
            pltpu.VMEM((count, width), BF16),
            pltpu.SemaphoreType.DMA((6,)),
        ],
        loose=range(6),
    )
    def load(weight, name):
        return call(
            load_kernel,
            (weight,),
            [pltpu.VMEM(weight.shape, BF16), shape((8, LANES), F32)],
            name,
            scratch=[pltpu.SemaphoreType.DMA],
            loose=(0,),
            cost=pl.CostEstimate(flops=0, bytes_accessed=2 * 2 * model * units, transcendentals=0),
            limit=8 * MIB,
        )

    gate_w, gate_mark = load(w_gate, "load_gate")
    up_w, up_mark = load(w_up, "load_up")
    down_w, down_mark = load(w_down, "load_down")
    def gather(block):
        if relative:
            second = swap(block, "z", 2)
            return [block, swap(block, "z", 1), second, swap(second, "z", 1)]
        return [lax.all_gather(block, "z", axis=0, tiled=False)]

    def exchange(blocks):
        return [swap(blocks[q], "expert", q) for q in range(groups - 1, 0, -1)] + [blocks[0]]

    arrived = exchange(sends)
    slices = gather(handed)
    picked = call(
        functools.partial(pick_kernel, relative, experts, hops),
        (position, *slices, up_mark),
        [shape((hops, CAP, width), BF16)] * experts,
        "pick",
    )
    (stacked,) = call(
        functools.partial(stack_kernel, groups),
        (*arrived, gate_mark, *slices[1:3]),
        [shape((groups, ROWS, width), BF16)],
        "stack",
    )
    blocks_x = [stacked] + [swap(stacked, "z", k) for k in range(1, hops)] if relative else gather(stacked)
    blocks_d = exchange(picked)
    own_x, own_d = call(
        functools.partial(join_kernel, groups),
        (down_mark, *blocks_d, *blocks_x),
        [shape((hops, *stacked.shape), BF16), shape((groups, *picked[0].shape), BF16)],
        "join",
    )
    far_x = swap(own_x, "core", 1)
    far_d = swap(own_d, "core", 1)

    cost = 2 * rows * model * units
    rows_x, hidden, active, slope, gates, rival, others, keep, give = call(
        functools.partial(forward_kernel, relative, groups, hops),
        (own_x, far_x, gate_w, up_w, down_w),
        [
            shape((rows, model), BF16),
            shape((rows, units), BF16),
            shape((rows, units), F32),
            shape((rows, units), F32),
            shape((rows, 1), F32),
            shape((rows, 1), F32),
            shape((rows, 1), F32),
            shape((hops, groups, ROWS, width), F32),
            shape((hops, groups, ROWS, width), BF16),
        ],
        "forward",
        scratch=[pltpu.VMEM((rows, model), F32)],
        cost=pl.CostEstimate(flops=3 * cost, bytes_accessed=6 * model * units, transcendentals=rows * units),
        limit=16 * MIB,
    )
    got = swap(give, "core", 1)
    rows_d, d_gate, d_up, router_keep, router_give = call(
        functools.partial(backward_kernel, relative, groups, hops),
        (own_d, far_d, rows_x, active, slope, hidden, gates, rival, others, down_w),
        [
            shape((rows, model), BF16),
            shape((rows, units), BF16),
            shape((rows, units), BF16),
            shape((hops, experts, width), F32),
            shape((hops, 2 * experts, width), BF16),
        ],
        "backward",
        scratch=[pltpu.VMEM((experts, model), F32)],
        cost=pl.CostEstimate(flops=cost, bytes_accessed=2 * model * units, transcendentals=0),
        limit=14 * MIB,
    )
    router_got = swap(router_give, "core", 1)
    merged = call(
        merge_kernel,
        (keep, got, router_keep, router_got),
        [shape((groups * CAP + 2 * experts, width), BF16)] * hops,
        "merge",
    )
    if relative:
        outs = [merged[0]] + [swap(merged[k], "z", k) for k in range(hops - 1, 0, -1)]
    else:
        outs = lax.all_to_all(jnp.stack(merged), "z", split_axis=0, concat_axis=0, tiled=True)
        outs = [outs[k] for k in range(hops)]

    parts = 8
    once = lambda *shape: pl.BlockSpec(shape, lambda i: (0,) * len(shape))
    strip = max(units // parts, LANES)
    at = lambda i: i if units >= LANES * parts else 0
    grad_gate, grad_up, grad_down, mark = pl.pallas_call(
        grads_kernel,
        grid=(parts,),
        out_shape=(
            shape(w_gate.shape, BF16),
            shape(w_up.shape, BF16),
            shape(w_down.shape, BF16),
            shape((8, LANES), F32),
        ),
        in_specs=[
            pl.BlockSpec((rows, model // parts), lambda i: (0, i)),
            once(rows, model),
            once(rows, units),
            once(rows, units),
            pl.BlockSpec((rows, strip), lambda i: (0, at(i))),
            anywhere,
        ],
        out_specs=(
            pl.BlockSpec((1, model // parts, units), lambda i: (0, i, 0)),
            pl.BlockSpec((1, model // parts, units), lambda i: (0, i, 0)),
            pl.BlockSpec((1, strip, model), lambda i: (0, at(i), 0)),
            once(8, LANES),
        ),
        compiler_params=pltpu.CompilerParams(vmem_limit_bytes=24 * MIB),
        cost_estimate=pl.CostEstimate(flops=3 * cost, bytes_accessed=6 * model * units, transcendentals=0),
        name="grads",
    )(rows_x, rows_d, d_gate, d_up, hidden, merged[0])

    backs = call(
        functools.partial(sum_kernel, experts, groups),
        (*outs, mark),
        [shape((height, width), BF16)] * groups,
        "total",
    )
    backs = exchange(backs)
    mixed, grad_router = call(
        functools.partial(combine_kernel, groups),
        (position, *backs),
        [shape((count, width), BF16), shape((experts, width), BF16)],
        "combine",
    )
    return (mixed, grad_gate, grad_up, grad_down, grad_router.T)


def solution(mesh):
    groups, etp = mesh.devices.shape
    inner = Mesh(mesh.devices.reshape(groups, etp // 2, 2), ("expert", "z", "core"))
    etp = ("z", "core")
    in_specs = (
        P("expert", etp),
        P("expert", None),
        P(),
        P(),
        P(etp, None),
        P("expert", None, etp),
        P("expert", None, etp),
        P("expert", etp, None),
        P("expert", etp),
    )
    out_specs = (
        P("expert", etp),
        P("expert", None, etp),
        P("expert", None, etp),
        P("expert", etp, None),
        P(etp, None),
    )
    return jax.shard_map(shards, mesh=inner, in_specs=in_specs, out_specs=out_specs, check_vma=False)
```

```python
import functools

import jax
import jax.numpy as jnp
from jax import lax
from jax.experimental import pallas as pl
from jax.experimental.pallas import tpu as pltpu
from jax.sharding import Mesh, PartitionSpec as P

CAPG = 32
RCAP = 8
CAP = CAPG + RCAP
META = 8
ROWS = CAP + META
MIB = 1024 * 1024
LANES = 128

F32 = jnp.float32
BF16 = jnp.bfloat16


def dot(a, b, dims):
    return lax.dot_general(a, b, (dims, ((), ())), preferred_element_type=F32)


def split3(value):
    hi = value.astype(BF16).astype(F32)
    rest = value - hi
    mid = rest.astype(BF16).astype(F32)
    return hi, mid, rest - mid


def chosen(position, experts):
    count = position.shape[1] // 2
    slots = lax.broadcasted_iota(jnp.int32, (experts * ROWS, 2 * count), 0)
    select = (slots == position).astype(F32)
    return (select[:, :count] + select[:, count:]).astype(BF16)


def pack_kernel(experts, *refs):
    sources, pos_ref, pass_ref, send_refs = refs[:6], refs[6], refs[7], refs[8 : 8 + experts]
    held, sems = [*refs[8 + experts : 13 + experts], pass_ref], refs[13 + experts]
    copies = [pltpu.make_async_copy(a, b, sems.at[i]) for i, (a, b) in enumerate(zip(sources, held))]
    for copy in copies:
        copy.start()
    for copy in copies:
        copy.wait()
    live_ref, flags_ref, ids_ref, router_ref, tok_ref, _ = held
    count, width = tok_ref.shape
    both = 2 * count
    lanes = max(experts, 8)
    group = lax.axis_index("expert")
    live = live_ref[group]
    ids = ids_ref[...]
    first, second = ids[0:1, :], ids[1:2, :]
    order = jnp.concatenate([first, second], axis=1)
    other = jnp.concatenate([second, first], axis=1)
    lane = lax.broadcasted_iota(jnp.int32, (1, both), 1)
    token = jnp.where(lane < count, lane, lane - count)
    alive = token < live
    expert_rows = lax.broadcasted_iota(jnp.int32, (lanes, both), 0)
    onehot = ((expert_rows == order) & alive).astype(F32)
    earlier = lax.broadcasted_iota(jnp.int32, (both, both), 0)
    later = lax.broadcasted_iota(jnp.int32, (both, both), 1)
    before = dot(onehot.astype(BF16), (earlier < later).astype(BF16), ((1,), (0,)))
    slot = jnp.sum(onehot * before, axis=0, keepdims=True).astype(jnp.int32)
    limit = jnp.full((1, both), CAPG, jnp.int32)
    for e in range(experts):
        limit = jnp.where(order == e, CAPG + RCAP * flags_ref[e], limit)
    kept = alive & (slot < limit)
    position = jnp.where(kept, (order ^ group) * ROWS + slot, -1)
    pos_ref[...] = position

    merged = chosen(position, experts)
    rows_x = dot(merged, tok_ref[...], ((1,), (0,)))

    logits = dot(router_ref[...], tok_ref[...], ((1,), (1,)))
    pick = lax.broadcasted_iota(jnp.int32, (experts, count), 0)
    gap = jnp.sum(
        jnp.where(pick == first, logits, 0.0) - jnp.where(pick == second, logits, 0.0),
        axis=0,
        keepdims=True,
    )
    hi, mid, low = split3(jnp.concatenate([gap, -gap], axis=1))
    meta_row = lax.broadcasted_iota(jnp.int32, (META, both), 0)
    meta = jnp.where(
        meta_row == 0,
        hi,
        jnp.where(
            meta_row == 1,
            mid,
            jnp.where(meta_row == 2, low, jnp.where(meta_row == 3, other.astype(F32), 0.0)),
        ),
    ).astype(BF16)
    span = min(width, LANES)
    near = lax.broadcasted_iota(jnp.int32, (span, both), 0)
    for e in range(experts):
        mine = ((near + e * ROWS == position) & (near < CAP)).astype(F32).astype(BF16)
        block = dot(meta, mine, ((1,), (1,)))
        if width > span:
            block = jnp.concatenate([block, jnp.zeros((META, width - span), F32)], axis=1)
        base = e * ROWS
        send_refs[e][...] = jnp.concatenate([rows_x[base : base + CAP], block], axis=0).astype(BF16)


def stack_kernel(count, *refs):
    for q in range(count):
        refs[-1][q] = refs[count - 1 - q][...]


def join_kernel(groups, _, *refs):
    blocks_d, blocks_x, own_x, own_d = refs[:groups], refs[groups:-2], refs[-2], refs[-1]
    for q in range(groups):
        own_d[q] = blocks_d[groups - 1 - q][...]
    if len(blocks_x) == 1:
        own_x[...] = blocks_x[0][...]
    else:
        for k in range(len(blocks_x)):
            own_x[k] = blocks_x[len(blocks_x) - 1 - k][...]


def pick_kernel(relative, experts, hops, pos_ref, *refs):
    sources, sends = refs[: len(refs) - experts - 1], refs[len(refs) - experts :]
    merged = chosen(pos_ref[...], experts)
    for k in range(hops):
        rows = dot(merged, sources[k][...] if relative else sources[0][k], ((1,), (0,)))
        for q in range(experts):
            sends[q][k] = rows[q * ROWS : q * ROWS + CAP].astype(BF16)


def column(row):
    size = row.shape[1]
    down = lax.broadcasted_iota(jnp.int32, (size, size), 0)
    across = lax.broadcasted_iota(jnp.int32, (size, size), 1)
    return jnp.sum(jnp.where(down == across, row, 0.0), axis=1, keepdims=True)


def visit(groups, hops, width, relative, body):
    core = lax.axis_index("core")
    z = lax.axis_index("z")
    if width % LANES == 0:
        for side in range(2):
            for k in range(hops):
                at = ((z ^ k if relative else k) * 2 + (core ^ side)) * width
                body(side, k, pl.ds(pl.multiple_of(at, LANES), width))
        return
    for here in range(2):

        @pl.when(core == here)
        def _():
            for side in range(2):
                for k in range(hops):
                    at = (k * 2 + (here ^ side)) * width
                    body(side, k, pl.ds(at, width))


def load_kernel(source, out, mark, sem):
    mark[...] = jnp.zeros(mark.shape, F32)
    copy = pltpu.make_async_copy(source, out, sem)
    copy.start()
    copy.wait()


def forward_kernel(relative, groups, hops, *refs):
    sides, (gate_ref, up_ref, down_ref) = refs[:2], refs[2:5]
    x_ref, hid_ref, active_ref, slope_ref, gates_ref, rival_ref, other_ref, keep_ref, give_ref, total = refs[
        5:
    ]
    width = keep_ref.shape[-1]
    model = x_ref.shape[1]
    units = hid_ref.shape[1]
    tile = min(units, 256)

    def place(side, k, features):
        for q in range(groups):
            x_ref[q * ROWS : (q + 1) * ROWS, features] = sides[side][k, q]

    visit(groups, hops, width, relative, place)
    for q in range(groups):
        logit = jnp.zeros((META, ROWS), F32)
        for k in range(hops):
            for side in range(2):
                meta = sides[side][k, q].astype(F32)[CAP:, :ROWS]
                logit = logit + meta
        gap = column(logit[0:1] + logit[1:2] + logit[2:3])
        here = slice(q * ROWS, (q + 1) * ROWS)
        gates_ref[here, :] = jax.nn.sigmoid(gap)
        rival_ref[here, :] = jax.nn.sigmoid(-gap)
        other_ref[here, :] = column(meta[3:4])

    rows_x = x_ref[...]
    for f in range(0, units, tile):
        now = slice(f, f + tile)
        gate_pre = dot(rows_x, gate_ref[0, :, now], ((1,), (0,)))
        up_pre = dot(rows_x, up_ref[0, :, now], ((1,), (0,)))
        sigma = jax.nn.sigmoid(gate_pre)
        active = gate_pre * sigma
        active_ref[:, now] = active
        slope_ref[:, now] = sigma * (1.0 + gate_pre * (1.0 - sigma)) * up_pre
        hid_ref[:, now] = (active * up_pre).astype(BF16)
    hidden = hid_ref[...]
    for f in range(0, model, 512):
        now = slice(f, f + 512)
        total[:, now] = gates_ref[...] * dot(hidden, down_ref[0, :, now], ((1,), (0,)))

    def emit(side, k, features):
        for q in range(groups):
            rows = total[q * ROWS : (q + 1) * ROWS, features]
            if side == 0:
                keep_ref[k, q] = rows
            else:
                give_ref[k, q] = rows.astype(BF16)

    visit(groups, hops, width, relative, emit)


def backward_kernel(relative, groups, hops, *refs):
    inputs = 2
    x_ref, active_ref, slope_ref, hid_ref, gates_ref, rival_ref, other_ref, down_ref = refs[inputs : inputs + 8]
    d_ref, dgate_ref, dup_ref, keep_ref, give_ref, scratch = refs[inputs + 8 :]
    experts, width = keep_ref.shape[1:]
    units = hid_ref.shape[1]
    tile = min(units, 256)

    def place(side, k, features):
        for q in range(groups):
            rows = gates_ref[q * ROWS : q * ROWS + CAP, :] * refs[side][q, k].astype(F32)
            rows = jnp.concatenate([rows, jnp.zeros((META, width), F32)], axis=0)
            d_ref[q * ROWS : (q + 1) * ROWS, features] = rows.astype(BF16)

    visit(groups, hops, width, relative, place)
    rows_d = d_ref[...]
    dots = jnp.zeros((rows_d.shape[0], 1), F32)
    for f in range(0, units, tile):
        now = slice(f, f + tile)
        d_hidden = dot(rows_d, down_ref[0, now, :], ((1,), (1,)))
        dgate_ref[:, now] = (d_hidden * slope_ref[:, now]).astype(BF16)
        dup_ref[:, now] = (d_hidden * active_ref[:, now]).astype(BF16)
        dots += jnp.sum(hid_ref[:, now].astype(F32) * d_hidden, axis=1, keepdims=True)
    weight = dots * rival_ref[...]
    lane = lax.broadcasted_iota(jnp.int32, (weight.shape[0], experts), 1)
    signed = jnp.where(lane == lax.axis_index("expert"), weight, 0.0) - jnp.where(
        lane == other_ref[...].astype(jnp.int32), weight, 0.0
    )
    router = jnp.zeros((experts, x_ref.shape[1]), F32)
    for piece in split3(signed):
        router = router + dot(piece.astype(BF16), x_ref[...], ((0,), (0,)))
    scratch[...] = router

    def emit(side, k, features):
        rows = scratch[:, features]
        if side == 0:
            keep_ref[k] = rows
        else:
            give_ref[k] = halves(rows).astype(BF16)

    visit(groups, hops, width, relative, emit)


def halves(rows):
    top = rows.astype(BF16).astype(F32)
    return jnp.concatenate([top, rows - top], axis=0)


def merge_kernel(keep_ref, got_ref, rkeep_ref, rgot_ref, *out_refs):
    experts = rkeep_ref.shape[1]
    hops = keep_ref.shape[0]
    for k in range(hops):
        got = rgot_ref[k].astype(F32)
        router = halves(rkeep_ref[k] + got[:experts] + got[experts:])
        put(out_refs[k], keep_ref[k] + got_ref[k].astype(F32), router)


def put(out_ref, blocks, router):
    rows = [blocks[q, :CAP] for q in range(blocks.shape[0])]
    out_ref[...] = jnp.concatenate([*rows, router], axis=0).astype(BF16)


def grads_kernel(x_ref, d_ref, dgate_ref, dup_ref, hid_ref, _, gate_ref, up_ref, down_ref, mark_ref):
    rows_x = x_ref[...]
    first = ((0,), (0,))
    gate_ref[0] = dot(rows_x, dgate_ref[...], first).astype(BF16)
    up_ref[0] = dot(rows_x, dup_ref[...], first).astype(BF16)
    down_ref[0] = dot(hid_ref[...], d_ref[...], first).astype(BF16)
    mark_ref[...] = jnp.zeros(mark_ref.shape, F32)


def sum_kernel(experts, groups, *refs):
    parts, sends = refs[: len(refs) - groups - 1], refs[len(refs) - groups :]
    total = parts[0][...].astype(F32)
    for ref in parts[1:]:
        total = total + ref[...].astype(F32)
    router = total[groups * CAP :]
    router = halves(router[:experts] + router[experts:])
    height, width = sends[0].shape
    for q, send in enumerate(sends):
        rows = [total[q * CAP : (q + 1) * CAP], router]
        if height > CAP + 2 * experts:
            rows.append(jnp.zeros((height - CAP - 2 * experts, width), F32))
        send[...] = jnp.concatenate(rows, axis=0).astype(BF16)


def combine_kernel(groups, pos_ref, *refs):
    backs, mixed_ref, router_ref = refs[:groups], refs[groups], refs[groups + 1]
    experts, width = router_ref.shape
    blocks = []
    router = jnp.zeros((2 * experts, width), F32)
    for ref in reversed(backs):
        block = ref[...].astype(F32)
        router = router + block[CAP : CAP + 2 * experts]
        blocks.append(block[:CAP])
        blocks.append(jnp.zeros((ROWS - CAP, width), F32))
    rows = jnp.concatenate(blocks, axis=0).astype(BF16)
    merged = chosen(pos_ref[...], experts)
    mixed_ref[...] = dot(merged, rows, ((0,), (0,))).astype(BF16)
    router_ref[...] = (router[:experts] + router[experts:]).astype(BF16)


def swap(block, axis, bits):
    size = lax.axis_size(axis)
    return lax.ppermute(block, axis, [(i, i ^ bits) for i in range(size)])


def shards(tokens, expert_ids, live_tokens, replicated, w_router, w_gate, w_up, w_down, cotangent):
    groups = lax.axis_size("expert")
    hops = lax.axis_size("z")
    experts = w_router.shape[1]
    count, width = tokens.shape
    _, model, units = w_gate.shape
    rows = groups * ROWS
    height = -(-(CAP + 2 * experts) // 16) * 16
    relative = width % LANES == 0 and hops == 4
    whole = pl.BlockSpec(memory_space=pltpu.VMEM)
    anywhere = pl.BlockSpec(memory_space=pl.ANY)
    fixed = pl.BlockSpec(memory_space=pltpu.HBM)
    shape = jax.ShapeDtypeStruct

    def call(kernel, args, outs, name, scratch=(), loose=(), cost=None, limit=4 * MIB):
        args = [pltpu.with_memory_space_constraint(a, pltpu.HBM) if i in loose else a for i, a in enumerate(args)]
        return pl.pallas_call(
            kernel,
            out_shape=tuple(outs),
            in_specs=[fixed if i in loose else whole for i in range(len(args))],
            out_specs=(whole,) * len(outs),
            scratch_shapes=list(scratch),
            compiler_params=pltpu.CompilerParams(vmem_limit_bytes=limit),
            cost_estimate=cost,
            name=name,
        )(*args)

    position, handed, *sends = call(
        functools.partial(pack_kernel, experts),
        (live_tokens, replicated, expert_ids.T, w_router.T, tokens, cotangent),
        [shape((1, 2 * count), jnp.int32), shape(cotangent.shape, BF16)] + [shape((ROWS, width), BF16)] * experts,
        "pack",
        scratch=[
            pltpu.SMEM(live_tokens.shape, jnp.int32),
            pltpu.SMEM(replicated.shape, jnp.int32),
            pltpu.VMEM((2, count), jnp.int32),
            pltpu.VMEM((experts, width), BF16),
            pltpu.VMEM((count, width), BF16),
            pltpu.SemaphoreType.DMA((6,)),
        ],
        loose=range(6),
    )
    def load(weight, name):
        return call(
            load_kernel,
            (weight,),
            [pltpu.VMEM(weight.shape, BF16), shape((8, LANES), F32)],
            name,
            scratch=[pltpu.SemaphoreType.DMA],
            loose=(0,),
            cost=pl.CostEstimate(flops=0, bytes_accessed=2 * 2 * model * units, transcendentals=0),
            limit=8 * MIB,
        )

    gate_w, gate_mark = load(w_gate, "load_gate")
    up_w, up_mark = load(w_up, "load_up")
    down_w, down_mark = load(w_down, "load_down")
    def gather(block):
        if relative:
            second = swap(block, "z", 2)
            return [block, swap(block, "z", 1), second, swap(second, "z", 1)]
        return [lax.all_gather(block, "z", axis=0, tiled=False)]

    def exchange(blocks):
        return [swap(blocks[q], "expert", q) for q in range(groups - 1, 0, -1)] + [blocks[0]]

    arrived = exchange(sends)
    slices = gather(handed)
    picked = call(
        functools.partial(pick_kernel, relative, experts, hops),
        (position, *slices, up_mark),
        [shape((hops, CAP, width), BF16)] * experts,
        "pick",
    )
    (stacked,) = call(
        functools.partial(stack_kernel, groups),
        (*arrived, gate_mark, *slices[1:3]),
        [shape((groups, ROWS, width), BF16)],
        "stack",
    )
    blocks_x = [swap(stacked, "z", k) for k in range(hops - 1, 0, -1)] + [stacked] if relative else gather(stacked)
    blocks_d = exchange(picked)
    own_x, own_d = call(
        functools.partial(join_kernel, groups),
        (down_mark, *blocks_d, *blocks_x),
        [shape((hops, *stacked.shape), BF16), shape((groups, *picked[0].shape), BF16)],
        "join",
    )
    far_x = swap(own_x, "core", 1)
    far_d = swap(own_d, "core", 1)

    cost = 2 * rows * model * units
    rows_x, hidden, active, slope, gates, rival, others, keep, give = call(
        functools.partial(forward_kernel, relative, groups, hops),
        (own_x, far_x, gate_w, up_w, down_w),
        [
            shape((rows, model), BF16),
            shape((rows, units), BF16),
            shape((rows, units), F32),
            shape((rows, units), F32),
            shape((rows, 1), F32),
            shape((rows, 1), F32),
            shape((rows, 1), F32),
            shape((hops, groups, ROWS, width), F32),
            shape((hops, groups, ROWS, width), BF16),
        ],
        "forward",
        scratch=[pltpu.VMEM((rows, model), F32)],
        cost=pl.CostEstimate(flops=3 * cost, bytes_accessed=6 * model * units, transcendentals=rows * units),
        limit=16 * MIB,
    )
    got = swap(give, "core", 1)
    rows_d, d_gate, d_up, router_keep, router_give = call(
        functools.partial(backward_kernel, relative, groups, hops),
        (own_d, far_d, rows_x, active, slope, hidden, gates, rival, others, down_w),
        [
            shape((rows, model), BF16),
            shape((rows, units), BF16),
            shape((rows, units), BF16),
            shape((hops, experts, width), F32),
            shape((hops, 2 * experts, width), BF16),
        ],
        "backward",
        scratch=[pltpu.VMEM((experts, model), F32)],
        cost=pl.CostEstimate(flops=cost, bytes_accessed=2 * model * units, transcendentals=0),
        limit=14 * MIB,
    )
    router_got = swap(router_give, "core", 1)
    merged = call(
        merge_kernel,
        (keep, got, router_keep, router_got),
        [shape((groups * CAP + 2 * experts, width), BF16)] * hops,
        "merge",
    )
    if relative:
        outs = [merged[0]] + [swap(merged[k], "z", k) for k in range(hops - 1, 0, -1)]
    else:
        outs = lax.all_to_all(jnp.stack(merged), "z", split_axis=0, concat_axis=0, tiled=True)
        outs = [outs[k] for k in range(hops)]

    parts = 8
    once = lambda *shape: pl.BlockSpec(shape, lambda i: (0,) * len(shape))
    strip = max(units // parts, LANES)
    at = lambda i: i if units >= LANES * parts else 0
    grad_gate, grad_up, grad_down, mark = pl.pallas_call(
        grads_kernel,
        grid=(parts,),
        out_shape=(
            shape(w_gate.shape, BF16),
            shape(w_up.shape, BF16),
            shape(w_down.shape, BF16),
            shape((8, LANES), F32),
        ),
        in_specs=[
            pl.BlockSpec((rows, model // parts), lambda i: (0, i)),
            once(rows, model),
            once(rows, units),
            once(rows, units),
            pl.BlockSpec((rows, strip), lambda i: (0, at(i))),
            anywhere,
        ],
        out_specs=(
            pl.BlockSpec((1, model // parts, units), lambda i: (0, i, 0)),
            pl.BlockSpec((1, model // parts, units), lambda i: (0, i, 0)),
            pl.BlockSpec((1, strip, model), lambda i: (0, at(i), 0)),
            once(8, LANES),
        ),
        compiler_params=pltpu.CompilerParams(vmem_limit_bytes=24 * MIB),
        cost_estimate=pl.CostEstimate(flops=3 * cost, bytes_accessed=6 * model * units, transcendentals=0),
        name="grads",
    )(rows_x, rows_d, d_gate, d_up, hidden, merged[0])

    backs = call(
        functools.partial(sum_kernel, experts, groups),
        (*outs, mark),
        [shape((height, width), BF16)] * groups,
        "total",
    )
    backs = exchange(backs)
    mixed, grad_router = call(
        functools.partial(combine_kernel, groups),
        (position, *backs),
        [shape((count, width), BF16), shape((experts, width), BF16)],
        "combine",
    )
    return (mixed, grad_gate, grad_up, grad_down, grad_router.T)


def solution(mesh):
    groups, etp = mesh.devices.shape
    inner = Mesh(mesh.devices.reshape(groups, etp // 2, 2), ("expert", "z", "core"))
    etp = ("z", "core")
    in_specs = (
        P("expert", etp),
        P("expert", None),
        P(),
        P(),
        P(etp, None),
        P("expert", None, etp),
        P("expert", None, etp),
        P("expert", etp, None),
        P("expert", etp),
    )
    out_specs = (
        P("expert", etp),
        P("expert", None, etp),
        P("expert", None, etp),
        P("expert", etp, None),
        P(etp, None),
    )
    return jax.shard_map(shards, mesh=inner, in_specs=in_specs, out_specs=out_specs, check_vma=False)
```
